32 devices in a mesh: wide: 8 (over y, x, core), narrow: 4 (over z).
Axes of the slice: x: 2, y: 2, z: 4, core: 2. Of those that a mesh axis runs over, the one named last changes fastest.
Arguments:
- input_five: bfloat16 [128, 5, 5, 2048], P('wide'), may hold values from -20 to 20
- input_seven: bfloat16 [128, 7, 7, 2048], P('wide'), may hold values from -20 to 20
- input_nine: bfloat16 [128, 9, 9, 2048], P('wide'), may hold values from -20 to 20
- upstream_five: bfloat16 [128, 5, 5, 2048], P('wide', None, None, 'narrow'), may hold values from -20 to 20
- upstream_seven: bfloat16 [128, 7, 7, 2048], P('wide', None, None, 'narrow'), may hold values from -20 to 20
- upstream_nine: bfloat16 [128, 9, 9, 2048], P('wide', None, None, 'narrow'), may hold values from -20 to 20
- reduce_weight: bfloat16 [2048, 512], P(None, 'narrow'), may hold values from -0.125 to 0.125
- spatial_weight: bfloat16 [3, 3, 512, 512], P(None, None, None, 'narrow'), may hold values from -0.09375 to 0.09375
- expand_weight: bfloat16 [512, 2048], P('narrow'), may hold values from -0.25 to 0.25
- gain_first: float32 [512], P('narrow'), may hold values from 0.1 to 1.9
- shift_first: float32 [512], P('narrow'), may hold values from -2.5 to 2.5
- gain_second: float32 [512], P('narrow'), may hold values from 0.1 to 1.9
- shift_second: float32 [512], P('narrow'), may hold values from -2.5 to 2.5
- gain_third: float32 [2048], P('narrow'), may hold values from 0.1 to 1.9
- shift_third: float32 [2048], P('narrow'), may hold values from -2.5 to 2.5
Outputs:
- output_five: bfloat16 [128, 5, 5, 2048], P('wide', None, None, 'narrow')
- output_seven: bfloat16 [128, 7, 7, 2048], P('wide', None, None, 'narrow')
- output_nine: bfloat16 [128, 9, 9, 2048], P('wide', None, None, 'narrow')
- ingrad_five: float32 [128, 5, 5, 2048], P('wide', None, None, 'narrow')
- ingrad_seven: float32 [128, 7, 7, 2048], P('wide', None, None, 'narrow')
- ingrad_nine: float32 [128, 9, 9, 2048], P('wide', None, None, 'narrow')
- reduce_grad: float32 [2048, 512], P(None, 'narrow')
- spatial_grad: float32 [3, 3, 512, 512], P(None, None, None, 'narrow')
- expand_grad: float32 [512, 2048], P('narrow')
- gaingrad_first: float32 [512], P('narrow')
- shiftgrad_first: float32 [512], P('narrow')
- gaingrad_second: float32 [512], P('narrow')
- shiftgrad_second: float32 [512], P('narrow')
- gaingrad_third: float32 [2048], P('narrow')
- shiftgrad_third: float32 [2048], P('narrow')
The draws below stay inside these ranges and needn't reach their ends.
All inputs are finite; a program needn't handle non-finite values.
Results may differ from the reference program's by a relative error of at most 0.015.
Values may be sent and summed in bfloat16 or wider, within the bound.
A program may use at most 192 MiB of HBM per device.

```python
import jax
import jax.numpy as jnp
from jax import lax

D = 2048
INNER = 512
IMAGES = 128


def rough_core(key, extent):
    return jnp.clip(jax.random.normal(key, extent, jnp.float32), -4.0, 4.0)


def shaped(key, core):
    images = core.shape[0]
    ranking = jnp.arange(images, dtype=jnp.float32).reshape(images, 1, 1, 1)
    rising = 0.5 + ranking / max(images - 1, 1)
    spread = jnp.exp(jax.random.uniform(key, (images, core.shape[1], core.shape[2], 1), jnp.float32, -1.15, 1.15))
    return (core * rising * spread).astype(jnp.bfloat16)


def draw_input_five(key, part):
    key = jax.random.fold_in(key, 1)
    extent = (IMAGES, 5, 5, D)
    core = rough_core(key, extent)
    return shaped(jax.random.fold_in(key, 11), core)


def draw_input_seven(key, part):
    key = jax.random.fold_in(key, 2)
    extent = (IMAGES, 7, 7, D)
    core = rough_core(key, extent)
    return shaped(jax.random.fold_in(key, 11), core)


def draw_input_nine(key, part):
    key = jax.random.fold_in(key, 3)
    extent = (IMAGES, 9, 9, D)
    core = rough_core(key, extent)
    return shaped(jax.random.fold_in(key, 11), core)


def draw_upstream_five(key, part):
    key = jax.random.fold_in(key, 4)
    extent = (IMAGES, 5, 5, D)
    core = rough_core(key, extent)
    return shaped(jax.random.fold_in(key, 11), core)


def draw_upstream_seven(key, part):
    key = jax.random.fold_in(key, 6)
    extent = (IMAGES, 7, 7, D)
    core = rough_core(key, extent)
    return shaped(jax.random.fold_in(key, 11), core)


def draw_upstream_nine(key, part):
    key = jax.random.fold_in(key, 7)
    extent = (IMAGES, 9, 9, D)
    core = rough_core(key, extent)
    return shaped(jax.random.fold_in(key, 11), core)


def block_levels(own_key, shape, cuts, low, top_value):
    def one(position, parts):
        draws = jax.random.uniform(jax.random.fold_in(jax.random.fold_in(own_key, 6), position), (parts,), jnp.float32, low / len(cuts), top_value / len(cuts))
        return jnp.repeat(jnp.exp(draws), shape[position] // parts).reshape((-1,) + (1,) * (len(shape) - position - 1))

    gain = one(*cuts[0])
    for cut in cuts[1:]:
        gain = gain * one(*cut)
    return gain


def noise(stream_key, dims, scale, bound, cuts=(), kind=jnp.bfloat16):
    result = scale * jax.random.normal(stream_key, dims, jnp.float32)
    if cuts:
        result = result * block_levels(stream_key, dims, cuts, -0.22, 0.18)
    return jnp.clip(result, -bound, bound).astype(kind)


def setup_inputs(seed: int = 0) -> dict:
    key_of = jax.random.split(jax.random.key(seed), 16)
    input_five = draw_input_five(jax.random.fold_in(key_of[15], 71), 0)
    input_seven = draw_input_seven(jax.random.fold_in(key_of[15], 71), 0)
    input_nine = draw_input_nine(jax.random.fold_in(key_of[15], 71), 0)
    upstream_five = draw_upstream_five(jax.random.fold_in(key_of[15], 71), 0)
    upstream_seven = draw_upstream_seven(jax.random.fold_in(key_of[15], 71), 0)
    upstream_nine = draw_upstream_nine(jax.random.fold_in(key_of[15], 71), 0)
    reduce_weight = noise(key_of[6], (D, INNER), D ** -0.5, 0.125, ((1, 4),))
    spatial_weight = noise(key_of[7], (3, 3, INNER, INNER), (9 * INNER) ** -0.5, 0.09375, ((3, 4),))
    expand_weight = noise(key_of[8], (INNER, D), INNER ** -0.5, 0.25, ((0, 4),))
    gain_first = jnp.clip(1.0 + 0.18 * jax.random.normal(key_of[9], (INNER,), jnp.float32), 0.1, 1.9)
    shift_first = noise(key_of[10], (INNER,), 0.5, 2.5, ((0, 4),), jnp.float32)
    gain_second = jnp.clip(1.0 + 0.18 * jax.random.normal(key_of[11], (INNER,), jnp.float32), 0.1, 1.9)
    shift_second = noise(key_of[12], (INNER,), 0.5, 2.5, ((0, 4),), jnp.float32)
    gain_third = jnp.clip(1.0 + 0.18 * jax.random.normal(key_of[13], (D,), jnp.float32), 0.1, 1.9)
    shift_third = noise(key_of[14], (D,), 0.5, 2.5, ((0, 4),), jnp.float32)
    return {"input_five": input_five, "input_seven": input_seven, "input_nine": input_nine, "upstream_five": upstream_five, "upstream_seven": upstream_seven, "upstream_nine": upstream_nine, "reduce_weight": reduce_weight, "spatial_weight": spatial_weight, "expand_weight": expand_weight, "gain_first": gain_first, "shift_first": shift_first, "gain_second": gain_second, "shift_second": shift_second, "gain_third": gain_third, "shift_third": shift_third}


EPS = 1e-05
LAYOUT = ('NHWC', 'HWIO', 'NHWC')

@jax.custom_vjp
def low(v):
    return lax.optimization_barrier(v.astype(jnp.bfloat16)).astype(jnp.float32)

@jax.custom_vjp
def low_back(v):
    return v

def low_keep(v):
    return (low(v), None)

def low_pass(kept, grad):
    return (grad,)

def back_keep(v):
    return (v, None)

def back_low(kept, grad):
    return (low(grad),)
low.defvjp(low_keep, low_pass)
low_back.defvjp(back_keep, back_low)

def batch_norm(hidden, gain_vec, shift_vec):
    average = lax.optimization_barrier(jnp.mean(hidden, axis=(0, 1, 2)))
    variance = lax.optimization_barrier(jnp.mean(hidden * hidden, axis=(0, 1, 2))) - average * average
    return (hidden - average) * lax.rsqrt(variance + EPS) * gain_vec + shift_vec

def bottleneck(inputs, reduce_weight, spatial_weight, expand_weight, gain_first, shift_first, gain_second, shift_second, gain_third, shift_third):
    highest = lax.Precision.HIGHEST
    hidden_first = low_back(jnp.einsum('bhwc,cd->bhwd', inputs, reduce_weight, precision=highest))
    active_first = low(jax.nn.silu(batch_norm(hidden_first, gain_first, shift_first)))
    hidden_second = low_back(lax.conv_general_dilated(active_first, spatial_weight, (1, 1), ((1, 1), (1, 1)), dimension_numbers=LAYOUT, precision=highest))
    active_second = low(jax.nn.silu(batch_norm(hidden_second, gain_second, shift_second)))
    hidden_third = low_back(jnp.einsum('bhwi,id->bhwd', active_second, expand_weight, precision=highest))
    return jax.nn.silu(batch_norm(hidden_third, gain_third, shift_third) + inputs)

def reference(input_five, input_seven, input_nine, upstream_five, upstream_seven, upstream_nine, reduce_weight, spatial_weight, expand_weight, gain_first, shift_first, gain_second, shift_second, gain_third, shift_third):

    def forward(first_in, second_in, third_in, *params):
        return (bottleneck(first_in, *params), bottleneck(second_in, *params), bottleneck(third_in, *params))
    floats = [a.astype(jnp.float32) for a in (input_five, input_seven, input_nine, reduce_weight, spatial_weight, expand_weight)]
    params = floats[3:] + [gain_first, shift_first, gain_second, shift_second, gain_third, shift_third]
    outputs, pullback = jax.vjp(forward, floats[0], floats[1], floats[2], *params)
    grads = pullback((upstream_five.astype(jnp.float32), upstream_seven.astype(jnp.float32), upstream_nine.astype(jnp.float32)))
    return (outputs[0].astype(jnp.bfloat16), outputs[1].astype(jnp.bfloat16), outputs[2].astype(jnp.bfloat16), grads[0], grads[1], grads[2], grads[3], grads[4], grads[5], grads[6], grads[7], grads[8], grads[9], grads[10], grads[11])
```

```python
import jax
import jax.numpy as jnp
from jax import lax
from jax.sharding import PartitionSpec as P

EPS = 1e-05
LAYOUT = ("NHWC", "HWIO", "NHWC")


def silu_slope(argument):
    logistic = jax.nn.sigmoid(argument)
    return logistic * (1.0 + argument * (1.0 - logistic))


def spatial(inputs, kernel):
    return lax.conv_general_dilated(
        inputs,
        kernel,
        (1, 1),
        ((1, 1), (1, 1)),
        dimension_numbers=LAYOUT,
        preferred_element_type=jnp.float32,
    )


def kernel_grad(inputs, gradient):
    height, breadth = (gradient.shape[1], gradient.shape[2])
    padded = jnp.pad(inputs, ((0, 0), (1, 1), (1, 1), (0, 0)))
    taps = []
    for vertical in range(3):
        for lateral in range(3):
            window = padded[:, vertical : vertical + height, lateral : lateral + breadth, :]
            taps.append(
                jnp.einsum("bhwc,bhwo->co", window, gradient, preferred_element_type=jnp.float32)
            )
    return jnp.stack(taps).reshape(3, 3, inputs.shape[3], gradient.shape[3])


def sums_forward(hidden):
    return (jnp.sum(hidden, axis=(0, 1, 2)), jnp.sum(hidden * hidden, axis=(0, 1, 2)))


def normed_of(hidden, sums, samples):
    average = sums[0] / samples
    inverse = lax.rsqrt(sums[1] / samples - average * average + EPS)
    return ((hidden - average) * inverse, inverse)


def sums_backward(upstream, normed):
    return (jnp.sum(upstream, axis=(0, 1, 2)), jnp.sum(upstream * normed, axis=(0, 1, 2)))


def hidden_grad(upstream, normed, inverse, gain, sums, samples):
    return (
        gain * inverse * (upstream - sums[0] / samples - normed * (sums[1] / samples))
    ).astype(jnp.bfloat16)


def each(function, *lists):
    return [function(*items) for items in zip(*lists)]


def columns(array, axis):
    own = array.shape[axis] // lax.axis_size("narrow")
    return lax.dynamic_slice_in_dim(array, lax.axis_index("narrow") * own, own, axis)


def dot(form, left, right):
    return jnp.einsum(form, left, right, preferred_element_type=jnp.float32)


def plain_body(
    input_five,
    input_seven,
    input_nine,
    upstream_five,
    upstream_seven,
    upstream_nine,
    reduce_weight,
    spatial_weight,
    expand_weight,
    gain_first,
    shift_first,
    gain_second,
    shift_second,
    gain_third,
    shift_third,
):
    inputs = [input_five, input_seven, input_nine]
    upstreams = [upstream_five, upstream_seven, upstream_nine]
    samples = [
        x.shape[0] * lax.axis_size("wide") * x.shape[1] * x.shape[2] for x in inputs
    ]
    whole_reduce = lax.all_gather(reduce_weight, "narrow", axis=1, tiled=True)
    whole_spatial = lax.all_gather(spatial_weight, "narrow", axis=3, tiled=True)
    own_expand = lax.all_to_all(expand_weight, "narrow", 1, 0, tiled=True)
    vectors = jnp.stack([gain_first, shift_first, gain_second, shift_second])
    gain1, shift1, gain2, shift2 = lax.all_gather(vectors, "narrow", axis=1, tiled=True)

    hidden1 = each(lambda x: dot("bhwc,cd->bhwd", x, whole_reduce), inputs)
    sums1 = lax.psum(each(sums_forward, hidden1), "wide")
    normed1, inverse1 = zip(*each(normed_of, hidden1, sums1, samples))
    pre1 = each(lambda n: n * gain1 + shift1, normed1)
    active1 = each(lambda p: jax.nn.silu(p).astype(jnp.bfloat16), pre1)

    hidden2 = each(lambda a: spatial(a, whole_spatial), active1)
    sums2 = lax.psum(each(sums_forward, hidden2), "wide")
    normed2, inverse2 = zip(*each(normed_of, hidden2, sums2, samples))
    pre2 = each(lambda n: n * gain2 + shift2, normed2)
    active2 = each(lambda p: jax.nn.silu(p).astype(jnp.bfloat16), pre2)

    hidden3 = each(lambda a: dot("bhwi,id->bhwd", a, own_expand), active2)
    sums3 = lax.psum(each(sums_forward, hidden3), "wide")
    normed3, inverse3 = zip(*each(normed_of, hidden3, sums3, samples))
    summed = each(
        lambda n, x: n * gain_third + shift_third + columns(x, 3).astype(jnp.float32),
        normed3,
        inputs,
    )
    results = each(lambda z: jax.nn.silu(z).astype(jnp.bfloat16), summed)
    grads_z = each(lambda u, z: u.astype(jnp.float32) * silu_slope(z), upstreams, summed)
    back3 = lax.psum(each(sums_backward, grads_z, normed3), "wide")
    grad3 = each(
        lambda e, n, r, s, m: hidden_grad(e, n, r, gain_third, s, m),
        grads_z,
        normed3,
        inverse3,
        back3,
        samples,
    )
    expand_grad = sum(each(lambda a, g: dot("bhwi,bhwd->id", a, g), active2, grad3))
    active_grad2 = each(
        lambda g: lax.psum(
            dot("bhwd,id->bhwi", g, own_expand).astype(jnp.bfloat16), "narrow"
        ).astype(jnp.float32),
        grad3,
    )
    grads_2 = each(lambda a, p: a * silu_slope(p), active_grad2, pre2)
    back2 = lax.psum(each(sums_backward, grads_2, normed2), "wide")
    grad2 = each(
        lambda e, n, r, s, m: hidden_grad(e, n, r, gain2, s, m),
        grads_2,
        normed2,
        inverse2,
        back2,
        samples,
    )
    spatial_grad = sum(each(lambda a, g: kernel_grad(a, columns(g, 3)), active1, grad2))
    flipped = jnp.transpose(whole_spatial[::-1, ::-1], (0, 1, 3, 2))
    grads_1 = each(lambda g, p: spatial(g, flipped) * silu_slope(p), grad2, pre1)
    back1 = lax.psum(each(sums_backward, grads_1, normed1), "wide")
    grad1 = each(
        lambda e, n, r, s, m: hidden_grad(e, n, r, gain1, s, m),
        grads_1,
        normed1,
        inverse1,
        back1,
        samples,
    )
    reduce_grad = sum(each(lambda x, g: dot("bhwc,bhwd->cd", x, columns(g, 3)), inputs, grad1))
    own_reduce = columns(whole_reduce, 0)
    in_grads = each(lambda g, e: dot("bhwd,cd->bhwc", g, own_reduce) + e, grad1, grads_z)

    low = [g.astype(jnp.bfloat16) for g in (reduce_grad, spatial_grad, expand_grad)]
    low[2] = lax.all_to_all(low[2], "narrow", 0, 1, tiled=True)
    totals = [g.astype(jnp.float32) for g in lax.psum(low, "wide")]

    def params(back, part):
        shift = sum(s[0] for s in back)
        gain = sum(s[1] for s in back)
        return [part(gain), part(shift)]

    def own(vector):
        return columns(vector, 0)

    small = params(back1, own) + params(back2, own) + params(back3, lambda v: v)
    return tuple(results + in_grads + totals + small)


def solution(mesh):
    rows = P("wide", None, None, None)
    blocks = P("wide", None, None, "narrow")
    weights = [P(None, "narrow"), P(None, None, None, "narrow"), P("narrow", None)]
    vectors = [P("narrow")] * 6
    return jax.shard_map(
        plain_body,
        mesh=mesh,
        in_specs=tuple([rows] * 3 + [blocks] * 3 + weights + vectors),
        out_specs=tuple([blocks] * 6 + weights + vectors),
        check_vma=False,
    )
```

```python
import functools

import jax
import jax.numpy as jnp
from jax import lax
from jax.experimental import pallas as pl
from jax.experimental.pallas import tpu as pltpu
from jax.sharding import PartitionSpec as P

EPS = 1e-05
LAYOUT = ("NHWC", "HWIO", "NHWC")


def silu_slope(argument):
    logistic = jax.nn.sigmoid(argument)
    return logistic * (1.0 + argument * (1.0 - logistic))


def spatial(inputs, kernel):
    return lax.conv_general_dilated(
        inputs,
        kernel,
        (1, 1),
        ((1, 1), (1, 1)),
        dimension_numbers=LAYOUT,
        preferred_element_type=jnp.float32,
    )


def kernel_grad(inputs, gradient):
    height, breadth = (gradient.shape[1], gradient.shape[2])
    padded = jnp.pad(inputs, ((0, 0), (1, 1), (1, 1), (0, 0)))
    taps = []
    for vertical in range(3):
        for lateral in range(3):
            window = padded[:, vertical : vertical + height, lateral : lateral + breadth, :]
            taps.append(
                jnp.einsum("bhwc,bhwo->co", window, gradient, preferred_element_type=jnp.float32)
            )
    return jnp.stack(taps).reshape(3, 3, inputs.shape[3], gradient.shape[3])


def sums_forward(hidden):
    return (jnp.sum(hidden, axis=(0, 1, 2)), jnp.sum(hidden * hidden, axis=(0, 1, 2)))


def normed_of(hidden, sums, samples):
    average = sums[0] / samples
    inverse = lax.rsqrt(sums[1] / samples - average * average + EPS)
    return ((hidden - average) * inverse, inverse)


def sums_backward(upstream, normed):
    return (jnp.sum(upstream, axis=(0, 1, 2)), jnp.sum(upstream * normed, axis=(0, 1, 2)))


def hidden_grad(upstream, normed, inverse, gain, sums, samples):
    return (
        gain * inverse * (upstream - sums[0] / samples - normed * (sums[1] / samples))
    ).astype(jnp.bfloat16)


def each(function, *lists):
    return [function(*items) for items in zip(*lists)]


def columns(array, axis):
    own = array.shape[axis] // lax.axis_size("narrow")
    return lax.dynamic_slice_in_dim(array, lax.axis_index("narrow") * own, own, axis)


def dot(form, left, right):
    return jnp.einsum(form, left, right, preferred_element_type=jnp.float32)


def plain_body(
    input_five,
    input_seven,
    input_nine,
    upstream_five,
    upstream_seven,
    upstream_nine,
    reduce_weight,
    spatial_weight,
    expand_weight,
    gain_first,
    shift_first,
    gain_second,
    shift_second,
    gain_third,
    shift_third,
):
    inputs = [input_five, input_seven, input_nine]
    upstreams = [upstream_five, upstream_seven, upstream_nine]
    samples = [
        x.shape[0] * lax.axis_size("wide") * x.shape[1] * x.shape[2] for x in inputs
    ]
    whole_reduce = lax.all_gather(reduce_weight, "narrow", axis=1, tiled=True)
    whole_spatial = lax.all_gather(spatial_weight, "narrow", axis=3, tiled=True)
    own_expand = lax.all_to_all(expand_weight, "narrow", 1, 0, tiled=True)
    vectors = jnp.stack([gain_first, shift_first, gain_second, shift_second])
    gain1, shift1, gain2, shift2 = lax.all_gather(vectors, "narrow", axis=1, tiled=True)

    hidden1 = each(lambda x: dot("bhwc,cd->bhwd", x, whole_reduce), inputs)
    sums1 = lax.psum(each(sums_forward, hidden1), "wide")
    normed1, inverse1 = zip(*each(normed_of, hidden1, sums1, samples))
    pre1 = each(lambda n: n * gain1 + shift1, normed1)
    active1 = each(lambda p: jax.nn.silu(p).astype(jnp.bfloat16), pre1)

    hidden2 = each(lambda a: spatial(a, whole_spatial), active1)
    sums2 = lax.psum(each(sums_forward, hidden2), "wide")
    normed2, inverse2 = zip(*each(normed_of, hidden2, sums2, samples))
    pre2 = each(lambda n: n * gain2 + shift2, normed2)
    active2 = each(lambda p: jax.nn.silu(p).astype(jnp.bfloat16), pre2)

    hidden3 = each(lambda a: dot("bhwi,id->bhwd", a, own_expand), active2)
    sums3 = lax.psum(each(sums_forward, hidden3), "wide")
    normed3, inverse3 = zip(*each(normed_of, hidden3, sums3, samples))
    summed = each(
        lambda n, x: n * gain_third + shift_third + columns(x, 3).astype(jnp.float32),
        normed3,
        inputs,
    )
    results = each(lambda z: jax.nn.silu(z).astype(jnp.bfloat16), summed)
    grads_z = each(lambda u, z: u.astype(jnp.float32) * silu_slope(z), upstreams, summed)
    back3 = lax.psum(each(sums_backward, grads_z, normed3), "wide")
    grad3 = each(
        lambda e, n, r, s, m: hidden_grad(e, n, r, gain_third, s, m),
        grads_z,
        normed3,
        inverse3,
        back3,
        samples,
    )
    expand_grad = sum(each(lambda a, g: dot("bhwi,bhwd->id", a, g), active2, grad3))
    active_grad2 = each(
        lambda g: lax.psum(
            dot("bhwd,id->bhwi", g, own_expand).astype(jnp.bfloat16), "narrow"
        ).astype(jnp.float32),
        grad3,
    )
    grads_2 = each(lambda a, p: a * silu_slope(p), active_grad2, pre2)
    back2 = lax.psum(each(sums_backward, grads_2, normed2), "wide")
    grad2 = each(
        lambda e, n, r, s, m: hidden_grad(e, n, r, gain2, s, m),
        grads_2,
        normed2,
        inverse2,
        back2,
        samples,
    )
    spatial_grad = sum(each(lambda a, g: kernel_grad(a, columns(g, 3)), active1, grad2))
    flipped = jnp.transpose(whole_spatial[::-1, ::-1], (0, 1, 3, 2))
    grads_1 = each(lambda g, p: spatial(g, flipped) * silu_slope(p), grad2, pre1)
    back1 = lax.psum(each(sums_backward, grads_1, normed1), "wide")
    grad1 = each(
        lambda e, n, r, s, m: hidden_grad(e, n, r, gain1, s, m),
        grads_1,
        normed1,
        inverse1,
        back1,
        samples,
    )
    reduce_grad = sum(each(lambda x, g: dot("bhwc,bhwd->cd", x, columns(g, 3)), inputs, grad1))
    own_reduce = columns(whole_reduce, 0)
    in_grads = each(lambda g, e: dot("bhwd,cd->bhwc", g, own_reduce) + e, grad1, grads_z)

    low = [g.astype(jnp.bfloat16) for g in (reduce_grad, spatial_grad, expand_grad)]
    low[2] = lax.all_to_all(low[2], "narrow", 0, 1, tiled=True)
    totals = [g.astype(jnp.float32) for g in lax.psum(low, "wide")]

    def params(back, part):
        shift = sum(s[0] for s in back)
        gain = sum(s[1] for s in back)
        return [part(gain), part(shift)]

    def own(vector):
        return columns(vector, 0)

    small = params(back1, own) + params(back2, own) + params(back3, lambda v: v)
    return tuple(results + in_grads + totals + small)


class Shape:
    def __init__(self, mesh, maps, images, depth, inner):
        self.wide, self.narrow = mesh.shape["wide"], mesh.shape["narrow"]
        self.chips = self.wide // 2
        self.maps = maps
        self.images = images
        self.depth, self.inner = depth, inner
        self.own = inner // self.narrow
        self.block = depth // self.narrow
        self.rows = [images * side * side for side in maps]
        self.samples = [float(rows * self.wide) for rows in self.rows]

    def fits(self):
        return (
            self.narrow >= 4
            and self.narrow % 2 == 0
            and self.wide % 2 == 0
            and self.block == self.inner
            and self.own % 128 == 0
            and self.images % 16 == 0
            and self.own % (16 * self.wide) == 0
            and self.inner % 512 == 0
        )


def image_rows(side):
    best = 1
    for count in range(1, side + 1):
        if side % count == 0 and count * side <= 49:
            best = count
    return best


def reduction_pieces(side):
    return 3 if side % 3 == 0 and side > 3 else 1


class Pool:
    def __init__(self, limit):
        self.limit, self.used = limit, 0
        self.ref = None

    def take(self):
        assert self.used < self.limit
        self.used += 1
        return self.ref.at[self.used - 1]


MESH = pl.DeviceIdType.MESH
SEMAPHORES = 400


def dot_nn(left, right):
    return lax.dot_general(
        left, right, (((1,), (0,)), ((), ())), preferred_element_type=jnp.float32
    )


def dot_nt(left, right):
    return lax.dot_general(
        left, right, (((1,), (1,)), ((), ())), preferred_element_type=jnp.float32
    )


def dot_tn(left, right):
    return lax.dot_general(
        left, right, (((0,), (0,)), ((), ())), preferred_element_type=jnp.float32
    )


def logistic(argument):
    return 0.5 * jnp.tanh(0.5 * argument) + 0.5


def block_kernel(shape, *refs):
    wide, narrow, chips = shape.wide, shape.narrow, shape.chips
    inner, own, block, images = shape.inner, shape.own, shape.block, shape.images
    refs = list(refs)

    def take(count):
        taken = refs[:count]
        del refs[:count]
        return taken

    x_in, u_in = take(3), take(3)
    rw_in, sw_in, ew_in = take(3)
    gain1, shift1, gain2, shift2, gain3, shift3 = take(6)
    y_out, i_out = take(3), take(3)
    rg_out, sg_out, eg_out = take(3)
    gg1, bg1, gg2, bg2, gg3, bg3 = take(6)
    xb = take(3)
    rwf, swf, ewf = take(3)
    h1, h2, h3, dz = take(3), take(3), take(3), take(3)
    apad, dpad = take(3), take(3)
    rin, rx = take(3), take(3)
    sacc, eacc, racc = take(3)
    sgb, egb, rgb = take(3)
    sr1, er1, rr1 = take(3)
    sr2, er2, rr2 = take(3)
    sfin, efin, rfin = take(3)
    epz, rpz = take(2)
    stat_s, stat_r, sums, vec, vec_all = take(5)
    (sem_ref,) = take(1)
    pool = Pool(SEMAPHORES)
    pool.ref = sem_ref

    w = lax.axis_index("wide")
    z = lax.axis_index("narrow")
    core = lax.rem(w, 2)
    chip = lax.div(w, 2)
    sibling = chip * 2 + (1 - core)
    half = narrow // 2
    low_side = z < half
    inward = jnp.where(low_side, z + 1, z - 1)
    outward = jnp.where(low_side, z - 1, z + 1)
    center = jnp.logical_or(z == half - 1, z == half)
    end = jnp.logical_or(z == 0, z == narrow - 1)
    finish = []

    def remote(source, target, device, when=None, send=None, recv=None):
        send = pool.take() if send is None else send
        recv = pool.take() if recv is None else recv

        def make():
            return pltpu.make_async_remote_copy(
                src_ref=source(),
                dst_ref=target(),
                send_sem=send,
                recv_sem=recv,
                device_id=device,
                device_id_type=MESH,
            )

        def start():
            make().start()

            def wait():
                if when is None:
                    make().wait_send()
                else:
                    pl.when(when)(lambda: make().wait_send())

            finish.append(wait)

        return start, lambda: make().wait_recv()

    def local(source, target):
        semaphore = pool.take()

        def make():
            return pltpu.make_async_copy(source(), target(), semaphore)

        return lambda: make().start(), lambda: make().wait()

    def span(start, size, unit):
        return pl.ds(pl.multiple_of(start * unit, unit), size)

    x_wait = [[None] * narrow for _ in range(3)]
    for g in range(3):
        for k in range(narrow):
            start, wait = local(
                lambda g=g, k=k: x_in[g].at[:, pl.ds(k * block, block)],
                lambda g=g, k=k: xb[g].at[k],
            )
            start()
            x_wait[g][k] = wait
    own_waits = []
    for source, target in (
        (lambda: rw_in, lambda: rwf.at[:, span(z, own, own)]),
        (lambda: sw_in, lambda: swf.at[:, :, span(z, own, own)]),
        (lambda: ew_in.at[:, span(z, block, block)], lambda: ewf.at[span(z, own, own), :]),
    ):
        start, wait = local(source, target)
        start()
        own_waits.append(wait)

    vec_all[z] = jnp.concatenate(
        [gain1[...], shift1[...], gain2[...], shift2[...], jnp.zeros((4, own), jnp.float32)], axis=0
    )

    barrier = pltpu.get_barrier_semaphore()
    for k in range(1, wide):
        pl.semaphore_signal(
            barrier, inc=1, device_id=(lax.rem(w + k, wide), z), device_id_type=MESH
        )
    for k in range(1, narrow):
        pl.semaphore_signal(
            barrier, inc=1, device_id=(w, lax.rem(z + k, narrow)), device_id_type=MESH
        )
    pl.semaphore_wait(barrier, wide - 1 + narrow - 1)

    vec_waits = []
    for k in range(1, narrow):
        start, wait = remote(
            lambda: vec_all.at[z], lambda: vec_all.at[z], (w, lax.rem(z + k, narrow))
        )
        start()
        vec_waits.append(wait)

    def gather(source_of, target_of):
        first = []
        for k in range(1, narrow):
            start, wait = remote(
                lambda: source_of(w), lambda: target_of(w, z), (w, lax.rem(z + k, narrow))
            )
            start()
            first.append(wait)
        second, third = [], []

        def spread():
            for k in range(1, narrow):
                first[k - 1]()
                origin = lax.rem(z + narrow - k, narrow)
                for j in range(1, chips):
                    peer = lax.rem(chip + j, chips) * 2 + core
                    start, wait = remote(
                        lambda origin=origin: target_of(w, origin),
                        lambda origin=origin: target_of(w, origin),
                        (peer, z),
                    )
                    start()
                    second.append((j, origin, wait))
                start, wait = remote(
                    lambda origin=origin: target_of(w, origin),
                    lambda origin=origin: target_of(w, origin),
                    (sibling, z),
                )
                start()
                third.append(wait)

        def cross():
            for j, origin, arrived in second:
                arrived()
                holder = lax.rem(chip + chips - j, chips) * 2 + core
                start, wait = remote(
                    lambda origin=origin, holder=holder: target_of(holder, origin),
                    lambda origin=origin, holder=holder: target_of(holder, origin),
                    (sibling, z),
                )
                start()
                third.append(wait)

        def ready():
            for wait in third:
                wait()

        return spread, cross, ready

    rw_piece, sw_piece = shape.depth // wide, inner // wide
    rw_spread, rw_cross, rw_ready = gather(
        lambda h: rw_in.at[span(h, rw_piece, rw_piece), :],
        lambda h, o: rwf.at[span(h, rw_piece, rw_piece), span(o, own, own)],
    )
    sw_spread, sw_cross, sw_ready = gather(
        lambda h: sw_in.at[:, span(h, sw_piece, sw_piece), :],
        lambda h, o: swf.at[:, span(h, sw_piece, sw_piece), span(o, own, own)],
    )
    ew_waits = []
    for k in range(1, narrow):
        peer = lax.rem(z + k, narrow)
        start, wait = remote(
            lambda peer=peer: ew_in.at[:, span(peer, block, block)],
            lambda: ewf.at[span(z, own, own), :],
            (w, peer),
        )
        start()
        ew_waits.append(wait)

    for g in range(3):
        side = shape.maps[g]
        for pad in (apad[g], dpad[g]):
            pad[0] = jnp.zeros((side + 2, images, inner), jnp.bfloat16)
            pad[side + 1] = jnp.zeros((side + 2, images, inner), jnp.bfloat16)
            for edge in (0, side + 1):
                pad[1 : side + 1, edge] = jnp.zeros((side, images, inner), jnp.bfloat16)

    for wait in vec_waits:
        wait()
    gathered = [
        jnp.concatenate([vec_all[k, row : row + 1, :] for k in range(narrow)], axis=1)
        for row in range(4)
    ]
    names = {}

    def put(name, value):
        if name not in names:
            names[name] = len(names)
        vec[names[name] : names[name] + 1, :] = value

    def get(name):
        return vec[names[name] : names[name] + 1, :]

    for name, value in zip(("g1", "b1", "g2", "b2"), gathered):
        put(name, value)
    put("g3", gain3[...])
    put("b3", shift3[...])

    tiles = inner // 128
    stat_sems = {}

    def stats_send(e, first, second):
        for b in range(tiles):
            stat_s[e, b : b + 1, :] = first[:, b * 128 : (b + 1) * 128]
            stat_s[e, tiles + b : tiles + b + 1, :] = second[:, b * 128 : (b + 1) * 128]
        stat_r[e, w] = stat_s[e]
        send, recv = pool.take(), pool.take()
        stat_sems[e] = (send, recv)

        def one(k, carry):
            pltpu.make_async_remote_copy(
                src_ref=stat_s.at[e],
                dst_ref=stat_r.at[e, w],
                send_sem=send,
                recv_sem=recv,
                device_id=(lax.rem(w + k, wide), z),
                device_id_type=MESH,
            ).start()
            return carry

        lax.fori_loop(1, wide, one, 0)

    def stats_all(e):
        send, recv = stat_sems[e]
        return pltpu.make_async_remote_copy(
            src_ref=stat_r.at[e, pl.ds(0, wide - 1)],
            dst_ref=stat_r.at[e, pl.ds(0, wide - 1)],
            send_sem=send,
            recv_sem=recv,
            device_id=(sibling, z),
            device_id_type=MESH,
        )

    def stats_wait(e):
        stats_all(e).wait_recv()
        finish.append(lambda: stats_all(e).wait_send())
        total = stat_r[e, 0]
        for k in range(1, wide):
            total = total + stat_r[e, k]
        return [
            jnp.concatenate([total[t * tiles + b : t * tiles + b + 1, :] for b in range(tiles)], axis=1)
            for t in range(2)
        ]

    def clear_sums():
        sums[0:2, :] = jnp.zeros((2, inner), jnp.float32)

    def add_sums(first, second):
        sums[0:1, :] += jnp.sum(first, axis=0, keepdims=True)
        sums[1:2, :] += jnp.sum(second, axis=0, keepdims=True)

    def send_sums(e):
        stats_send(e, sums[0:1, :], sums[1:2, :])

    def norm_vectors(g, level):
        e = g * 6 + level
        first, second = stats_wait(e)
        mean = first / shape.samples[g]
        inverse = lax.rsqrt(second / shape.samples[g] - mean * mean + EPS)
        scale = inverse * get(f"g{level + 1}")
        put(f"r{level}_{g}", inverse)
        put(f"m{level}_{g}", -mean * inverse)
        put(f"a{level}_{g}", scale)
        put(f"c{level}_{g}", get(f"b{level + 1}") - mean * scale)

    def back_vectors(g, level, e):
        shift_sum, gain_sum = stats_wait(e)
        put(f"sb{level}_{g}", shift_sum)
        put(f"sg{level}_{g}", gain_sum)
        scale = get(f"a{level}_{g}")
        inverse = get(f"r{level}_{g}")
        c1 = scale * (gain_sum / shape.samples[g])
        put(f"k1{level}_{g}", -inverse * c1)
        put(f"k0{level}_{g}", -get(f"m{level}_{g}") * c1 - scale * (shift_sum / shape.samples[g]))

    def loop(count, function):
        if count == 1:
            function(0)
        else:
            pl.loop(0, count)(function)

    def line(g):
        return shape.maps[g] * images

    def lines(g, function):
        size = line(g)
        pl.loop(0, shape.maps[g])(lambda y: function(y, pl.ds(pl.multiple_of(y * size, 16), size)))

    def slabs(g, function):
        count = image_rows(shape.maps[g])
        size = count * line(g)
        loop(
            shape.maps[g] // count,
            lambda s: function(s * count, count, pl.ds(pl.multiple_of(s * size, 16), size)),
        )

    k_own, k_a2, k_dh, k_p = [lax.rem(z + k, narrow) for k in range(4)]

    def f1(g):
        for k in range(narrow):
            x_wait[g][k]()
        clear_sums()

        def slab(y, count, rows):
            left = jnp.concatenate([xb[g][k, rows, :] for k in range(narrow)], axis=1)
            result = dot_nn(left, rwf[...])
            h1[g][rows, :] = result
            add_sums(result, result * result)

        slabs(g, slab)
        send_sums(g * 6)
        start, wait = local(lambda: u_in[g], lambda: xb[g].at[k_dh])
        start()
        u_wait[g] = wait

    u_wait = [None] * 3

    def a1(g):
        norm_vectors(g, 0)
        scale, offset = get(f"a0_{g}"), get(f"c0_{g}")
        side = shape.maps[g]

        def one(y, rows):
            pre = h1[g][rows, :] * scale + offset
            value = (pre * logistic(pre)).astype(jnp.bfloat16)
            apad[g][y + 1, pl.ds(1, side)] = value.reshape(side, images, inner)

        lines(g, one)

    def windows(pad, g, y, count):
        side = shape.maps[g]
        return [
            pad[pl.ds(y + i, count), pl.ds(j, side)].reshape(count * side * images, inner)
            for i in range(3)
            for j in range(3)
        ]

    def f2(g):
        clear_sums()

        def slab(y, count, rows):
            left = jnp.concatenate(windows(apad[g], g, y, count), axis=1)
            result = dot_nn(left, swf[...].reshape(9 * inner, inner))
            h2[g][rows, :] = result
            add_sums(result, result * result)

        slabs(g, slab)
        send_sums(g * 6 + 1)

    def a2(g):
        norm_vectors(g, 1)
        scale, offset = get(f"a1_{g}"), get(f"c1_{g}")

        def one(y, rows):
            pre = h2[g][rows, :] * scale + offset
            xb[g][k_a2, rows, :] = (pre * logistic(pre)).astype(jnp.bfloat16)

        lines(g, one)

    def f3(g):
        clear_sums()

        def slab(y, count, rows):
            result = dot_nn(xb[g][k_a2, rows, :], ewf[...])
            h3[g][rows, :] = result
            add_sums(result, result * result)

        slabs(g, slab)
        send_sums(g * 6 + 2)

    y_wait = [None] * 3

    def a3(g):
        norm_vectors(g, 2)
        u_wait[g]()
        clear_sums()
        scale, offset = get(f"a2_{g}"), get(f"c2_{g}")
        inverse, minus = get(f"r2_{g}"), get(f"m2_{g}")

        def one(y, rows):
            hidden = h3[g][rows, :]
            total = hidden * scale + offset + xb[g][k_own, rows, :].astype(jnp.float32)
            sig = logistic(total)
            xb[g][k_p, rows, :] = (total * sig).astype(jnp.bfloat16)
            slope = sig * (1.0 + total * (1.0 - sig))
            grad = xb[g][k_dh, rows, :].astype(jnp.float32) * slope
            dz[g][rows, :] = grad.astype(jnp.bfloat16)
            add_sums(grad, grad * (hidden * inverse + minus))

        lines(g, one)
        send_sums(g * 6 + 3)
        start, wait = local(lambda: xb[g].at[k_p], lambda: y_out[g])
        start()
        y_wait[g] = wait

    def b3(g):
        back_vectors(g, 2, g * 6 + 3)
        scale, k1, k0 = get(f"a2_{g}"), get(f"k12_{g}"), get(f"k02_{g}")
        y_wait[g]()

        def one(y, rows):
            value = dz[g][rows, :].astype(jnp.float32) * scale + h3[g][rows, :] * k1 + k0
            xb[g][k_dh, rows, :] = value.astype(jnp.bfloat16)

        lines(g, one)

        def slab(y, count, rows):
            result = dot_nt(xb[g][k_dh, rows, :], ewf[...])
            xb[g][k_p, rows, :] = result.astype(jnp.bfloat16)

        slabs(g, slab)

    def eg(g):
        result = dot_tn(xb[g][k_a2], xb[g][k_dh])
        for k in range(narrow):
            part = result[k * own : (k + 1) * own, :].reshape(eacc.shape[1:])
            eacc[k] = part if g == order[0] else eacc[k] + part

    reductions = {}

    def zparts(g):
        count = reduction_pieces(shape.maps[g])
        size = shape.rows[g] // count
        return [pl.ds(c * size, size) for c in range(count)]

    def za(g, c):
        rows = zparts(g)[c]
        sends = {}
        in_send, in_recv = pool.take(), pool.take()
        x_send, x_recv = pool.take(), pool.take()
        o_send = pool.take()
        partial = xb[g].at[k_p, rows, :]

        def to_center():
            return pltpu.make_async_remote_copy(
                src_ref=xb[g].at[k_p, rows, :],
                dst_ref=rx[g].at[rows, :],
                send_sem=x_send,
                recv_sem=x_recv,
                device_id=(w, inward),
                device_id_type=MESH,
            )

        def to_inner():
            return pltpu.make_async_remote_copy(
                src_ref=xb[g].at[k_p, rows, :],
                dst_ref=rin[g].at[rows, :],
                send_sem=in_send,
                recv_sem=in_recv,
                device_id=(w, inward),
                device_id_type=MESH,
            )

        def to_outer():
            return pltpu.make_async_remote_copy(
                src_ref=rx[g].at[rows, :],
                dst_ref=rx[g].at[rows, :],
                send_sem=o_send,
                recv_sem=x_recv,
                device_id=(w, outward),
                device_id_type=MESH,
            )

        @pl.when(jnp.logical_not(end))
        def _():
            to_inner().wait_recv()
            xb[g][k_p, rows, :] = (
                xb[g][k_p, rows, :].astype(jnp.float32) + rin[g][rows, :].astype(jnp.float32)
            ).astype(jnp.bfloat16)

        @pl.when(center)
        def _():
            to_center().start()

        @pl.when(jnp.logical_not(center))
        def _():
            to_inner().start()

        reductions[g, c] = (to_center, to_inner, to_outer)

    def zb(g, c):
        rows = zparts(g)[c]
        to_center, to_inner, to_outer = reductions[g, c]
        to_center().wait_recv()

        @pl.when(center)
        def _():
            rx[g][rows, :] = (
                rx[g][rows, :].astype(jnp.float32) + xb[g][k_p, rows, :].astype(jnp.float32)
            ).astype(jnp.bfloat16)

        @pl.when(jnp.logical_not(end))
        def _():
            to_outer().start()

        def done():
            pl.when(center)(lambda: to_center().wait_send())
            pl.when(jnp.logical_not(center))(lambda: to_inner().wait_send())
            pl.when(jnp.logical_not(end))(lambda: to_outer().wait_send())

        finish.append(done)

    def g2(g):
        clear_sums()
        scale, offset = get(f"a1_{g}"), get(f"c1_{g}")
        inverse, minus = get(f"r1_{g}"), get(f"m1_{g}")

        def one(y, rows):
            hidden = h2[g][rows, :]
            pre = hidden * scale + offset
            sig = logistic(pre)
            grad = rx[g][rows, :].astype(jnp.float32) * (sig * (1.0 + pre * (1.0 - sig)))
            h3[g][rows, :] = grad
            add_sums(grad, grad * (hidden * inverse + minus))

        lines(g, one)
        send_sums(g * 6 + 4)

    def d2(g):
        back_vectors(g, 1, g * 6 + 4)
        scale, k1, k0 = get(f"a1_{g}"), get(f"k11_{g}"), get(f"k01_{g}")
        side = shape.maps[g]

        def one(y, rows):
            value = h3[g][rows, :] * scale + h2[g][rows, :] * k1 + k0
            dpad[g][y + 1, pl.ds(1, side)] = value.astype(jnp.bfloat16).reshape(side, images, inner)

        lines(g, one)

    def sg(g):
        side = shape.maps[g]
        left = apad[g][pl.ds(1, side), pl.ds(1, side)].reshape(shape.rows[g], inner)
        right = jnp.concatenate(
            [
                dpad[g][pl.ds(2 - i, side), pl.ds(2 - j, side), :, span(z, own, own)].reshape(
                    shape.rows[g], own
                )
                for i in range(3)
                for j in range(3)
            ],
            axis=1,
        )
        result = dot_tn(left, right)
        for t in range(9):
            part = result[:, t * own : (t + 1) * own].reshape(sacc.shape[1:])
            sacc[t] = part if g == order[0] else sacc[t] + part

    def f1b(g):
        clear_sums()
        scale, offset = get(f"a0_{g}"), get(f"c0_{g}")
        inverse, minus = get(f"r0_{g}"), get(f"m0_{g}")

        def slab(y, count, rows):
            left = jnp.concatenate(windows(dpad[g], g, y, count), axis=1)
            right = jnp.concatenate([swf[8 - t] for t in range(9)], axis=1)
            h2[g][rows, :] = dot_nt(left, right)

        slabs(g, slab)

        def one(y, rows):
            hidden = h1[g][rows, :]
            pre = hidden * scale + offset
            sig = logistic(pre)
            grad = h2[g][rows, :] * (sig * (1.0 + pre * (1.0 - sig)))
            h2[g][rows, :] = grad
            add_sums(grad, grad * (hidden * inverse + minus))

        lines(g, one)
        send_sums(g * 6 + 5)

    def d1(g):
        back_vectors(g, 0, g * 6 + 5)
        scale, k1, k0 = get(f"a0_{g}"), get(f"k10_{g}"), get(f"k00_{g}")

        def one(y, rows):
            value = h2[g][rows, :] * scale + h1[g][rows, :] * k1 + k0
            xb[g][k_dh, rows, :] = value.astype(jnp.bfloat16)

        lines(g, one)

    def ig(g):
        def slab(y, count, rows):
            right = rwf[span(z, block, block), :]
            h3[g][rows, :] = dot_nt(xb[g][k_dh, rows, :], right) + dz[g][rows, :].astype(
                jnp.float32
            )

        slabs(g, slab)
        start, wait = local(lambda: h3[g], lambda: i_out[g])
        start()
        finish.append(wait)

    def rg(g):
        result = dot_tn(xb[g][k_own], xb[g][k_dh])
        for k in range(narrow):
            part = result[:, k * own : (k + 1) * own].reshape(racc.shape[1:])
            racc[k] = part if g == order[0] else racc[k] + part

    class Total:
        def __init__(self, acc, low, first, second, final, piece, out):
            self.acc, self.low, self.first, self.second = acc, low, first, second
            self.final, self.piece, self.out = final, piece, out
            self.count = acc.shape[0]

        def one(self):
            def cast(a):
                self.low[a] = self.acc[a, :, 1 - core].astype(jnp.bfloat16)

            pl.loop(0, self.count)(cast)
            start, self.got1 = remote(lambda: self.low, lambda: self.first, (sibling, z))
            start()

        def two(self):
            self.got1()

            def add(a):
                self.first[a] = (
                    self.first[a].astype(jnp.float32) + self.acc[a, :, core]
                ).astype(jnp.bfloat16)

            pl.loop(0, self.count)(add)
            self.got2 = []
            for j in range(1, chips):
                peer = lax.rem(chip + j, chips)
                start, wait = remote(
                    lambda peer=peer: self.first.at[:, peer],
                    lambda: self.second.at[chip],
                    (peer * 2 + core, z),
                )
                start()
                self.got2.append(wait)

        def three(self):
            for wait in self.got2:
                wait()
            self.second[chip] = self.first[:, chip]
            target = self.final.at[:, chip, core] if self.piece is None else self.piece

            def add(a):
                total = self.second[0, a].astype(jnp.float32)
                for k in range(1, chips):
                    total = total + self.second[k, a].astype(jnp.float32)
                target[a] = total.astype(jnp.bfloat16)

            pl.loop(0, self.count)(add)
            if self.piece is None:
                self.send_pieces()
                return
            self.got3 = []
            for k in range(1, narrow):
                peer = lax.rem(z + k, narrow)
                start, wait = remote(
                    lambda peer=peer: self.piece.at[peer],
                    lambda: self.final.at[z, chip, core],
                    (w, peer),
                )
                start()
                self.got3.append(wait)
            self.final[z, chip, core] = self.piece[z]

        def exchange(self):
            for wait in self.got3:
                wait()
            self.send_pieces()

        def send_pieces(self):
            self.got4, self.got5 = [], []
            for j in range(1, chips):
                peer = lax.rem(chip + j, chips)
                start, wait = remote(
                    lambda: self.final.at[:, chip, core],
                    lambda: self.final.at[:, chip, core],
                    (peer * 2 + core, z),
                )
                start()
                self.got4.append((j, wait))
            start, wait = remote(
                lambda: self.final.at[:, chip, core],
                lambda: self.final.at[:, chip, core],
                (sibling, z),
            )
            start()
            self.got5.append(wait)

        def four(self):
            for j, arrived in self.got4:
                arrived()
                holder = lax.rem(chip + chips - j, chips)
                start, wait = remote(
                    lambda holder=holder: self.final.at[:, holder, core],
                    lambda holder=holder: self.final.at[:, holder, core],
                    (sibling, z),
                )
                start()
                self.got5.append(wait)

        def five(self):
            for wait in self.got5:
                wait()

            def widen(a):
                self.acc[a] = self.final[a].astype(jnp.float32)

            pl.loop(0, self.count)(widen)
            for source, target in self.out:
                start, wait = local(source, target)
                start()
                finish.append(wait)

    stotal = Total(sacc, sgb, sr1, sr2, sfin, None, [(lambda: sacc, lambda: sg_out)])
    etotal = Total(
        eacc,
        egb,
        er1,
        er2,
        efin,
        epz,
        [
            (
                lambda k=k: eacc.at[k],
                lambda k=k: eg_out.at[:, :, :, pl.ds(k * block, block)],
            )
            for k in range(narrow)
        ],
    )
    rtotal = Total(racc, rgb, rr1, rr2, rfin, rpz, [(lambda: racc, lambda: rg_out)])

    def params():
        for level, gain_out, shift_out in ((0, gg1, bg1), (1, gg2, bg2), (2, gg3, bg3)):
            for kind, out in (("sg", gain_out), ("sb", shift_out)):
                total = get(f"{kind}{level}_0") + get(f"{kind}{level}_1") + get(f"{kind}{level}_2")
                if level == 2:
                    out[...] = total
                else:
                    put("scratch", total)
                    row = names["scratch"]
                    out[...] = vec[row : row + 1, span(z, own, own)]

    order = (0, 1, 2)

    def weights_first():
        for wait in own_waits:
            wait()
        rw_spread()
        rw_cross()
        rw_ready()

    def expand_ready():
        for wait in ew_waits:
            wait()

    plan = [
        (weights_first,),
        (f1, 0),
        (sw_spread,),
        (f1, 1),
        (f1, 2),
        (sw_cross,),
        (a1, 0),
        (sw_ready,),
        (f2, 0),
        (a1, 1),
        (f2, 1),
        (a2, 0),
        (expand_ready,),
        (f3, 0),
        (a1, 2),
        (a3, 0),
        (a2, 1),
        (f3, 1),
        (b3, 0),
        (za, 0, 0),
        (f2, 2),
        (a3, 1),
        (zb, 0, 0),
        (a2, 2),
        (b3, 1),
        (za, 1, 0),
        (f3, 2),
        (eg, 0),
        (g2, 0),
        (a3, 2),
        (zb, 1, 0),
        (d2, 0),
        (b3, 2),
        (za, 2, 0),
        (za, 2, 1),
        (za, 2, 2),
        (f1b, 0),
        (zb, 2, 0),
        (sg, 0),
        (zb, 2, 1),
        (d1, 0),
        (zb, 2, 2),
        (eg, 1),
        (eg, 2),
        (etotal.one,),
        (g2, 1),
        (etotal.two,),
        (ig, 0),
        (rg, 0),
        (d2, 1),
        (etotal.three,),
        (f1b, 1),
        (etotal.exchange,),
        (sg, 1),
        (d1, 1),
        (etotal.four,),
        (ig, 1),
        (rg, 1),
        (etotal.five,),
        (g2, 2),
        (d2, 2),
        (sg, 2),
        (stotal.one,),
        (f1b, 2),
        (stotal.two,),
        (d1, 2),
        (rg, 2),
        (rtotal.one,),
        (stotal.three,),
        (rtotal.two,),
        (ig, 2),
        (stotal.four,),
        (rtotal.three,),
        (stotal.five,),
        (rtotal.exchange,),
        (params,),
        (rtotal.four,),
        (rtotal.five,),
    ]
    for step, *arguments in plan:
        step(*arguments)
    for wait in finish:
        wait()


def kernel_call(shape, args):
    inner, own, block, depth = shape.inner, shape.own, shape.block, shape.depth
    wide, narrow, chips, images = shape.wide, shape.narrow, shape.chips, shape.images
    bf16, f32 = jnp.bfloat16, jnp.float32

    def struct(dims, kind):
        return jax.ShapeDtypeStruct(dims, kind)

    spread = [
        (9, chips, 2, inner // wide, own),
        (narrow, chips, 2, own // wide, block),
        (narrow, chips, 2, block // wide, own),
    ]
    outs = (
        [struct((rows, block), bf16) for rows in shape.rows]
        + [struct((rows, block), f32) for rows in shape.rows]
        + [struct(spread[2], f32), struct(spread[0], f32), struct((chips, 2, own // wide, depth), f32)]
        + [struct((1, own), f32)] * 4
        + [struct((1, block), f32)] * 2
    )
    anywhere = pl.BlockSpec(memory_space=pl.ANY)
    vmem = pl.BlockSpec(memory_space=pltpu.VMEM)

    def each_rows(columns, kind):
        return [pltpu.VMEM((rows, columns), kind) for rows in shape.rows]

    def padded():
        return [pltpu.VMEM((side + 2, side + 2, images, inner), bf16) for side in shape.maps]

    scratch = (
        [pltpu.VMEM((narrow, rows, block), bf16) for rows in shape.rows]
        + [
            pltpu.VMEM((depth, inner), bf16),
            pltpu.VMEM((9, inner, inner), bf16),
            pltpu.VMEM((inner, block), bf16),
        ]
        + each_rows(inner, f32)
        + each_rows(inner, f32)
        + each_rows(block, f32)
        + each_rows(block, bf16)
        + padded()
        + padded()
        + each_rows(inner, bf16)
        + each_rows(inner, bf16)
        + [pltpu.VMEM(dims, f32) for dims in spread]
        + [pltpu.VMEM((a, c, b, lanes), bf16) for a, c, _, b, lanes in spread]
        + [pltpu.VMEM((a, c, b, lanes), bf16) for a, c, _, b, lanes in spread]
        + [pltpu.VMEM((c, a, b, lanes), bf16) for a, c, _, b, lanes in spread]
        + [pltpu.VMEM(dims, bf16) for dims in spread]
        + [pltpu.VMEM((a, b, lanes), bf16) for a, _, _, b, lanes in spread[1:]]
        + [
            pltpu.VMEM((18, 2 * inner // 128, 128), f32),
            pltpu.VMEM((18, wide, 2 * inner // 128, 128), f32),
            pltpu.VMEM((8, inner), f32),
            pltpu.VMEM((96, inner), f32),
            pltpu.VMEM((narrow, 8, own), f32),
            pltpu.SemaphoreType.DMA((SEMAPHORES,)),
        ]
    )
    return pl.pallas_call(
        functools.partial(block_kernel, shape),
        out_shape=outs,
        in_specs=[anywhere] * 9 + [vmem] * 6,
        out_specs=[anywhere] * 9 + [vmem] * 6,
        scratch_shapes=scratch,
        compiler_params=pltpu.CompilerParams(
            collective_id=0, has_side_effects=True, vmem_limit_bytes=VMEM_BYTES
        ),
        name="bottleneck",
    )(*args)


VMEM_BYTES = 66 * 1000 * 1000


def kernel_body(shape, *arguments):
    inputs, upstreams = arguments[:3], arguments[3:6]
    reduce_weight, spatial_weight, expand_weight = arguments[6:9]
    vectors = arguments[9:]

    def flat(array):
        return jnp.transpose(array, (1, 2, 0, 3)).reshape(-1, array.shape[3])

    def unflat(array, side):
        return jnp.transpose(
            array.reshape(side, side, shape.images, array.shape[1]), (2, 0, 1, 3)
        )

    results = kernel_call(
        shape,
        [flat(x) for x in inputs]
        + [flat(u) for u in upstreams]
        + [
            reduce_weight,
            spatial_weight.reshape(9, shape.inner, shape.own),
            expand_weight,
        ]
        + [v.reshape(1, -1) for v in vectors],
    )
    maps = list(shape.maps)
    images = [unflat(r, side) for r, side in zip(results[:6], maps + maps)]
    weights = [
        results[6].reshape(reduce_weight.shape),
        results[7].reshape(spatial_weight.shape),
        results[8].reshape(expand_weight.shape),
    ]
    return tuple(images + weights + [r.reshape(-1) for r in results[9:]])


def body(mesh, *arguments):
    inputs, reduce_weight = arguments[0], arguments[6]
    shape = Shape(
        mesh,
        [x.shape[1] for x in arguments[:3]],
        inputs.shape[0],
        inputs.shape[3],
        arguments[8].shape[0] * mesh.shape["narrow"],
    )
    if shape.fits():
        return kernel_body(shape, *arguments)
    return plain_body(*arguments)


def solution(mesh):
    rows = P("wide", None, None, None)
    blocks = P("wide", None, None, "narrow")
    weights = [P(None, "narrow"), P(None, None, None, "narrow"), P("narrow", None)]
    vectors = [P("narrow")] * 6
    return jax.shard_map(
        functools.partial(body, mesh),
        mesh=mesh,
        in_specs=tuple([rows] * 3 + [blocks] * 3 + weights + vectors),
        out_specs=tuple([blocks] * 6 + weights + vectors),
        check_vma=False,
    )
```

```python
import functools

import jax
import jax.numpy as jnp
from jax import lax
from jax.experimental import pallas as pl
from jax.experimental.pallas import tpu as pltpu
from jax.sharding import PartitionSpec as P

EPS = 1e-05
LAYOUT = ("NHWC", "HWIO", "NHWC")


def silu_slope(argument):
    logistic = jax.nn.sigmoid(argument)
    return logistic * (1.0 + argument * (1.0 - logistic))


def spatial(inputs, kernel):
    return lax.conv_general_dilated(
        inputs,
        kernel,
        (1, 1),
        ((1, 1), (1, 1)),
        dimension_numbers=LAYOUT,
        preferred_element_type=jnp.float32,
    )


def kernel_grad(inputs, gradient):
    height, breadth = (gradient.shape[1], gradient.shape[2])
    padded = jnp.pad(inputs, ((0, 0), (1, 1), (1, 1), (0, 0)))
    taps = []
    for vertical in range(3):
        for lateral in range(3):
            window = padded[:, vertical : vertical + height, lateral : lateral + breadth, :]
            taps.append(
                jnp.einsum("bhwc,bhwo->co", window, gradient, preferred_element_type=jnp.float32)
            )
    return jnp.stack(taps).reshape(3, 3, inputs.shape[3], gradient.shape[3])


def sums_forward(hidden):
    return (jnp.sum(hidden, axis=(0, 1, 2)), jnp.sum(hidden * hidden, axis=(0, 1, 2)))


def normed_of(hidden, sums, samples):
    average = sums[0] / samples
    inverse = lax.rsqrt(sums[1] / samples - average * average + EPS)
    return ((hidden - average) * inverse, inverse)


def sums_backward(upstream, normed):
    return (jnp.sum(upstream, axis=(0, 1, 2)), jnp.sum(upstream * normed, axis=(0, 1, 2)))


def hidden_grad(upstream, normed, inverse, gain, sums, samples):
    return (
        gain * inverse * (upstream - sums[0] / samples - normed * (sums[1] / samples))
    ).astype(jnp.bfloat16)


def each(function, *lists):
    return [function(*items) for items in zip(*lists)]


def columns(array, axis):
    own = array.shape[axis] // lax.axis_size("narrow")
    return lax.dynamic_slice_in_dim(array, lax.axis_index("narrow") * own, own, axis)


def dot(form, left, right):
    return jnp.einsum(form, left, right, preferred_element_type=jnp.float32)


def plain_body(
    input_five,
    input_seven,
    input_nine,
    upstream_five,
    upstream_seven,
    upstream_nine,
    reduce_weight,
    spatial_weight,
    expand_weight,
    gain_first,
    shift_first,
    gain_second,
    shift_second,
    gain_third,
    shift_third,
):
    inputs = [input_five, input_seven, input_nine]
    upstreams = [upstream_five, upstream_seven, upstream_nine]
    samples = [
        x.shape[0] * lax.axis_size("wide") * x.shape[1] * x.shape[2] for x in inputs
    ]
    whole_reduce = lax.all_gather(reduce_weight, "narrow", axis=1, tiled=True)
    whole_spatial = lax.all_gather(spatial_weight, "narrow", axis=3, tiled=True)
    own_expand = lax.all_to_all(expand_weight, "narrow", 1, 0, tiled=True)
    vectors = jnp.stack([gain_first, shift_first, gain_second, shift_second])
    gain1, shift1, gain2, shift2 = lax.all_gather(vectors, "narrow", axis=1, tiled=True)

    hidden1 = each(lambda x: dot("bhwc,cd->bhwd", x, whole_reduce), inputs)
    sums1 = lax.psum(each(sums_forward, hidden1), "wide")
    normed1, inverse1 = zip(*each(normed_of, hidden1, sums1, samples))
    pre1 = each(lambda n: n * gain1 + shift1, normed1)
    active1 = each(lambda p: jax.nn.silu(p).astype(jnp.bfloat16), pre1)

    hidden2 = each(lambda a: spatial(a, whole_spatial), active1)
    sums2 = lax.psum(each(sums_forward, hidden2), "wide")
    normed2, inverse2 = zip(*each(normed_of, hidden2, sums2, samples))
    pre2 = each(lambda n: n * gain2 + shift2, normed2)
    active2 = each(lambda p: jax.nn.silu(p).astype(jnp.bfloat16), pre2)

    hidden3 = each(lambda a: dot("bhwi,id->bhwd", a, own_expand), active2)
    sums3 = lax.psum(each(sums_forward, hidden3), "wide")
    normed3, inverse3 = zip(*each(normed_of, hidden3, sums3, samples))
    summed = each(
        lambda n, x: n * gain_third + shift_third + columns(x, 3).astype(jnp.float32),
        normed3,
        inputs,
    )
    results = each(lambda z: jax.nn.silu(z).astype(jnp.bfloat16), summed)
    grads_z = each(lambda u, z: u.astype(jnp.float32) * silu_slope(z), upstreams, summed)
    back3 = lax.psum(each(sums_backward, grads_z, normed3), "wide")
    grad3 = each(
        lambda e, n, r, s, m: hidden_grad(e, n, r, gain_third, s, m),
        grads_z,
        normed3,
        inverse3,
        back3,
        samples,
    )
    expand_grad = sum(each(lambda a, g: dot("bhwi,bhwd->id", a, g), active2, grad3))
    active_grad2 = each(
        lambda g: lax.psum(
            dot("bhwd,id->bhwi", g, own_expand).astype(jnp.bfloat16), "narrow"
        ).astype(jnp.float32),
        grad3,
    )
    grads_2 = each(lambda a, p: a * silu_slope(p), active_grad2, pre2)
    back2 = lax.psum(each(sums_backward, grads_2, normed2), "wide")
    grad2 = each(
        lambda e, n, r, s, m: hidden_grad(e, n, r, gain2, s, m),
        grads_2,
        normed2,
        inverse2,
        back2,
        samples,
    )
    spatial_grad = sum(each(lambda a, g: kernel_grad(a, columns(g, 3)), active1, grad2))
    flipped = jnp.transpose(whole_spatial[::-1, ::-1], (0, 1, 3, 2))
    grads_1 = each(lambda g, p: spatial(g, flipped) * silu_slope(p), grad2, pre1)
    back1 = lax.psum(each(sums_backward, grads_1, normed1), "wide")
    grad1 = each(
        lambda e, n, r, s, m: hidden_grad(e, n, r, gain1, s, m),
        grads_1,
        normed1,
        inverse1,
        back1,
        samples,
    )
    reduce_grad = sum(each(lambda x, g: dot("bhwc,bhwd->cd", x, columns(g, 3)), inputs, grad1))
    own_reduce = columns(whole_reduce, 0)
    in_grads = each(lambda g, e: dot("bhwd,cd->bhwc", g, own_reduce) + e, grad1, grads_z)

    low = [g.astype(jnp.bfloat16) for g in (reduce_grad, spatial_grad, expand_grad)]
    low[2] = lax.all_to_all(low[2], "narrow", 0, 1, tiled=True)
    totals = [g.astype(jnp.float32) for g in lax.psum(low, "wide")]

    def params(back, part):
        shift = sum(s[0] for s in back)
        gain = sum(s[1] for s in back)
        return [part(gain), part(shift)]

    def own(vector):
        return columns(vector, 0)

    small = params(back1, own) + params(back2, own) + params(back3, lambda v: v)
    return tuple(results + in_grads + totals + small)


class Shape:
    def __init__(self, mesh, maps, images, depth, inner):
        self.wide, self.narrow = mesh.shape["wide"], mesh.shape["narrow"]
        self.chips = self.wide // 2
        self.maps = maps
        self.images = images
        self.depth, self.inner = depth, inner
        self.own = inner // self.narrow
        self.block = depth // self.narrow
        self.rows = [images * side * side for side in maps]
        self.samples = [float(rows * self.wide) for rows in self.rows]

    def fits(self):
        return (
            self.narrow >= 4
            and self.narrow % 2 == 0
            and self.chips == 4
            and self.wide == 8
            and min(self.maps) >= 3
            and self.block == self.inner
            and self.own % 128 == 0
            and self.images % 16 == 0
            and self.own % (16 * self.wide) == 0
            and self.inner % 512 == 0
        )


def cuts(side, most):
    longest = max(1, most // side)
    number = -(-side // longest)
    edges = [side * n // number for n in range(number + 1)]
    return [(a, b - a) for a, b in zip(edges, edges[1:])]


class Pool:
    def __init__(self, ref):
        self.ref, self.used = ref, 0

    def take(self):
        assert self.used < SEMAPHORES
        self.used += 1
        return self.ref.at[self.used - 1]


MESH = pl.DeviceIdType.MESH
INVERSE, MINUS, SCALE, OFFSET, SHIFTSUM, GAINSUM, LINEAR, CONSTANT = range(8)
GIVEN, SPARE = 72, 80
SEMAPHORES = 512
VMEM_BYTES = 67_000_000
SLAB, CHUNK = 28, 16
WEIGHT_PARTS = 3


def dot_nn(left, right):
    return lax.dot_general(
        left, right, (((1,), (0,)), ((), ())), preferred_element_type=jnp.float32
    )


def dot_nt(left, right):
    return lax.dot_general(
        left, right, (((1,), (1,)), ((), ())), preferred_element_type=jnp.float32
    )


def dot_tn(left, right):
    return lax.dot_general(
        left, right, (((0,), (0,)), ((), ())), preferred_element_type=jnp.float32
    )


def logistic(argument):
    return 0.5 * jnp.tanh(0.5 * argument) + 0.5


class Step:
    def __init__(self, key, run, time, after, rank, hook=None):
        self.key, self.run, self.time = key, run, time
        self.after, self.rank, self.hook = after, rank, hook
        self.ready = 0.0


def arrange(steps, trace=None):
    named = {step.key: step for step in steps}
    done = {}
    now = 0.0
    order = []
    waiting = list(steps)
    while waiting:
        best = None
        for place, step in enumerate(waiting):
            if any(key not in done for key, _ in step.after):
                continue
            at = max([step.ready] + [done[key] + delay for key, delay in step.after])
            choice = (max(at, now), step.rank, place)
            if best is None or choice < best[0]:
                best = (choice, step)
        (start, _, _), step = best
        now = start + step.time
        done[step.key] = now
        waiting.remove(step)
        order.append(step)
        if trace is not None:
            trace.append((start, now, step.key))
        if step.hook is not None:
            step.hook(now, named)
    return order


def block_kernel(shape, *refs):
    wide, narrow, chips = shape.wide, shape.narrow, shape.chips
    inner, own, block, images = shape.inner, shape.own, shape.block, shape.images
    maps = shape.maps
    refs = list(refs)

    def take(count):
        taken = refs[:count]
        del refs[:count]
        return taken

    x_in, u_in = take(3), take(3)
    rw_in, sw_in, ew_in = take(3)
    vec_in = take(6)
    y_out, i_out = take(3), take(3)
    rg_out, sg_out, eg_out = take(3)
    vec_out = take(6)
    xb = take(3)
    rwf, swf, ewf = take(3)
    h1, h2, h3, dz = take(3), take(3), take(3), take(3)
    apad, dpad = take(3), take(3)
    rin, rx = take(3), take(3)
    sacc, eacc, racc = take(3)
    slow, elow, rlow = take(3)
    sr1, er1, rr1 = take(3)
    sr2, er2, rr2 = take(3)
    sfin, efin, rfin = take(3)
    epz, rpz = take(2)
    stat_s, stat_r, sums, vec, vec_all = take(5)
    vec_own, vec_made = take(6), take(6)
    pool = Pool(*take(1))

    w = lax.axis_index("wide")
    z = lax.axis_index("narrow")
    core = lax.rem(w, 2)
    chip = lax.div(w, 2)
    sibling = chip * 2 + (1 - core)
    half = narrow // 2
    inward = jnp.where(z < half, z + 1, z - 1)
    outward = jnp.where(z < half, z - 1, z + 1)
    center = jnp.logical_or(z == half - 1, z == half)
    end = jnp.logical_or(z == 0, z == narrow - 1)
    k_own, k_a2, k_dh, k_p = [lax.rem(z + k, narrow) for k in range(4)]
    finish = []
    arrivals = []

    def once(wait):
        made = []

        def noted():
            if not made:
                made.append(True)
                wait()

        arrivals.append(noted)
        return noted

    def remote(source, target, device):
        send, recv = pool.take(), pool.take()

        def make():
            return pltpu.make_async_remote_copy(
                src_ref=source(),
                dst_ref=target(),
                send_sem=send,
                recv_sem=recv,
                device_id=device,
                device_id_type=MESH,
            )

        make().start()
        finish.append(lambda: make().wait_send())
        return once(lambda: make().wait_recv())

    def local(source, target):
        semaphore = pool.take()

        def make():
            return pltpu.make_async_copy(source(), target(), semaphore)

        make().start()
        return once(lambda: make().wait())

    def span(start, size, unit):
        return pl.ds(pl.multiple_of(start * unit, unit), size)

    def rows_of(g, cut):
        return pl.ds(cut[0] * maps[g] * images, cut[1] * maps[g] * images)

    slabs = [cuts(side, SLAB) for side in maps]
    chunks = [cuts(side, CHUNK) for side in maps]

    def lines(g, cut, function):
        size = maps[g] * images
        if cut[1] == 1:
            function(cut[0], pl.ds(cut[0] * size, size))
        else:
            pl.loop(cut[0], cut[0] + cut[1])(
                lambda y: function(y, pl.ds(pl.multiple_of(y * size, 16), size))
            )

    chip_x = chip + 1 - 2 * lax.rem(chip, 2)
    chip_y = lax.rem(chip + 2, chips)
    chip_far = lax.rem(chip_x + 2, chips)
    origins = [lax.rem(z + narrow - k, narrow) for k in range(1, narrow)]

    class Gather:
        def __init__(self, source, target):
            self.source, self.target = source, target
            self.from_x, self.from_y, self.far, self.crossed = [], [], [], []

        def first(self):
            self.arrived = [
                remote(
                    lambda peer=peer: self.source(w, peer),
                    lambda: self.target(w, z),
                    (w, peer),
                )
                for peer in [lax.rem(z + k, narrow) for k in range(1, narrow)]
            ]

        def send(self, holder, origin, part, device):
            def piece():
                return self.target(holder * 2 + core, origin, part)

            return remote(piece, piece, (device, z))

        def spread(self):
            for origin, wait in zip(origins, self.arrived):
                wait()
                self.from_x.append(self.send(chip, origin, None, chip_x * 2 + core))
                self.from_y.append(self.send(chip, origin, None, chip_y * 2 + core))
            for origin in origins:
                self.crossed.append(self.send(chip, origin, None, sibling))

        def relay(self):
            for origin, got_x, got_y in zip(origins, self.from_x, self.from_y):
                got_x()
                along_y = self.send(chip_x, origin, 0, chip_y * 2 + core)
                got_y()
                along_x = self.send(chip_y, origin, 1, chip_x * 2 + core)
                self.far.append((along_y, along_x))
            for origin in origins:
                self.crossed.append(self.send(chip_x, origin, None, sibling))
                self.crossed.append(self.send(chip_y, origin, None, sibling))

        def cross(self):
            for origin, waits in zip(origins, self.far):
                for wait in waits:
                    wait()
                self.crossed.append(self.send(chip_far, origin, None, sibling))

        def ready(self):
            for wait in self.crossed:
                wait()

    rw_piece, sw_piece, ew_piece = shape.depth // wide, inner // wide, own // wide
    part = 9 // WEIGHT_PARTS

    def half_of(h, size, unit, half):
        if half is None:
            return span(h, size, size)
        return pl.ds(pl.multiple_of(h * size + half * (size // 2), unit), size // 2)

    def sw_item(n):
        taps = pl.ds(n * part, part)
        return Gather(
            lambda h, peer: sw_in.at[taps, span(h, sw_piece, sw_piece), :],
            lambda h, o, half=None: swf.at[taps, half_of(h, sw_piece, 16, half), span(o, own, own)],
        )

    gathers = (
        [
            Gather(
                lambda h, peer: rw_in.at[span(h, rw_piece, rw_piece), :],
                lambda h, o, half=None: rwf.at[half_of(h, rw_piece, 16, half), span(o, own, own)],
            )
        ]
        + [sw_item(n) for n in range(WEIGHT_PARTS)]
        + [
            Gather(
                lambda h, peer: ew_in.at[span(h, ew_piece, ew_piece), span(peer, block, block)],
                lambda h, o, half=None: ewf.at[
                    pl.ds(pl.multiple_of(o * own + h * ew_piece, 16), ew_piece),
                    pl.ds(0, block) if half is None else pl.ds(half * (block // 2), block // 2),
                ],
            )
        ]
    )
    x_wait = [[None] * narrow for _ in range(3)]
    u_wait, y_wait = [None] * 3, [None] * 3
    own_waits, vec_waits = [], []

    def slot(kind, level, g):
        return (kind * 3 + level) * 3 + g

    def put(place, value):
        vec[place : place + 1, :] = value

    def get(place):
        return vec[place : place + 1, :]

    def begin():
        got = [local(lambda a=a: a, lambda b=b: b) for a, b in zip(vec_in, vec_own)]
        barrier = pltpu.get_barrier_semaphore()
        for k in range(1, wide):
            pl.semaphore_signal(
                barrier, inc=1, device_id=(lax.rem(w + k, wide), z), device_id_type=MESH
            )
        for k in range(1, narrow):
            pl.semaphore_signal(
                barrier, inc=1, device_id=(w, lax.rem(z + k, narrow)), device_id_type=MESH
            )
        for source, target in (
            (lambda: rw_in, lambda: rwf.at[:, span(z, own, own)]),
            (lambda: sw_in, lambda: swf.at[:, :, span(z, own, own)]),
            (lambda: ew_in.at[:, span(z, block, block)], lambda: ewf.at[span(z, own, own), :]),
        ):
            own_waits.append(local(source, target))
        for g in range(3):
            for k in range(narrow):
                x_wait[g][k] = local(
                    lambda g=g, k=k: x_in[g].at[:, pl.ds(k * block, block)],
                    lambda g=g, k=k: xb[g].at[k],
                )
        for wait in got:
            wait()
        vec_all[z] = jnp.concatenate(
            [v[...] for v in vec_own[:4]] + [jnp.zeros((4, own), jnp.float32)], axis=0
        )
        pl.semaphore_wait(barrier, wide - 1 + narrow - 1)
        for k in range(1, narrow):
            vec_waits.append(
                remote(lambda: vec_all.at[z], lambda: vec_all.at[z], (w, lax.rem(z + k, narrow)))
            )
        for item in gathers:
            item.first()

    def pads():
        for g in range(3):
            side = maps[g]
            for pad in (apad[g], dpad[g]):
                pad[0] = jnp.zeros((side + 2, images, inner), jnp.bfloat16)
                pad[side + 1] = jnp.zeros((side + 2, images, inner), jnp.bfloat16)
                for edge in (0, side + 1):
                    pad[1 : side + 1, edge] = jnp.zeros((side, images, inner), jnp.bfloat16)
        for acc in (sacc, eacc, racc):

            def clear(a, acc=acc):
                acc[a] = jnp.zeros(acc.shape[1:], jnp.float32)

            pl.loop(0, acc.shape[0])(clear)

    def vectors():
        for wait in vec_waits:
            wait()
        for row in range(4):
            put(
                GIVEN + row,
                jnp.concatenate([vec_all[k, row : row + 1, :] for k in range(narrow)], axis=1),
            )
        for row in (4, 5):
            put(GIVEN + row, vec_own[row][...])

    tiles = inner // 128
    stat_sems, stat_arrived = {}, {}

    def stats_all(e):
        send, recv = stat_sems[e]
        return pltpu.make_async_remote_copy(
            src_ref=stat_r.at[e, pl.ds(0, wide - 1)],
            dst_ref=stat_r.at[e, pl.ds(0, wide - 1)],
            send_sem=send,
            recv_sem=recv,
            device_id=(sibling, z),
            device_id_type=MESH,
        )

    def stats_wait(e):
        stat_arrived[e]()
        total = stat_r[e, 0]
        for k in range(1, wide):
            total = total + stat_r[e, k]
        return [
            jnp.concatenate(
                [total[t * tiles + b : t * tiles + b + 1, :] for b in range(tiles)], axis=1
            )
            for t in range(2)
        ]

    class Sums:
        def __init__(self, e):
            self.row = 2 * e
            self.e = e

        def clear(self):
            sums[self.row : self.row + 2, :] = jnp.zeros((2, inner), jnp.float32)

        def add(self, first, second):
            sums[self.row : self.row + 1, :] += jnp.sum(first, axis=0, keepdims=True)
            sums[self.row + 1 : self.row + 2, :] += jnp.sum(second, axis=0, keepdims=True)

    totals_of = {e: Sums(e) for e in range(18)}

    def send_sums(e):
        row = totals_of[e].row
        for t in range(2):
            for b in range(tiles):
                stat_s[e, t * tiles + b : t * tiles + b + 1, :] = sums[
                    row + t : row + t + 1, b * 128 : (b + 1) * 128
                ]
        stat_r[e, w] = stat_s[e]
        send, recv = pool.take(), pool.take()
        stat_sems[e] = (send, recv)
        stat_arrived[e] = once(lambda: stats_all(e).wait_recv())
        finish.append(lambda: stats_all(e).wait_send())

        def one(k, carry):
            pltpu.make_async_remote_copy(
                src_ref=stat_s.at[e],
                dst_ref=stat_r.at[e, w],
                send_sem=send,
                recv_sem=recv,
                device_id=(lax.rem(w + k, wide), z),
                device_id_type=MESH,
            ).start()
            return carry

        lax.fori_loop(1, wide, one, 0)

    def norm_vectors(g, level):
        first, second = stats_wait(g * 6 + level)
        mean = first / shape.samples[g]
        inverse = lax.rsqrt(second / shape.samples[g] - mean * mean + EPS)
        scale = inverse * get(GIVEN + 2 * level)
        put(slot(INVERSE, level, g), inverse)
        put(slot(MINUS, level, g), -mean * inverse)
        put(slot(SCALE, level, g), scale)
        put(slot(OFFSET, level, g), get(GIVEN + 2 * level + 1) - mean * scale)

    def back_vectors(g, level):
        shift_sum, gain_sum = stats_wait(g * 6 + 5 - level)
        put(slot(SHIFTSUM, level, g), shift_sum)
        put(slot(GAINSUM, level, g), gain_sum)
        scale = get(slot(SCALE, level, g))
        c1 = scale * (gain_sum / shape.samples[g])
        put(slot(LINEAR, level, g), -get(slot(INVERSE, level, g)) * c1)
        put(slot(CONSTANT, level, g), -get(slot(MINUS, level, g)) * c1 - scale * (shift_sum / shape.samples[g]))

    def f1(g, cut):
        run = totals_of[g * 6]
        if cut[0] == 0:
            for wait in x_wait[g]:
                wait()
            run.clear()
        rows = rows_of(g, cut)
        left = jnp.concatenate([xb[g][k, rows, :] for k in range(narrow)], axis=1)
        result = dot_nn(left, rwf[...])
        h1[g][rows, :] = result
        run.add(result, result * result)

    def f1_end(g):
        send_sums(g * 6)
        u_wait[g] = local(lambda: u_in[g], lambda: xb[g].at[k_dh])

    def a1(g):
        scale, offset = get(slot(SCALE, 0, g)), get(slot(OFFSET, 0, g))
        side = maps[g]

        def one(y, rows):
            pre = h1[g][rows, :] * scale + offset
            value = (pre * logistic(pre)).astype(jnp.bfloat16)
            apad[g][y + 1, pl.ds(1, side)] = value.reshape(side, images, inner)

        lines(g, (0, side), one)

    def windows(pad, g, cut, lines_of_taps):
        side = maps[g]
        return jnp.concatenate(
            [
                pad[cut[0] + i : cut[0] + i + cut[1], j : j + side].reshape(
                    cut[1] * side * images, inner
                )
                for i in lines_of_taps
                for j in range(3)
            ],
            axis=1,
        )

    def f2(g, n, cut):
        run = totals_of[g * 6 + 1]
        rows = rows_of(g, cut)
        result = dot_nn(windows(apad[g], g, cut, (n,)), swf[3 * n : 3 * n + 3].reshape(-1, inner))
        if n > 0:
            result = result + h2[g][rows, :]
        h2[g][rows, :] = result
        if n == 2:
            if cut[0] == 0:
                run.clear()
            run.add(result, result * result)

    def a2(g):
        scale, offset = get(slot(SCALE, 1, g)), get(slot(OFFSET, 1, g))

        def one(y, rows):
            pre = h2[g][rows, :] * scale + offset
            xb[g][k_a2, rows, :] = (pre * logistic(pre)).astype(jnp.bfloat16)

        lines(g, (0, maps[g]), one)

    def f3(g):
        run = totals_of[g * 6 + 2]
        run.clear()
        for cut in slabs[g]:
            rows = rows_of(g, cut)
            result = dot_nn(xb[g][k_a2, rows, :], ewf[...])
            h3[g][rows, :] = result
            run.add(result, result * result)

    def a3(g):
        run = totals_of[g * 6 + 3]
        run.clear()
        scale, offset = get(slot(SCALE, 2, g)), get(slot(OFFSET, 2, g))
        inverse, minus = get(slot(INVERSE, 2, g)), get(slot(MINUS, 2, g))

        def one(y, rows):
            hidden = h3[g][rows, :]
            total = hidden * scale + offset + xb[g][k_own, rows, :].astype(jnp.float32)
            sig = logistic(total)
            xb[g][k_p, rows, :] = (total * sig).astype(jnp.bfloat16)
            slope = sig * (1.0 + total * (1.0 - sig))
            grad = xb[g][k_dh, rows, :].astype(jnp.float32) * slope
            dz[g][rows, :] = grad
            run.add(grad, grad * (hidden * inverse + minus))

        lines(g, (0, maps[g]), one)

    def a3_end(g):
        send_sums(g * 6 + 3)
        y_wait[g] = local(lambda: xb[g].at[k_p], lambda: y_out[g])

    def b3(g, cut):
        scale, k1, k0 = get(slot(SCALE, 2, g)), get(slot(LINEAR, 2, g)), get(slot(CONSTANT, 2, g))
        rows = rows_of(g, cut)
        value = dz[g][rows, :] * scale + h3[g][rows, :] * k1 + k0
        low = value.astype(jnp.bfloat16)
        xb[g][k_dh, rows, :] = low
        xb[g][k_p, rows, :] = dot_nt(low, ewf[...]).astype(jnp.bfloat16)
        c = chunks[g].index(cut)
        reductions[g, c] = copies = Reduction(g, c)
        pl.when(end)(lambda: copies.to_inner().start())

    def eg(g):
        result = dot_tn(xb[g][k_a2], xb[g][k_dh])
        for k in range(narrow):
            piece = result[k * own : (k + 1) * own, :].reshape(eacc.shape[1:])
            eacc[k] += piece

    reductions = {}

    class Reduction:
        def __init__(self, g, c):
            self.g, self.rows = g, rows_of(g, chunks[g][c])
            self.sems = [pool.take() for _ in range(5)]
            self.inwards = once(self.add_outer)
            self.across = once(self.add_other)
            self.home = once(lambda: pl.when(end)(lambda: self.to_center().wait_recv()))
            finish.append(self.sent)

        def copy(self, source, target, send, recv, device):
            return pltpu.make_async_remote_copy(
                src_ref=source.at[self.rows, :],
                dst_ref=target.at[self.rows, :],
                send_sem=self.sems[send],
                recv_sem=self.sems[recv],
                device_id=(w, device),
                device_id_type=MESH,
            )

        def to_inner(self):
            return self.copy(xb[self.g].at[k_p], rin[self.g], 0, 1, inward)

        def to_center(self):
            return self.copy(xb[self.g].at[k_p], rx[self.g], 2, 3, inward)

        def to_outer(self):
            return self.copy(rx[self.g], rx[self.g], 4, 3, outward)

        def add_outer(self):
            g, rows = self.g, self.rows

            @pl.when(jnp.logical_not(end))
            def _():
                self.to_inner().wait_recv()
                xb[g][k_p, rows, :] = (
                    xb[g][k_p, rows, :].astype(jnp.float32) + rin[g][rows, :].astype(jnp.float32)
                ).astype(jnp.bfloat16)
                pl.when(center)(lambda: self.to_center().start())
                pl.when(jnp.logical_not(center))(lambda: self.to_inner().start())

        def add_other(self):
            g, rows = self.g, self.rows

            @pl.when(jnp.logical_not(end))
            def _():
                self.to_center().wait_recv()

                @pl.when(center)
                def _():
                    rx[g][rows, :] = (
                        rx[g][rows, :].astype(jnp.float32)
                        + xb[g][k_p, rows, :].astype(jnp.float32)
                    ).astype(jnp.bfloat16)

                self.to_outer().start()

        def sent(self):
            pl.when(center)(lambda: self.to_center().wait_send())
            pl.when(jnp.logical_not(center))(lambda: self.to_inner().wait_send())
            pl.when(jnp.logical_not(end))(lambda: self.to_outer().wait_send())

    def za(g, c):
        reductions[g, c].inwards()

    def zb(g, c):
        reductions[g, c].across()

    def g2(g, c):
        run = totals_of[g * 6 + 4]
        if c == 0:
            run.clear()
        reductions[g, c].home()
        scale, offset = get(slot(SCALE, 1, g)), get(slot(OFFSET, 1, g))
        inverse, minus = get(slot(INVERSE, 1, g)), get(slot(MINUS, 1, g))

        def one(y, rows):
            hidden = h2[g][rows, :]
            pre = hidden * scale + offset
            sig = logistic(pre)
            grad = rx[g][rows, :].astype(jnp.float32) * (sig * (1.0 + pre * (1.0 - sig)))
            h3[g][rows, :] = grad
            run.add(grad, grad * (hidden * inverse + minus))

        lines(g, chunks[g][c], one)

    def d2(g):
        scale, k1, k0 = get(slot(SCALE, 1, g)), get(slot(LINEAR, 1, g)), get(slot(CONSTANT, 1, g))
        side = maps[g]

        def one(y, rows):
            value = h3[g][rows, :] * scale + h2[g][rows, :] * k1 + k0
            dpad[g][y + 1, pl.ds(1, side)] = value.astype(jnp.bfloat16).reshape(side, images, inner)

        lines(g, (0, side), one)

    def sg(g):
        side = maps[g]
        left = apad[g][1 : side + 1, 1 : side + 1].reshape(shape.rows[g], inner)
        right = jnp.concatenate(
            [
                dpad[g][2 - i : 2 - i + side, 2 - j : 2 - j + side, :, span(z, own, own)].reshape(
                    shape.rows[g], own
                )
                for i in range(3)
                for j in range(3)
            ],
            axis=1,
        )
        result = dot_tn(left, right)
        for t in range(9):
            piece = result[:, t * own : (t + 1) * own].reshape(sacc.shape[1:])
            sacc[t] += piece

    def f1b(g, cut):
        run = totals_of[g * 6 + 5]
        if cut[0] == 0:
            run.clear()
        rows = rows_of(g, cut)
        left = windows(dpad[g], g, cut, range(3))
        right = jnp.concatenate([swf[8 - t] for t in range(9)], axis=1)
        h2[g][rows, :] = dot_nt(left, right)

    def g1(g, cut):
        run = totals_of[g * 6 + 5]
        scale, offset = get(slot(SCALE, 0, g)), get(slot(OFFSET, 0, g))
        inverse, minus = get(slot(INVERSE, 0, g)), get(slot(MINUS, 0, g))

        def one(y, rows):
            hidden = h1[g][rows, :]
            pre = hidden * scale + offset
            sig = logistic(pre)
            grad = h2[g][rows, :] * (sig * (1.0 + pre * (1.0 - sig)))
            h2[g][rows, :] = grad
            run.add(grad, grad * (hidden * inverse + minus))

        lines(g, cut, one)

    def d1(g):
        scale, k1, k0 = get(slot(SCALE, 0, g)), get(slot(LINEAR, 0, g)), get(slot(CONSTANT, 0, g))

        def one(y, rows):
            value = h2[g][rows, :] * scale + h1[g][rows, :] * k1 + k0
            xb[g][k_dh, rows, :] = value.astype(jnp.bfloat16)

        lines(g, (0, maps[g]), one)

    def ig(g):
        for cut in slabs[g]:
            rows = rows_of(g, cut)
            right = rwf[span(z, block, block), :]
            h3[g][rows, :] = dot_nt(xb[g][k_dh, rows, :], right) + dz[g][rows, :]
        finish.append(local(lambda: h3[g], lambda: i_out[g]))

    def rg(g):
        result = dot_tn(xb[g][k_own], xb[g][k_dh])
        for k in range(narrow):
            piece = result[:, k * own : (k + 1) * own].reshape(racc.shape[1:])
            racc[k] += piece

    class Total:
        def __init__(self, acc, low, first, second, final, piece, out):
            self.acc, self.low, self.first, self.second = acc, low, first, second
            self.final, self.piece, self.out = final, piece, out
            self.count = acc.shape[0]

        def one(self):
            def cast(a):
                self.low[a] = self.acc[a, :, 1 - core].astype(jnp.bfloat16)

            pl.loop(0, self.count)(cast)
            self.got1 = remote(lambda: self.low, lambda: self.first, (sibling, z))

        def two(self):
            self.got1()

            def add(a):
                self.first[a] = (
                    self.first[a].astype(jnp.float32) + self.acc[a, :, core]
                ).astype(jnp.bfloat16)

            pl.loop(0, self.count)(add)
            self.got2 = []
            for j in range(1, chips):
                peer = lax.rem(chip + j, chips)
                self.got2.append(
                    remote(
                        lambda peer=peer: self.first.at[:, peer],
                        lambda: self.second.at[chip],
                        (peer * 2 + core, z),
                    )
                )

        def three(self):
            for wait in self.got2:
                wait()
            self.second[chip] = self.first[:, chip]
            target = self.final.at[:, chip, core] if self.piece is None else self.piece

            def add(a):
                total = self.second[0, a].astype(jnp.float32)
                for k in range(1, chips):
                    total = total + self.second[k, a].astype(jnp.float32)
                target[a] = total.astype(jnp.bfloat16)

            pl.loop(0, self.count)(add)
            if self.piece is None:
                self.send_pieces()
                return
            self.got3 = []
            for k in range(1, narrow):
                peer = lax.rem(z + k, narrow)
                self.got3.append(
                    remote(
                        lambda peer=peer: self.piece.at[peer],
                        lambda: self.final.at[z, chip, core],
                        (w, peer),
                    )
                )
            self.final[z, chip, core] = self.piece[z]

        def exchange(self):
            for wait in self.got3:
                wait()
            self.send_pieces()

        def send_pieces(self):
            self.got4, self.got5 = [], []

            def piece():
                return self.final.at[:, chip, core]

            for j in range(1, chips):
                peer = lax.rem(chip + j, chips)
                self.got4.append((j, remote(piece, piece, (peer * 2 + core, z))))
            self.got5.append(remote(piece, piece, (sibling, z)))

        def four(self):
            for j, arrived in self.got4:
                arrived()
                holder = lax.rem(chip + chips - j, chips)

                def piece(holder=holder):
                    return self.final.at[:, holder, core]

                self.got5.append(remote(piece, piece, (sibling, z)))

        def five(self):
            for wait in self.got5:
                wait()
            finish.append(local(lambda: self.final, lambda: self.out))

    stotal = Total(sacc, slow, sr1, sr2, sfin, None, sg_out)
    etotal = Total(eacc, elow, er1, er2, efin, epz, eg_out)
    rtotal = Total(racc, rlow, rr1, rr2, rfin, rpz, rg_out)

    def params():
        for place in range(6):
            level, kind = place // 2, GAINSUM if place % 2 == 0 else SHIFTSUM
            total = sum(get(slot(kind, level, g)) for g in range(3))
            if level == 2:
                vec_made[place][...] = total
            else:
                put(SPARE, total)
                vec_made[place][...] = vec[SPARE : SPARE + 1, span(z, own, own)]
            finish.append(
                local(lambda place=place: vec_made[place], lambda place=place: vec_out[place])
            )

    steps = []
    order = T.order

    def add(key, run, time, after, rank, hook=None):
        steps.append(Step(key, run, time, after, rank, hook))

    START, CLEAR, VECTORS = (begin,), (pads,), (vectors,)
    add(START, begin, 5.0, [], 0)
    add(CLEAR, pads, 1.0, [(START, 0.0)], 1)
    add(VECTORS, vectors, 0.2, [(START, 5.0)], 2)

    def spread(n):
        gathers[n].spread()

    def relay(n):
        gathers[n].relay()

    def cross(n):
        gathers[n].cross()

    def ready(n):
        if n == 0:
            for wait in own_waits:
                wait()
        gathers[n].ready()

    for n in range(len(gathers)):
        wait = T.xy[n]
        for f, time, after in (
            (spread, 0.2, [(START, T.z[n])]),
            (relay, 0.2, [((spread, n), wait)]),
            (cross, 0.1, [((relay, n), wait * 0.7)]),
            (ready, 0.1, [((cross, n), 1.5)]),
        ):
            if n > 0 and f is not ready:
                after = after + [((f, n - 1), T.xy[n] * 0.8 if f is relay else 0.0)]
            add((f, n), functools.partial(f, n), time, after, 0.0 if n < 4 else 0.1)

    link = {za: 0.0, zb: 0.0, g2: 0.0}

    def transfer(key, size):
        def hook(now, named):
            link[key[0]] = max(link[key[0]], now) + size * T.hop
            named[key].ready = link[key[0]] + T.lat

        return hook

    class Do:
        def __init__(self, g):
            self.g = g

        def f1(self, s):
            f1(self.g, slabs[self.g][s])
            if s == len(slabs[self.g]) - 1:
                f1_end(self.g)

        def a1(self):
            norm_vectors(self.g, 0)
            a1(self.g)

        def f2(self, n, s):
            f2(self.g, n, slabs[self.g][s])
            if n == 2 and s == len(slabs[self.g]) - 1:
                send_sums(self.g * 6 + 1)

        def a2(self):
            norm_vectors(self.g, 1)
            a2(self.g)
            f3(self.g)
            send_sums(self.g * 6 + 2)

        def a3(self):
            norm_vectors(self.g, 2)
            u_wait[self.g]()
            a3(self.g)
            a3_end(self.g)

        def b3(self, c):
            if c == 0:
                back_vectors(self.g, 2)
                y_wait[self.g]()
            b3(self.g, chunks[self.g][c])

        def g2(self, c):
            g2(self.g, c)
            if c == len(chunks[self.g]) - 1:
                send_sums(self.g * 6 + 4)

        def d2(self):
            back_vectors(self.g, 1)
            d2(self.g)

        def f1b(self, s):
            f1b(self.g, slabs[self.g][s])
            g1(self.g, slabs[self.g][s])
            if s == len(slabs[self.g]) - 1:
                send_sums(self.g * 6 + 5)

        def d1(self):
            back_vectors(self.g, 0)
            d1(self.g)

    before = None
    for turn, g in enumerate(order):
        do = Do(g)
        size = [shape.rows[g] * n / maps[g] for _, n in chunks[g]]
        scale = shape.rows[g] / 1000.0
        per, last = len(slabs[g]), len(chunks[g]) - 1
        early, late = 2 + turn * 0.3, 4 + turn * 0.3
        for s in range(per):
            after = [((ready, 0), 0.0)] if s == 0 else [((f1, g, s - 1), 0.0)]
            add((f1, g, s), functools.partial(do.f1, s), T.f1 * scale / per, after, early)
        after = [((f1, g, per - 1), T.stat0), (VECTORS, 0.0), (CLEAR, 0.0)]
        add((a1, g), do.a1, T.a1 * scale + 0.2, after, early)
        behind = (a1, g)
        for n in range(3):
            for s in range(per):
                after = [(behind, 0.0), ((ready, n + 1), 0.0)]
                behind = (f2, g, n, s)
                add(behind, functools.partial(do.f2, n, s), T.f2 * scale / per / 3, after, early - 0.1 * n)
        after = [(behind, T.stat), ((ready, 4), 0.0)]
        add((a2, g), do.a2, T.a2 * scale + 0.2, after, early - 0.5)
        add((a3, g), do.a3, T.a3 * scale + 0.2, [((a2, g), T.stat)], early - 0.5)
        for c in range(last + 1):
            after = [((a3, g), T.stat)] if c == 0 else [((b3, g, c - 1), 0.0)]
            if c == 0 and before is not None:
                after.append((before, 0.0))
            add((b3, g, c), functools.partial(do.b3, c), T.b3 * size[c] / 1000.0, after, 1 + turn * 0.3, transfer((za, g, c), size[c]))
            after = [((b3, g, c), 0.0)] + ([((za, g, c - 1), 0.0)] if c else [])
            add((za, g, c), functools.partial(za, g, c), T.za, after, 0, transfer((zb, g, c), size[c]))
            after = [((za, g, c), 0.0)] + ([((zb, g, c - 1), 0.0)] if c else [])
            add((zb, g, c), functools.partial(zb, g, c), T.za, after, 0, transfer((g2, g, c), size[c]))
            after = [((zb, g, c), 0.0)] + ([((g2, g, c - 1), 0.0)] if c else [])
            add((g2, g, c), functools.partial(do.g2, c), T.g2 * size[c] / 1000.0, after, late - 1.5)
        before = (b3, g, last)
        add((d2, g), do.d2, T.d2 * scale + 0.2, [((g2, g, last), T.stat)], late - 1)
        add((eg, g), functools.partial(eg, g), T.eg * scale, [(before, 0.0)], 6)
        final = turn == len(order) - 1
        add((sg, g), functools.partial(sg, g), T.sg * scale, [((d2, g), 0.0)], late - T.sg_rank if turn else 5)
        for s in range(per):
            after = [((d2, g), 0.0)] if s == 0 else [((f1b, g, s - 1), 0.0)]
            add((f1b, g, s), functools.partial(do.f1b, s), T.f1b * scale / per, after, late - 0.4)
        after = [((f1b, g, per - 1), T.stat), ((eg, g), 0.0)]
        add((d1, g), do.d1, T.d1 * scale + 0.2, after, late - 0.5)
        add((rg, g), functools.partial(rg, g), T.rg * scale, [((d1, g), 0.0)], late - 0.5)
        add((ig, g), functools.partial(ig, g), T.ig * scale, [((d1, g), 0.0)], 8)
    for total, source, xfer in ((etotal, eg, 3.0), (stotal, sg, 6.5), (rtotal, rg, 3.5)):
        add((total, 1), total.one, 0.3, [((source, g), 0.0) for g in range(3)], 1)
        add((total, 2), total.two, 0.3, [((total, 1), 2.5)], 1)
        after = [((total, 2), xfer + 2)]
        if total is etotal:
            after.append(((zb, order[-1], len(chunks[order[-1]]) - 1), 0.0))
        add((total, 3), total.three, 0.4, after, 1)
        if total.piece is not None:
            add((total, 4), total.exchange, 0.2, [((total, 3), 2.5)], 1)
        after = [((total, 3 if total.piece is None else 4), xfer + 2)]
        add((total, 5), total.four, 0.2, after, 1)
        add((total, 6), total.five, 0.1, [((total, 5), 2.5)], 7)
    add((params,), params, 0.3, [((d1, g), 0.0) for g in range(3)], 7)
    for step in arrange(steps, TRACE)[:PLAN_END]:
        step.run()
    for wait in arrivals:
        wait()
    for wait in finish:
        wait()


PLAN_END = None
TRACE = None


class T:
    order = (1, 2, 0)
    z = (8.0, 14.5, 18.5, 23.0, 24.0)
    xy = (5.5, 5.0, 5.0, 5.0, 2.0)
    stat0, stat = 4.5, 3.5
    f1, a1, f2, a2, a3, b3 = 2.5, 0.7, 5.4, 1.3, 2.0, 2.1
    hop, lat, za = 0.022, 1.5, 0.1
    g2, d2, eg, sg, f1b, d1, rg, ig = 1.4, 0.4, 0.7, 2.0, 6.3, 0.4, 0.7, 0.7
    sg_rank = 0.45


def kernel_call(shape, args):
    inner, own, block, depth = shape.inner, shape.own, shape.block, shape.depth
    wide, narrow, chips, images = shape.wide, shape.narrow, shape.chips, shape.images
    bf16, f32 = jnp.bfloat16, jnp.float32

    def struct(dims, kind):
        return jax.ShapeDtypeStruct(dims, kind)

    spread = [
        (9, chips, 2, inner // wide, own),
        (narrow, chips, 2, own // wide, block),
        (narrow, chips, 2, block // wide, own),
    ]
    outs = (
        [struct((rows, block), bf16) for rows in shape.rows]
        + [struct((rows, block), f32) for rows in shape.rows]
        + [struct(spread[2], bf16), struct(spread[0], bf16), struct(spread[1], bf16)]
        + [struct((1, own), f32)] * 4
        + [struct((1, block), f32)] * 2
    )
    anywhere = pl.BlockSpec(memory_space=pl.ANY)

    def each_rows(columns, kind):
        return [pltpu.VMEM((rows, columns), kind) for rows in shape.rows]

    def padded():
        return [pltpu.VMEM((side + 2, side + 2, images, inner), bf16) for side in shape.maps]

    scratch = (
        [pltpu.VMEM((narrow, rows, block), bf16) for rows in shape.rows]
        + [
            pltpu.VMEM((depth, inner), bf16),
            pltpu.VMEM((9, inner, inner), bf16),
            pltpu.VMEM((inner, block), bf16),
        ]
        + each_rows(inner, f32)
        + each_rows(inner, f32)
        + each_rows(block, f32)
        + each_rows(block, f32)
        + padded()
        + padded()
        + each_rows(inner, bf16)
        + each_rows(inner, bf16)
        + [pltpu.VMEM(dims, f32) for dims in spread]
        + [pltpu.VMEM((a, c, b, lanes), bf16) for a, c, _, b, lanes in spread]
        + [pltpu.VMEM((a, c, b, lanes), bf16) for a, c, _, b, lanes in spread]
        + [pltpu.VMEM((c, a, b, lanes), bf16) for a, c, _, b, lanes in spread]
        + [pltpu.VMEM(dims, bf16) for dims in spread]
        + [pltpu.VMEM((a, b, lanes), bf16) for a, _, _, b, lanes in spread[1:]]
        + [
            pltpu.VMEM((18, 2 * inner // 128, 128), f32),
            pltpu.VMEM((18, wide, 2 * inner // 128, 128), f32),
            pltpu.VMEM((40, inner), f32),
            pltpu.VMEM((96, inner), f32),
            pltpu.VMEM((narrow, 8, own), f32),
        ]
        + ([pltpu.VMEM((1, own), f32)] * 4 + [pltpu.VMEM((1, block), f32)] * 2) * 2
        + [pltpu.SemaphoreType.DMA((SEMAPHORES,))]
    )
    return pl.pallas_call(
        functools.partial(block_kernel, shape),
        out_shape=outs,
        in_specs=[anywhere] * 15,
        out_specs=[anywhere] * 15,
        scratch_shapes=scratch,
        compiler_params=pltpu.CompilerParams(
            collective_id=0, has_side_effects=True, vmem_limit_bytes=VMEM_BYTES
        ),
        name="bottleneck",
    )(*args)


def last_kernel(shape, *refs):
    narrow, block = shape.narrow, shape.block
    source, target, held, high, sems = refs[:15], refs[15:30], refs[30:45], refs[45:48], refs[48]
    pool = Pool(sems)
    finish = []

    def copy(source, target):
        semaphore = pool.take()

        def make():
            return pltpu.make_async_copy(source, target, semaphore)

        make().start()
        return lambda: make().wait()

    places = [6, 7, 8, 3, 4, 5, 0, 1, 2] + list(range(9, 15))
    got = {place: copy(source[place], held[place]) for place in places}
    for place in places:
        got[place]()
        if place not in (6, 7, 8):
            finish.append(copy(held[place], target[place]))
            continue
        wide = high[place - 6]

        def widen(a, place=place, wide=wide):
            wide[a] = held[place][a].astype(jnp.float32)

        pl.loop(0, wide.shape[0])(widen)
        if place < 8:
            finish.append(copy(wide, target[place]))
            continue
        for k in range(narrow):
            finish.append(
                copy(wide.at[k], target[place].at[:, :, :, pl.ds(k * block, block)])
            )
    for wait in finish:
        wait()


def last_call(shape, args):
    f32 = jnp.float32
    outs = [jax.ShapeDtypeStruct(a.shape, f32 if 6 <= n < 9 else a.dtype) for n, a in enumerate(args)]
    outs[8] = jax.ShapeDtypeStruct((*args[8].shape[1:-1], shape.depth), f32)
    anywhere = pl.BlockSpec(memory_space=pl.ANY)
    return pl.pallas_call(
        functools.partial(last_kernel, shape),
        out_shape=outs,
        in_specs=[anywhere] * 15,
        out_specs=[anywhere] * 15,
        scratch_shapes=[pltpu.VMEM(a.shape, a.dtype) for a in args]
        + [pltpu.VMEM(a.shape, f32) for a in args[6:9]]
        + [pltpu.SemaphoreType.DMA((64,))],
        compiler_params=pltpu.CompilerParams(vmem_limit_bytes=VMEM_BYTES),
        name="results",
    )(*args)


def kernel_body(shape, *arguments):
    inputs, upstreams = arguments[:3], arguments[3:6]
    reduce_weight, spatial_weight, expand_weight = arguments[6:9]
    vectors = arguments[9:]

    def flat(array):
        return jnp.transpose(array, (1, 2, 0, 3)).reshape(-1, array.shape[3])

    def unflat(array, side):
        return jnp.transpose(
            array.reshape(side, side, shape.images, array.shape[1]), (2, 0, 1, 3)
        )

    results = kernel_call(
        shape,
        [flat(x) for x in inputs]
        + [flat(u) for u in upstreams]
        + [
            reduce_weight,
            spatial_weight.reshape(9, shape.inner, shape.own),
            expand_weight,
        ]
        + [v.reshape(1, -1) for v in vectors],
    )
    results = last_call(shape, results)
    maps = list(shape.maps)
    images = [unflat(r, side) for r, side in zip(results[:6], maps + maps)]
    weights = [
        results[6].reshape(reduce_weight.shape),
        results[7].reshape(spatial_weight.shape),
        results[8].reshape(expand_weight.shape),
    ]
    return tuple(images + weights + [r.reshape(-1) for r in results[9:]])


def body(mesh, *arguments):
    inputs, reduce_weight = arguments[0], arguments[6]
    shape = Shape(
        mesh,
        [x.shape[1] for x in arguments[:3]],
        inputs.shape[0],
        inputs.shape[3],
        arguments[8].shape[0] * mesh.shape["narrow"],
    )
    if shape.fits():
        return kernel_body(shape, *arguments)
    return plain_body(*arguments)


def solution(mesh):
    rows = P("wide", None, None, None)
    blocks = P("wide", None, None, "narrow")
    weights = [P(None, "narrow"), P(None, None, None, "narrow"), P("narrow", None)]
    vectors = [P("narrow")] * 6
    return jax.shard_map(
        functools.partial(body, mesh),
        mesh=mesh,
        in_specs=tuple([rows] * 3 + [blocks] * 3 + weights + vectors),
        out_specs=tuple([blocks] * 6 + weights + vectors),
        check_vma=False,
    )
```

```python
import functools

import jax
import jax.numpy as jnp
from jax import lax
from jax.experimental import pallas as pl
from jax.experimental.pallas import tpu as pltpu
from jax.sharding import PartitionSpec as P

EPS = 1e-05
LAYOUT = ("NHWC", "HWIO", "NHWC")


def silu_slope(argument):
    logistic = jax.nn.sigmoid(argument)
    return logistic * (1.0 + argument * (1.0 - logistic))


def spatial(inputs, kernel):
    return lax.conv_general_dilated(
        inputs,
        kernel,
        (1, 1),
        ((1, 1), (1, 1)),
        dimension_numbers=LAYOUT,
        preferred_element_type=jnp.float32,
    )


def kernel_grad(inputs, gradient):
    height, breadth = (gradient.shape[1], gradient.shape[2])
    padded = jnp.pad(inputs, ((0, 0), (1, 1), (1, 1), (0, 0)))
    taps = []
    for vertical in range(3):
        for lateral in range(3):
            window = padded[:, vertical : vertical + height, lateral : lateral + breadth, :]
            taps.append(
                jnp.einsum("bhwc,bhwo->co", window, gradient, preferred_element_type=jnp.float32)
            )
    return jnp.stack(taps).reshape(3, 3, inputs.shape[3], gradient.shape[3])


def sums_forward(hidden):
    return (jnp.sum(hidden, axis=(0, 1, 2)), jnp.sum(hidden * hidden, axis=(0, 1, 2)))


def normed_of(hidden, sums, samples):
    average = sums[0] / samples
    inverse = lax.rsqrt(sums[1] / samples - average * average + EPS)
    return ((hidden - average) * inverse, inverse)


def sums_backward(upstream, normed):
    return (jnp.sum(upstream, axis=(0, 1, 2)), jnp.sum(upstream * normed, axis=(0, 1, 2)))


def hidden_grad(upstream, normed, inverse, gain, sums, samples):
    return (
        gain * inverse * (upstream - sums[0] / samples - normed * (sums[1] / samples))
    ).astype(jnp.bfloat16)


def each(function, *lists):
    return [function(*items) for items in zip(*lists)]


def columns(array, axis):
    own = array.shape[axis] // lax.axis_size("narrow")
    return lax.dynamic_slice_in_dim(array, lax.axis_index("narrow") * own, own, axis)


def dot(form, left, right):
    return jnp.einsum(form, left, right, preferred_element_type=jnp.float32)


def plain_body(
    input_five,
    input_seven,
    input_nine,
    upstream_five,
    upstream_seven,
    upstream_nine,
    reduce_weight,
    spatial_weight,
    expand_weight,
    gain_first,
    shift_first,
    gain_second,
    shift_second,
    gain_third,
    shift_third,
):
    inputs = [input_five, input_seven, input_nine]
    upstreams = [upstream_five, upstream_seven, upstream_nine]
    samples = [
        x.shape[0] * lax.axis_size("wide") * x.shape[1] * x.shape[2] for x in inputs
    ]
    whole_reduce = lax.all_gather(reduce_weight, "narrow", axis=1, tiled=True)
    whole_spatial = lax.all_gather(spatial_weight, "narrow", axis=3, tiled=True)
    own_expand = lax.all_to_all(expand_weight, "narrow", 1, 0, tiled=True)
    vectors = jnp.stack([gain_first, shift_first, gain_second, shift_second])
    gain1, shift1, gain2, shift2 = lax.all_gather(vectors, "narrow", axis=1, tiled=True)

    hidden1 = each(lambda x: dot("bhwc,cd->bhwd", x, whole_reduce), inputs)
    sums1 = lax.psum(each(sums_forward, hidden1), "wide")
    normed1, inverse1 = zip(*each(normed_of, hidden1, sums1, samples))
    pre1 = each(lambda n: n * gain1 + shift1, normed1)
    active1 = each(lambda p: jax.nn.silu(p).astype(jnp.bfloat16), pre1)

    hidden2 = each(lambda a: spatial(a, whole_spatial), active1)
    sums2 = lax.psum(each(sums_forward, hidden2), "wide")
    normed2, inverse2 = zip(*each(normed_of, hidden2, sums2, samples))
    pre2 = each(lambda n: n * gain2 + shift2, normed2)
    active2 = each(lambda p: jax.nn.silu(p).astype(jnp.bfloat16), pre2)

    hidden3 = each(lambda a: dot("bhwi,id->bhwd", a, own_expand), active2)
    sums3 = lax.psum(each(sums_forward, hidden3), "wide")
    normed3, inverse3 = zip(*each(normed_of, hidden3, sums3, samples))
    summed = each(
        lambda n, x: n * gain_third + shift_third + columns(x, 3).astype(jnp.float32),
        normed3,
        inputs,
    )
    results = each(lambda z: jax.nn.silu(z).astype(jnp.bfloat16), summed)
    grads_z = each(lambda u, z: u.astype(jnp.float32) * silu_slope(z), upstreams, summed)
    back3 = lax.psum(each(sums_backward, grads_z, normed3), "wide")
    grad3 = each(
        lambda e, n, r, s, m: hidden_grad(e, n, r, gain_third, s, m),
        grads_z,
        normed3,
        inverse3,
        back3,
        samples,
    )
    expand_grad = sum(each(lambda a, g: dot("bhwi,bhwd->id", a, g), active2, grad3))
    active_grad2 = each(
        lambda g: lax.psum(
            dot("bhwd,id->bhwi", g, own_expand).astype(jnp.bfloat16), "narrow"
        ).astype(jnp.float32),
        grad3,
    )
    grads_2 = each(lambda a, p: a * silu_slope(p), active_grad2, pre2)
    back2 = lax.psum(each(sums_backward, grads_2, normed2), "wide")
    grad2 = each(
        lambda e, n, r, s, m: hidden_grad(e, n, r, gain2, s, m),
        grads_2,
        normed2,
        inverse2,
        back2,
        samples,
    )
    spatial_grad = sum(each(lambda a, g: kernel_grad(a, columns(g, 3)), active1, grad2))
    flipped = jnp.transpose(whole_spatial[::-1, ::-1], (0, 1, 3, 2))
    grads_1 = each(lambda g, p: spatial(g, flipped) * silu_slope(p), grad2, pre1)
    back1 = lax.psum(each(sums_backward, grads_1, normed1), "wide")
    grad1 = each(
        lambda e, n, r, s, m: hidden_grad(e, n, r, gain1, s, m),
        grads_1,
        normed1,
        inverse1,
        back1,
        samples,
    )
    reduce_grad = sum(each(lambda x, g: dot("bhwc,bhwd->cd", x, columns(g, 3)), inputs, grad1))
    own_reduce = columns(whole_reduce, 0)
    in_grads = each(lambda g, e: dot("bhwd,cd->bhwc", g, own_reduce) + e, grad1, grads_z)

    low = [g.astype(jnp.bfloat16) for g in (reduce_grad, spatial_grad, expand_grad)]
    low[2] = lax.all_to_all(low[2], "narrow", 0, 1, tiled=True)
    totals = [g.astype(jnp.float32) for g in lax.psum(low, "wide")]

    def params(back, part):
        shift = sum(s[0] for s in back)
        gain = sum(s[1] for s in back)
        return [part(gain), part(shift)]

    def own(vector):
        return columns(vector, 0)

    small = params(back1, own) + params(back2, own) + params(back3, lambda v: v)
    return tuple(results + in_grads + totals + small)


class Shape:
    def __init__(self, mesh, maps, images, depth, inner):
        self.wide, self.narrow = mesh.shape["wide"], mesh.shape["narrow"]
        self.chips = self.wide // 2
        self.maps = maps
        self.images = images
        self.depth, self.inner = depth, inner
        self.own = inner // self.narrow
        self.block = depth // self.narrow
        self.rows = [images * side * side for side in maps]
        self.samples = [float(rows * self.wide) for rows in self.rows]

    def fits(self):
        return (
            self.narrow >= 4
            and self.narrow % 2 == 0
            and self.chips == 4
            and self.wide == 8
            and min(self.maps) >= 3
            and self.block == self.inner
            and self.own % 128 == 0
            and self.images % 16 == 0
            and self.own % (16 * self.wide) == 0
            and self.inner % 512 == 0
        )


def cuts(side, most):
    longest = max(1, most // side)
    number = -(-side // longest)
    edges = [side * n // number for n in range(number + 1)]
    return [(a, b - a) for a, b in zip(edges, edges[1:])]


class Pool:
    def __init__(self, ref):
        self.ref, self.used = ref, 0

    def take(self):
        assert self.used < SEMAPHORES
        self.used += 1
        return self.ref.at[self.used - 1]


MESH = pl.DeviceIdType.MESH
INVERSE, MINUS, SCALE, OFFSET, SHIFTSUM, GAINSUM, LINEAR, CONSTANT = range(8)
GIVEN, SPARE = 72, 80
SEMAPHORES = 600
VMEM_BYTES = 67_000_000
SLAB, CHUNK = 28, 9
WEIGHT_PARTS = 3


def dot_nn(left, right):
    return lax.dot_general(
        left, right, (((1,), (0,)), ((), ())), preferred_element_type=jnp.float32
    )


def dot_nt(left, right):
    return lax.dot_general(
        left, right, (((1,), (1,)), ((), ())), preferred_element_type=jnp.float32
    )


def dot_tn(left, right):
    return lax.dot_general(
        left, right, (((0,), (0,)), ((), ())), preferred_element_type=jnp.float32
    )


def logistic(argument):
    return 0.5 * jnp.tanh(0.5 * argument) + 0.5


class Step:
    def __init__(self, key, run, time, after, rank, hook=None):
        self.key, self.run, self.time = key, run, time
        self.after, self.rank, self.hook = after, rank, hook
        self.ready = 0.0


def arrange(steps, trace=None):
    named = {step.key: step for step in steps}
    done = {}
    now = 0.0
    order = []
    waiting = list(steps)
    while waiting:
        best = None
        for place, step in enumerate(waiting):
            if any(key not in done for key, _ in step.after):
                continue
            at = max([step.ready] + [done[key] + delay for key, delay in step.after])
            choice = (max(at, now), step.rank, place)
            if best is None or choice < best[0]:
                best = (choice, step)
        (start, _, _), step = best
        now = start + step.time
        done[step.key] = now
        waiting.remove(step)
        order.append(step)
        if trace is not None:
            trace.append((start, now, step.key))
        if step.hook is not None:
            step.hook(now, named)
    return order


def block_kernel(shape, *refs):
    wide, narrow, chips = shape.wide, shape.narrow, shape.chips
    inner, own, block, images = shape.inner, shape.own, shape.block, shape.images
    maps = shape.maps
    refs = list(refs)

    def take(count):
        taken = refs[:count]
        del refs[:count]
        return taken

    x_in, u_in = take(3), take(3)
    rw_in, sw_in, ew_in = take(3)
    vec_in = take(6)
    y_out, i_out = take(3), take(3)
    rg_out, sg_out, eg_out = take(3)
    vec_out = take(6)
    xb = take(3)
    rwf, swf, ewf = take(3)
    h1, h2, h3, dz = take(3), take(3), take(3), take(3)
    apad, dpad = take(3), take(3)
    rin, rx = take(3), take(3)
    sacc, eacc, racc = take(3)
    slow, elow, rlow = take(3)
    sr1, er1, rr1 = take(3)
    sr2, er2, rr2 = take(3)
    sfin, efin, rfin = take(3)
    epz, rpz = take(2)
    stat_s, stat_r, sums, vec, vec_all = take(5)
    vec_own, vec_made = take(6), take(6)
    pool = Pool(*take(1))

    w = lax.axis_index("wide")
    z = lax.axis_index("narrow")
    core = lax.rem(w, 2)
    chip = lax.div(w, 2)
    sibling = chip * 2 + (1 - core)
    half = narrow // 2
    inward = jnp.where(z < half, z + 1, z - 1)
    outward = jnp.where(z < half, z - 1, z + 1)
    center = jnp.logical_or(z == half - 1, z == half)
    end = jnp.logical_or(z == 0, z == narrow - 1)
    k_own, k_a2, k_dh, k_p = [lax.rem(z + k, narrow) for k in range(4)]
    finish = []
    arrivals = []

    def once(wait):
        made = []

        def noted():
            if not made:
                made.append(True)
                wait()

        arrivals.append(noted)
        return noted

    def remote(source, target, device):
        send, recv = pool.take(), pool.take()

        def make():
            return pltpu.make_async_remote_copy(
                src_ref=source(),
                dst_ref=target(),
                send_sem=send,
                recv_sem=recv,
                device_id=device,
                device_id_type=MESH,
            )

        make().start()
        finish.append(lambda: make().wait_send())
        return once(lambda: make().wait_recv())

    def local(source, target):
        semaphore = pool.take()

        def make():
            return pltpu.make_async_copy(source(), target(), semaphore)

        make().start()
        return once(lambda: make().wait())

    def span(start, size, unit):
        return pl.ds(pl.multiple_of(start * unit, unit), size)

    def rows_of(g, cut):
        return pl.ds(cut[0] * maps[g] * images, cut[1] * maps[g] * images)

    slabs = [cuts(side, SLAB) for side in maps]
    chunks = [cuts(side, CHUNK) for side in maps]

    def lines(g, cut, function):
        size = maps[g] * images
        if cut[1] == 1:
            function(cut[0], pl.ds(cut[0] * size, size))
        else:
            pl.loop(cut[0], cut[0] + cut[1])(
                lambda y: function(y, pl.ds(pl.multiple_of(y * size, 16), size))
            )

    chip_x = chip + 1 - 2 * lax.rem(chip, 2)
    chip_y = lax.rem(chip + 2, chips)
    chip_far = lax.rem(chip_x + 2, chips)
    origins = [lax.rem(z + narrow - k, narrow) for k in range(1, narrow)]

    class Gather:
        def __init__(self, source, target):
            self.source, self.target = source, target
            self.from_x, self.from_y, self.far, self.crossed = [], [], [], []

        def first(self):
            self.arrived = [
                remote(
                    lambda peer=peer: self.source(w, peer),
                    lambda: self.target(w, z),
                    (w, peer),
                )
                for peer in [lax.rem(z + k, narrow) for k in range(1, narrow)]
            ]

        def send(self, holder, origin, part, device):
            def piece():
                return self.target(holder * 2 + core, origin, part)

            return remote(piece, piece, (device, z))

        def spread(self):
            for origin, wait in zip(origins, self.arrived):
                wait()
                self.from_x.append(self.send(chip, origin, None, chip_x * 2 + core))
                self.from_y.append(self.send(chip, origin, None, chip_y * 2 + core))
            for origin in origins:
                self.crossed.append(self.send(chip, origin, None, sibling))

        def relay(self):
            for origin, got_x, got_y in zip(origins, self.from_x, self.from_y):
                got_x()
                along_y = self.send(chip_x, origin, 0, chip_y * 2 + core)
                got_y()
                along_x = self.send(chip_y, origin, 1, chip_x * 2 + core)
                self.far.append((along_y, along_x))
            for origin in origins:
                self.crossed.append(self.send(chip_x, origin, None, sibling))
                self.crossed.append(self.send(chip_y, origin, None, sibling))

        def cross(self):
            for origin, waits in zip(origins, self.far):
                for wait in waits:
                    wait()
                self.crossed.append(self.send(chip_far, origin, None, sibling))

        def ready(self):
            for wait in self.crossed:
                wait()

    rw_piece, sw_piece, ew_piece = shape.depth // wide, inner // wide, own // wide
    part = 9 // WEIGHT_PARTS

    def half_of(h, size, unit, half):
        if half is None:
            return span(h, size, size)
        return pl.ds(pl.multiple_of(h * size + half * (size // 2), unit), size // 2)

    def sw_item(n):
        taps = pl.ds(n * part, part)
        return Gather(
            lambda h, peer: sw_in.at[taps, span(h, sw_piece, sw_piece), :],
            lambda h, o, half=None: swf.at[taps, half_of(h, sw_piece, 16, half), span(o, own, own)],
        )

    gathers = (
        [
            Gather(
                lambda h, peer: rw_in.at[span(h, rw_piece, rw_piece), :],
                lambda h, o, half=None: rwf.at[half_of(h, rw_piece, 16, half), span(o, own, own)],
            )
        ]
        + [sw_item(n) for n in range(WEIGHT_PARTS)]
        + [
            Gather(
                lambda h, peer: ew_in.at[span(h, ew_piece, ew_piece), span(peer, block, block)],
                lambda h, o, half=None: ewf.at[
                    pl.ds(pl.multiple_of(o * own + h * ew_piece, 16), ew_piece),
                    pl.ds(0, block) if half is None else pl.ds(half * (block // 2), block // 2),
                ],
            )
        ]
    )
    x_wait = [[None] * narrow for _ in range(3)]
    u_wait, y_wait = [None] * 3, [None] * 3
    own_waits, vec_waits = [], []

    def slot(kind, level, g):
        return (kind * 3 + level) * 3 + g

    def put(place, value):
        vec[place : place + 1, :] = value

    def get(place):
        return vec[place : place + 1, :]

    def begin():
        got = [local(lambda a=a: a, lambda b=b: b) for a, b in zip(vec_in, vec_own)]
        barrier = pltpu.get_barrier_semaphore()
        for k in range(1, wide):
            pl.semaphore_signal(
                barrier, inc=1, device_id=(lax.rem(w + k, wide), z), device_id_type=MESH
            )
        for k in range(1, narrow):
            pl.semaphore_signal(
                barrier, inc=1, device_id=(w, lax.rem(z + k, narrow)), device_id_type=MESH
            )
        for source, target in (
            (lambda: rw_in, lambda: rwf.at[:, span(z, own, own)]),
            (lambda: sw_in, lambda: swf.at[:, :, span(z, own, own)]),
            (lambda: ew_in.at[:, span(z, block, block)], lambda: ewf.at[span(z, own, own), :]),
        ):
            own_waits.append(local(source, target))
        for g in range(3):
            for k in range(narrow):
                x_wait[g][k] = local(
                    lambda g=g, k=k: x_in[g].at[:, pl.ds(k * block, block)],
                    lambda g=g, k=k: xb[g].at[k],
                )
        for wait in got:
            wait()
        vec_all[z] = jnp.concatenate(
            [v[...] for v in vec_own[:4]] + [jnp.zeros((4, own), jnp.float32)], axis=0
        )
        pl.semaphore_wait(barrier, wide - 1 + narrow - 1)
        for k in range(1, narrow):
            vec_waits.append(
                remote(lambda: vec_all.at[z], lambda: vec_all.at[z], (w, lax.rem(z + k, narrow)))
            )
        for item in gathers:
            item.first()

    def pads():
        for g in range(3):
            side = maps[g]
            for pad in (apad[g], dpad[g]):
                pad[0] = jnp.zeros((side + 2, images, inner), jnp.bfloat16)
                pad[side + 1] = jnp.zeros((side + 2, images, inner), jnp.bfloat16)
                for edge in (0, side + 1):
                    pad[1 : side + 1, edge] = jnp.zeros((side, images, inner), jnp.bfloat16)
        for acc in (sacc, eacc, racc):

            def clear(a, acc=acc):
                acc[a] = jnp.zeros(acc.shape[1:], jnp.float32)

            pl.loop(0, acc.shape[0])(clear)

    def vectors():
        for wait in vec_waits:
            wait()
        for row in range(4):
            put(
                GIVEN + row,
                jnp.concatenate([vec_all[k, row : row + 1, :] for k in range(narrow)], axis=1),
            )
        for row in (4, 5):
            put(GIVEN + row, vec_own[row][...])

    tiles = inner // 128
    stat_sems, stat_arrived = {}, {}

    def stats_all(e):
        send, recv = stat_sems[e]
        return pltpu.make_async_remote_copy(
            src_ref=stat_r.at[e, pl.ds(0, wide - 1)],
            dst_ref=stat_r.at[e, pl.ds(0, wide - 1)],
            send_sem=send,
            recv_sem=recv,
            device_id=(sibling, z),
            device_id_type=MESH,
        )

    def stats_wait(e):
        stat_arrived[e]()
        total = stat_r[e, 0]
        for k in range(1, wide):
            total = total + stat_r[e, k]
        return [
            jnp.concatenate(
                [total[t * tiles + b : t * tiles + b + 1, :] for b in range(tiles)], axis=1
            )
            for t in range(2)
        ]

    class Sums:
        def __init__(self, e):
            self.row = 2 * e
            self.e = e

        def clear(self):
            sums[self.row : self.row + 2, :] = jnp.zeros((2, inner), jnp.float32)

        def add(self, first, second):
            sums[self.row : self.row + 1, :] += jnp.sum(first, axis=0, keepdims=True)
            sums[self.row + 1 : self.row + 2, :] += jnp.sum(second, axis=0, keepdims=True)

    totals_of = {e: Sums(e) for e in range(18)}

    def send_sums(e):
        row = totals_of[e].row
        for t in range(2):
            for b in range(tiles):
                stat_s[e, t * tiles + b : t * tiles + b + 1, :] = sums[
                    row + t : row + t + 1, b * 128 : (b + 1) * 128
                ]
        stat_r[e, w] = stat_s[e]
        send, recv = pool.take(), pool.take()
        stat_sems[e] = (send, recv)
        stat_arrived[e] = once(lambda: stats_all(e).wait_recv())
        finish.append(lambda: stats_all(e).wait_send())

        def one(k, carry):
            pltpu.make_async_remote_copy(
                src_ref=stat_s.at[e],
                dst_ref=stat_r.at[e, w],
                send_sem=send,
                recv_sem=recv,
                device_id=(lax.rem(w + k, wide), z),
                device_id_type=MESH,
            ).start()
            return carry

        lax.fori_loop(1, wide, one, 0)

    def norm_vectors(g, level):
        first, second = stats_wait(g * 6 + level)
        mean = first / shape.samples[g]
        inverse = lax.rsqrt(second / shape.samples[g] - mean * mean + EPS)
        scale = inverse * get(GIVEN + 2 * level)
        put(slot(INVERSE, level, g), inverse)
        put(slot(MINUS, level, g), -mean * inverse)
        put(slot(SCALE, level, g), scale)
        put(slot(OFFSET, level, g), get(GIVEN + 2 * level + 1) - mean * scale)

    def back_vectors(g, level):
        shift_sum, gain_sum = stats_wait(g * 6 + 5 - level)
        put(slot(SHIFTSUM, level, g), shift_sum)
        put(slot(GAINSUM, level, g), gain_sum)
        scale = get(slot(SCALE, level, g))
        c1 = scale * (gain_sum / shape.samples[g])
        put(slot(LINEAR, level, g), -get(slot(INVERSE, level, g)) * c1)
        put(slot(CONSTANT, level, g), -get(slot(MINUS, level, g)) * c1 - scale * (shift_sum / shape.samples[g]))

    def f1(g, cut):
        run = totals_of[g * 6]
        if cut[0] == 0:
            for wait in x_wait[g]:
                wait()
            run.clear()
        rows = rows_of(g, cut)
        left = jnp.concatenate([xb[g][k, rows, :] for k in range(narrow)], axis=1)
        result = dot_nn(left, rwf[...])
        h1[g][rows, :] = result
        run.add(result, result * result)

    def f1_end(g):
        send_sums(g * 6)
        u_wait[g] = local(lambda: u_in[g], lambda: xb[g].at[k_dh])

    def a1(g):
        scale, offset = get(slot(SCALE, 0, g)), get(slot(OFFSET, 0, g))
        side = maps[g]

        def one(y, rows):
            pre = h1[g][rows, :] * scale + offset
            value = (pre * logistic(pre)).astype(jnp.bfloat16)
            apad[g][y + 1, pl.ds(1, side)] = value.reshape(side, images, inner)

        lines(g, (0, side), one)

    def windows(pad, g, cut, lines_of_taps):
        side = maps[g]
        return jnp.concatenate(
            [
                pad[cut[0] + i : cut[0] + i + cut[1], j : j + side].reshape(
                    cut[1] * side * images, inner
                )
                for i in lines_of_taps
                for j in range(3)
            ],
            axis=1,
        )

    def f2(g, n, cut):
        run = totals_of[g * 6 + 1]
        rows = rows_of(g, cut)
        result = dot_nn(windows(apad[g], g, cut, (n,)), swf[3 * n : 3 * n + 3].reshape(-1, inner))
        if n > 0:
            result = result + h2[g][rows, :]
        h2[g][rows, :] = result
        if n == 2:
            if cut[0] == 0:
                run.clear()
            run.add(result, result * result)

    def a2(g):
        scale, offset = get(slot(SCALE, 1, g)), get(slot(OFFSET, 1, g))

        def one(y, rows):
            pre = h2[g][rows, :] * scale + offset
            xb[g][k_a2, rows, :] = (pre * logistic(pre)).astype(jnp.bfloat16)

        lines(g, (0, maps[g]), one)

    def f3(g):
        run = totals_of[g * 6 + 2]
        run.clear()
        for cut in slabs[g]:
            rows = rows_of(g, cut)
            result = dot_nn(xb[g][k_a2, rows, :], ewf[...])
            h3[g][rows, :] = result
            run.add(result, result * result)

    def a3(g):
        run = totals_of[g * 6 + 3]
        run.clear()
        scale, offset = get(slot(SCALE, 2, g)), get(slot(OFFSET, 2, g))
        inverse, minus = get(slot(INVERSE, 2, g)), get(slot(MINUS, 2, g))

        def one(y, rows):
            hidden = h3[g][rows, :]
            total = hidden * scale + offset + xb[g][k_own, rows, :].astype(jnp.float32)
            sig = logistic(total)
            xb[g][k_p, rows, :] = (total * sig).astype(jnp.bfloat16)
            slope = sig * (1.0 + total * (1.0 - sig))
            grad = xb[g][k_dh, rows, :].astype(jnp.float32) * slope
            dz[g][rows, :] = grad
            run.add(grad, grad * (hidden * inverse + minus))

        lines(g, (0, maps[g]), one)

    def a3_end(g):
        send_sums(g * 6 + 3)
        y_wait[g] = local(lambda: xb[g].at[k_p], lambda: y_out[g])

    def b3(g, cut):
        scale, k1, k0 = get(slot(SCALE, 2, g)), get(slot(LINEAR, 2, g)), get(slot(CONSTANT, 2, g))
        rows = rows_of(g, cut)
        value = dz[g][rows, :] * scale + h3[g][rows, :] * k1 + k0
        low = value.astype(jnp.bfloat16)
        xb[g][k_dh, rows, :] = low
        xb[g][k_p, rows, :] = dot_nt(low, ewf[...]).astype(jnp.bfloat16)
        c = chunks[g].index(cut)
        reductions[g, c] = copies = Reduction(g, c)
        pl.when(end)(lambda: copies.to_inner().start())

    def eg(g):
        result = dot_tn(xb[g][k_a2], xb[g][k_dh])
        for k in range(narrow):
            piece = result[k * own : (k + 1) * own, :].reshape(eacc.shape[1:])
            eacc[k] += piece

    reductions = {}

    class Reduction:
        def __init__(self, g, c):
            self.g, self.rows = g, rows_of(g, chunks[g][c])
            self.sems = [pool.take() for _ in range(5)]
            self.inwards = once(self.add_outer)
            self.across = once(self.add_other)
            self.home = once(lambda: pl.when(end)(lambda: self.to_center().wait_recv()))
            finish.append(self.sent)

        def copy(self, source, target, send, recv, device):
            return pltpu.make_async_remote_copy(
                src_ref=source.at[self.rows, :],
                dst_ref=target.at[self.rows, :],
                send_sem=self.sems[send],
                recv_sem=self.sems[recv],
                device_id=(w, device),
                device_id_type=MESH,
            )

        def to_inner(self):
            return self.copy(xb[self.g].at[k_p], rin[self.g], 0, 1, inward)

        def to_center(self):
            return self.copy(xb[self.g].at[k_p], rx[self.g], 2, 3, inward)

        def to_outer(self):
            return self.copy(rx[self.g], rx[self.g], 4, 3, outward)

        def add_outer(self):
            g, rows = self.g, self.rows

            @pl.when(jnp.logical_not(end))
            def _():
                self.to_inner().wait_recv()
                xb[g][k_p, rows, :] = (
                    xb[g][k_p, rows, :].astype(jnp.float32) + rin[g][rows, :].astype(jnp.float32)
                ).astype(jnp.bfloat16)
                pl.when(center)(lambda: self.to_center().start())
                pl.when(jnp.logical_not(center))(lambda: self.to_inner().start())

        def add_other(self):
            g, rows = self.g, self.rows

            @pl.when(jnp.logical_not(end))
            def _():
                self.to_center().wait_recv()

                @pl.when(center)
                def _():
                    rx[g][rows, :] = (
                        rx[g][rows, :].astype(jnp.float32)
                        + xb[g][k_p, rows, :].astype(jnp.float32)
                    ).astype(jnp.bfloat16)

                self.to_outer().start()

        def sent(self):
            pl.when(center)(lambda: self.to_center().wait_send())
            pl.when(jnp.logical_not(center))(lambda: self.to_inner().wait_send())
            pl.when(jnp.logical_not(end))(lambda: self.to_outer().wait_send())

    def za(g, c):
        reductions[g, c].inwards()

    def zb(g, c):
        reductions[g, c].across()

    def g2(g, c):
        run = totals_of[g * 6 + 4]
        if c == 0:
            run.clear()
        reductions[g, c].home()
        scale, offset = get(slot(SCALE, 1, g)), get(slot(OFFSET, 1, g))
        inverse, minus = get(slot(INVERSE, 1, g)), get(slot(MINUS, 1, g))

        def one(y, rows):
            hidden = h2[g][rows, :]
            pre = hidden * scale + offset
            sig = logistic(pre)
            grad = rx[g][rows, :].astype(jnp.float32) * (sig * (1.0 + pre * (1.0 - sig)))
            h3[g][rows, :] = grad
            run.add(grad, grad * (hidden * inverse + minus))

        lines(g, chunks[g][c], one)

    def d2(g):
        scale, k1, k0 = get(slot(SCALE, 1, g)), get(slot(LINEAR, 1, g)), get(slot(CONSTANT, 1, g))
        side = maps[g]

        def one(y, rows):
            value = h3[g][rows, :] * scale + h2[g][rows, :] * k1 + k0
            dpad[g][y + 1, pl.ds(1, side)] = value.astype(jnp.bfloat16).reshape(side, images, inner)

        lines(g, (0, side), one)

    def sg(g):
        side = maps[g]
        left = apad[g][1 : side + 1, 1 : side + 1].reshape(shape.rows[g], inner)
        right = jnp.concatenate(
            [
                dpad[g][2 - i : 2 - i + side, 2 - j : 2 - j + side, :, span(z, own, own)].reshape(
                    shape.rows[g], own
                )
                for i in range(3)
                for j in range(3)
            ],
            axis=1,
        )
        result = dot_tn(left, right)
        for t in range(9):
            piece = result[:, t * own : (t + 1) * own].reshape(sacc.shape[1:])
            sacc[t] += piece

    def f1b(g, cut):
        run = totals_of[g * 6 + 5]
        if cut[0] == 0:
            run.clear()
        rows = rows_of(g, cut)
        left = windows(dpad[g], g, cut, range(3))
        right = jnp.concatenate([swf[8 - t] for t in range(9)], axis=1)
        h2[g][rows, :] = dot_nt(left, right)

    def g1(g, cut):
        run = totals_of[g * 6 + 5]
        scale, offset = get(slot(SCALE, 0, g)), get(slot(OFFSET, 0, g))
        inverse, minus = get(slot(INVERSE, 0, g)), get(slot(MINUS, 0, g))

        def one(y, rows):
            hidden = h1[g][rows, :]
            pre = hidden * scale + offset
            sig = logistic(pre)
            grad = h2[g][rows, :] * (sig * (1.0 + pre * (1.0 - sig)))
            h2[g][rows, :] = grad
            run.add(grad, grad * (hidden * inverse + minus))

        lines(g, cut, one)

    def d1(g):
        scale, k1, k0 = get(slot(SCALE, 0, g)), get(slot(LINEAR, 0, g)), get(slot(CONSTANT, 0, g))

        def one(y, rows):
            value = h2[g][rows, :] * scale + h1[g][rows, :] * k1 + k0
            xb[g][k_dh, rows, :] = value.astype(jnp.bfloat16)

        lines(g, (0, maps[g]), one)

    def ig(g):
        for cut in slabs[g]:
            rows = rows_of(g, cut)
            right = rwf[span(z, block, block), :]
            h3[g][rows, :] = dot_nt(xb[g][k_dh, rows, :], right) + dz[g][rows, :]
        finish.append(local(lambda: h3[g], lambda: i_out[g]))

    def rg(g):
        result = dot_tn(xb[g][k_own], xb[g][k_dh])
        for k in range(narrow):
            piece = result[:, k * own : (k + 1) * own].reshape(racc.shape[1:])
            racc[k] += piece

    class Total:
        def __init__(self, acc, low, first, second, final, piece, out):
            self.acc, self.low, self.first, self.second = acc, low, first, second
            self.final, self.piece, self.out = final, piece, out
            self.count = acc.shape[0]

        def one(self):
            def cast(a):
                self.low[a] = self.acc[a, :, 1 - core].astype(jnp.bfloat16)

            pl.loop(0, self.count)(cast)
            self.got1 = remote(lambda: self.low, lambda: self.first, (sibling, z))

        def two(self):
            self.got1()

            def add(a):
                self.first[a] = (
                    self.first[a].astype(jnp.float32) + self.acc[a, :, core]
                ).astype(jnp.bfloat16)

            pl.loop(0, self.count)(add)
            self.got2 = []
            for j in range(1, chips):
                peer = lax.rem(chip + j, chips)
                self.got2.append(
                    remote(
                        lambda peer=peer: self.first.at[:, peer],
                        lambda: self.second.at[chip],
                        (peer * 2 + core, z),
                    )
                )

        def three(self):
            for wait in self.got2:
                wait()
            self.second[chip] = self.first[:, chip]
            target = self.final.at[:, chip, core] if self.piece is None else self.piece

            def add(a):
                total = self.second[0, a].astype(jnp.float32)
                for k in range(1, chips):
                    total = total + self.second[k, a].astype(jnp.float32)
                target[a] = total.astype(jnp.bfloat16)

            pl.loop(0, self.count)(add)
            if self.piece is None:
                self.send_pieces()
                return
            self.got3 = []
            for k in range(1, narrow):
                peer = lax.rem(z + k, narrow)
                self.got3.append(
                    remote(
                        lambda peer=peer: self.piece.at[peer],
                        lambda: self.final.at[z, chip, core],
                        (w, peer),
                    )
                )
            self.final[z, chip, core] = self.piece[z]

        def exchange(self):
            for wait in self.got3:
                wait()
            self.send_pieces()

        def send_pieces(self):
            self.got4, self.got5 = [], []

            def piece():
                return self.final.at[:, chip, core]

            for j in range(1, chips):
                peer = lax.rem(chip + j, chips)
                self.got4.append((j, remote(piece, piece, (peer * 2 + core, z))))
            self.got5.append(remote(piece, piece, (sibling, z)))

        def four(self):
            for j, arrived in self.got4:
                arrived()
                holder = lax.rem(chip + chips - j, chips)

                def piece(holder=holder):
                    return self.final.at[:, holder, core]

                self.got5.append(remote(piece, piece, (sibling, z)))

        def five(self):
            for wait in self.got5:
                wait()
            finish.append(local(lambda: self.final, lambda: self.out))

    stotal = Total(sacc, slow, sr1, sr2, sfin, None, sg_out)
    etotal = Total(eacc, elow, er1, er2, efin, epz, eg_out)
    rtotal = Total(racc, rlow, rr1, rr2, rfin, rpz, rg_out)

    def params():
        for place in range(6):
            level, kind = place // 2, GAINSUM if place % 2 == 0 else SHIFTSUM
            total = sum(get(slot(kind, level, g)) for g in range(3))
            if level == 2:
                vec_made[place][...] = total
            else:
                put(SPARE, total)
                vec_made[place][...] = vec[SPARE : SPARE + 1, span(z, own, own)]
            finish.append(
                local(lambda place=place: vec_made[place], lambda place=place: vec_out[place])
            )

    steps = []
    order = T.order

    def add(key, run, time, after, rank, hook=None):
        steps.append(Step(key, run, time, after, rank, hook))

    START, CLEAR, VECTORS = (begin,), (pads,), (vectors,)
    add(START, begin, 5.0, [], 0)
    add(CLEAR, pads, 1.0, [(START, 0.0)], 1)
    add(VECTORS, vectors, 0.2, [(START, 5.0)], 2)

    def spread(n):
        gathers[n].spread()

    def relay(n):
        gathers[n].relay()

    def cross(n):
        gathers[n].cross()

    def ready(n):
        if n == 0:
            for wait in own_waits:
                wait()
        gathers[n].ready()

    for n in range(len(gathers)):
        wait = T.xy[n]
        for f, time, after in (
            (spread, 0.2, [(START, T.z[n])]),
            (relay, 0.2, [((spread, n), wait)]),
            (cross, 0.1, [((relay, n), wait * 0.7)]),
            (ready, 0.1, [((cross, n), 1.5)]),
        ):
            if n > 0 and f is not ready:
                after = after + [((f, n - 1), T.xy[n] * 0.8 if f is relay else 0.0)]
            add((f, n), functools.partial(f, n), time, after, 0.0 if n < 4 else 0.1)

    link = {za: 0.0, zb: 0.0, g2: 0.0}

    def transfer(key, size):
        def hook(now, named):
            link[key[0]] = max(link[key[0]], now) + size * T.hop
            named[key].ready = link[key[0]] + T.lat

        return hook

    class Do:
        def __init__(self, g):
            self.g = g

        def f1(self, s):
            f1(self.g, slabs[self.g][s])
            if s == len(slabs[self.g]) - 1:
                f1_end(self.g)

        def a1(self):
            norm_vectors(self.g, 0)
            a1(self.g)

        def f2(self, n, s):
            f2(self.g, n, slabs[self.g][s])
            if n == 2 and s == len(slabs[self.g]) - 1:
                send_sums(self.g * 6 + 1)

        def a2(self):
            norm_vectors(self.g, 1)
            a2(self.g)
            f3(self.g)
            send_sums(self.g * 6 + 2)

        def a3(self):
            norm_vectors(self.g, 2)
            u_wait[self.g]()
            a3(self.g)
            a3_end(self.g)

        def b3(self, c):
            if c == 0:
                back_vectors(self.g, 2)
                y_wait[self.g]()
            b3(self.g, chunks[self.g][c])

        def g2(self, c):
            g2(self.g, c)
            if c == len(chunks[self.g]) - 1:
                send_sums(self.g * 6 + 4)

        def d2(self):
            back_vectors(self.g, 1)
            d2(self.g)

        def f1b(self, s):
            f1b(self.g, slabs[self.g][s])
            g1(self.g, slabs[self.g][s])
            if s == len(slabs[self.g]) - 1:
                send_sums(self.g * 6 + 5)

        def d1(self):
            back_vectors(self.g, 0)
            d1(self.g)

    before = None
    for turn, g in enumerate(order):
        do = Do(g)
        size = [shape.rows[g] * n / maps[g] for _, n in chunks[g]]
        scale = shape.rows[g] / 1000.0
        per, last = len(slabs[g]), len(chunks[g]) - 1
        early, late = 2 + turn * 0.3, 4 + turn * 0.3
        for s in range(per):
            after = [((ready, 0), 0.0)] if s == 0 else [((f1, g, s - 1), 0.0)]
            add((f1, g, s), functools.partial(do.f1, s), T.f1 * scale / per, after, early)
        after = [((f1, g, per - 1), T.stat0), (VECTORS, 0.0), (CLEAR, 0.0)]
        add((a1, g), do.a1, T.a1 * scale + 0.2, after, early)
        behind = (a1, g)
        for n in range(3):
            for s in range(per):
                after = [(behind, 0.0), ((ready, n + 1), 0.0)]
                behind = (f2, g, n, s)
                add(behind, functools.partial(do.f2, n, s), T.f2 * scale / per / 3, after, early - 0.1 * n)
        after = [(behind, T.stat), ((ready, 4), 0.0)]
        add((a2, g), do.a2, T.a2 * scale + 0.2, after, early - 0.5)
        add((a3, g), do.a3, T.a3 * scale + 0.2, [((a2, g), T.stat)], early - 0.5)
        for c in range(last + 1):
            after = [((a3, g), T.stat)] if c == 0 else [((b3, g, c - 1), 0.0)]
            if c == 0 and before is not None:
                after.append((before, 0.0))
            add((b3, g, c), functools.partial(do.b3, c), T.b3 * size[c] / 1000.0, after, 1 + turn * 0.3, transfer((za, g, c), size[c]))
            after = [((b3, g, c), 0.0)] + ([((za, g, c - 1), 0.0)] if c else [])
            add((za, g, c), functools.partial(za, g, c), T.za, after, 0, transfer((zb, g, c), size[c]))
            after = [((za, g, c), 0.0)] + ([((zb, g, c - 1), 0.0)] if c else [])
            add((zb, g, c), functools.partial(zb, g, c), T.za, after, 0, transfer((g2, g, c), size[c]))
            after = [((zb, g, c), 0.0)] + ([((g2, g, c - 1), 0.0)] if c else [])
            add((g2, g, c), functools.partial(do.g2, c), T.g2 * size[c] / 1000.0, after, late - 1.5)
        before = (b3, g, last)
        add((d2, g), do.d2, T.d2 * scale + 0.2, [((g2, g, last), T.stat)], late - 1)
        add((eg, g), functools.partial(eg, g), T.eg * scale, [(before, 0.0)], 6)
        final = turn == len(order) - 1
        add((sg, g), functools.partial(sg, g), T.sg * scale, [((d2, g), 0.0)], 3.0 if final else late - T.sg_rank if turn else 5)
        for s in range(per):
            after = [((d2, g), 0.0)] if s == 0 else [((f1b, g, s - 1), 0.0)]
            if turn == len(order) - 2 and s == per - 1:
                after.append(((g2, order[-1], len(chunks[order[-1]]) - 1), 0.0))
            add((f1b, g, s), functools.partial(do.f1b, s), T.f1b * scale / per, after, late - 0.4)
        after = [((f1b, g, per - 1), T.stat_late), ((eg, g), 0.0)]
        add((d1, g), do.d1, T.d1 * scale + 0.2, after, late - 0.5)
        add((rg, g), functools.partial(rg, g), T.rg * scale, [((d1, g), 0.0)], late - 0.5)
        add((ig, g), functools.partial(ig, g), T.ig * scale, [((d1, g), 0.0)], 8)
    for total, source, xfer in ((etotal, eg, 3.0), (stotal, sg, 6.5), (rtotal, rg, 3.5)):
        add((total, 1), total.one, 0.3, [((source, g), 0.0) for g in range(3)], 1)
        add((total, 2), total.two, 0.3, [((total, 1), 2.5)], 1)
        after = [((total, 2), xfer + 2)]
        if total is etotal:
            after.append(((zb, order[-1], len(chunks[order[-1]]) - 1), 0.0))
        add((total, 3), total.three, 0.4, after, 1)
        if total.piece is not None:
            add((total, 4), total.exchange, 0.2, [((total, 3), 5.0 if total is etotal else 2.5)], 1)
        after = [((total, 3 if total.piece is None else 4), xfer + 2)]
        add((total, 5), total.four, 0.2, after, 1)
        add((total, 6), total.five, 0.1, [((total, 5), 2.5)], 7)
    add((params,), params, 0.3, [((d1, g), 0.0) for g in range(3)], 7)
    for step in arrange(steps, TRACE)[:PLAN_END]:
        step.run()
    for wait in arrivals:
        wait()
    for wait in finish:
        wait()


PLAN_END = None
TRACE = None


class T:
    order = (2, 1, 0)
    z = (8.0, 14.5, 18.5, 23.0, 24.0)
    xy = (5.0, 5.0, 5.0, 5.0, 2.0)
    stat0, stat, stat_late = 4.5, 2.8, 5.0
    f1, a1, f2, a2, a3, b3 = 2.5, 0.7, 5.4, 1.3, 2.0, 2.1
    hop, lat, za = 0.022, 1.5, 0.1
    g2, d2, eg, sg, f1b, d1, rg, ig = 1.4, 0.4, 0.7, 2.0, 6.3, 0.4, 0.7, 0.7
    sg_rank = 0.45


def kernel_call(shape, args):
    inner, own, block, depth = shape.inner, shape.own, shape.block, shape.depth
    wide, narrow, chips, images = shape.wide, shape.narrow, shape.chips, shape.images
    bf16, f32 = jnp.bfloat16, jnp.float32

    def struct(dims, kind):
        return jax.ShapeDtypeStruct(dims, kind)

    spread = [
        (9, chips, 2, inner // wide, own),
        (narrow, chips, 2, own // wide, block),
        (narrow, chips, 2, block // wide, own),
    ]
    outs = (
        [struct((rows, block), bf16) for rows in shape.rows]
        + [struct((rows, block), f32) for rows in shape.rows]
        + [struct(spread[2], bf16), struct(spread[0], bf16), struct(spread[1], bf16)]
        + [struct((1, own), f32)] * 4
        + [struct((1, block), f32)] * 2
    )
    anywhere = pl.BlockSpec(memory_space=pl.ANY)

    def each_rows(columns, kind):
        return [pltpu.VMEM((rows, columns), kind) for rows in shape.rows]

    def padded():
        return [pltpu.VMEM((side + 2, side + 2, images, inner), bf16) for side in shape.maps]

    scratch = (
        [pltpu.VMEM((narrow, rows, block), bf16) for rows in shape.rows]
        + [
            pltpu.VMEM((depth, inner), bf16),
            pltpu.VMEM((9, inner, inner), bf16),
            pltpu.VMEM((inner, block), bf16),
        ]
        + each_rows(inner, f32)
        + each_rows(inner, f32)
        + each_rows(block, f32)
        + each_rows(block, f32)
        + padded()
        + padded()
        + each_rows(inner, bf16)
        + each_rows(inner, bf16)
        + [pltpu.VMEM(dims, f32) for dims in spread]
        + [pltpu.VMEM((a, c, b, lanes), bf16) for a, c, _, b, lanes in spread]
        + [pltpu.VMEM((a, c, b, lanes), bf16) for a, c, _, b, lanes in spread]
        + [pltpu.VMEM((c, a, b, lanes), bf16) for a, c, _, b, lanes in spread]
        + [pltpu.VMEM(dims, bf16) for dims in spread]
        + [pltpu.VMEM((a, b, lanes), bf16) for a, _, _, b, lanes in spread[1:]]
        + [
            pltpu.VMEM((18, 2 * inner // 128, 128), f32),
            pltpu.VMEM((18, wide, 2 * inner // 128, 128), f32),
            pltpu.VMEM((40, inner), f32),
            pltpu.VMEM((96, inner), f32),
            pltpu.VMEM((narrow, 8, own), f32),
        ]
        + ([pltpu.VMEM((1, own), f32)] * 4 + [pltpu.VMEM((1, block), f32)] * 2) * 2
        + [pltpu.SemaphoreType.DMA((SEMAPHORES,))]
    )
    return pl.pallas_call(
        functools.partial(block_kernel, shape),
        out_shape=outs,
        in_specs=[anywhere] * 15,
        out_specs=[anywhere] * 15,
        scratch_shapes=scratch,
        compiler_params=pltpu.CompilerParams(
            collective_id=0, has_side_effects=True, vmem_limit_bytes=VMEM_BYTES
        ),
        name="bottleneck",
    )(*args)


def last_kernel(shape, *refs):
    narrow, block = shape.narrow, shape.block
    source, target, held, high, sems = refs[:15], refs[15:30], refs[30:45], refs[45:48], refs[48]
    pool = Pool(sems)
    finish = []

    def copy(source, target):
        semaphore = pool.take()

        def make():
            return pltpu.make_async_copy(source, target, semaphore)

        make().start()
        return lambda: make().wait()

    places = [6, 7, 8, 3, 4, 5, 0, 1, 2] + list(range(9, 15))
    got = {place: copy(source[place], held[place]) for place in places}
    for place in places:
        got[place]()
        if place not in (6, 7, 8):
            finish.append(copy(held[place], target[place]))
            continue
        wide = high[place - 6]

        def widen(a, place=place, wide=wide):
            wide[a] = held[place][a].astype(jnp.float32)

        pl.loop(0, wide.shape[0])(widen)
        if place < 8:
            finish.append(copy(wide, target[place]))
            continue
        for k in range(narrow):
            finish.append(
                copy(wide.at[k], target[place].at[:, :, :, pl.ds(k * block, block)])
            )
    for wait in finish:
        wait()


def last_call(shape, args):
    f32 = jnp.float32
    outs = [jax.ShapeDtypeStruct(a.shape, f32 if 6 <= n < 9 else a.dtype) for n, a in enumerate(args)]
    outs[8] = jax.ShapeDtypeStruct((*args[8].shape[1:-1], shape.depth), f32)
    anywhere = pl.BlockSpec(memory_space=pl.ANY)
    return pl.pallas_call(
        functools.partial(last_kernel, shape),
        out_shape=outs,
        in_specs=[anywhere] * 15,
        out_specs=[anywhere] * 15,
        scratch_shapes=[pltpu.VMEM(a.shape, a.dtype) for a in args]
        + [pltpu.VMEM(a.shape, f32) for a in args[6:9]]
        + [pltpu.SemaphoreType.DMA((64,))],
        compiler_params=pltpu.CompilerParams(vmem_limit_bytes=VMEM_BYTES),
        name="results",
    )(*args)


def kernel_body(shape, *arguments):
    inputs, upstreams = arguments[:3], arguments[3:6]
    reduce_weight, spatial_weight, expand_weight = arguments[6:9]
    vectors = arguments[9:]

    def flat(array):
        return jnp.transpose(array, (1, 2, 0, 3)).reshape(-1, array.shape[3])

    def unflat(array, side):
        return jnp.transpose(
            array.reshape(side, side, shape.images, array.shape[1]), (2, 0, 1, 3)
        )

    results = kernel_call(
        shape,
        [flat(x) for x in inputs]
        + [flat(u) for u in upstreams]
        + [
            reduce_weight,
            spatial_weight.reshape(9, shape.inner, shape.own),
            expand_weight,
        ]
        + [v.reshape(1, -1) for v in vectors],
    )
    results = last_call(shape, results)
    maps = list(shape.maps)
    images = [unflat(r, side) for r, side in zip(results[:6], maps + maps)]
    weights = [
        results[6].reshape(reduce_weight.shape),
        results[7].reshape(spatial_weight.shape),
        results[8].reshape(expand_weight.shape),
    ]
    return tuple(images + weights + [r.reshape(-1) for r in results[9:]])


def body(mesh, *arguments):
    inputs, reduce_weight = arguments[0], arguments[6]
    shape = Shape(
        mesh,
        [x.shape[1] for x in arguments[:3]],
        inputs.shape[0],
        inputs.shape[3],
        arguments[8].shape[0] * mesh.shape["narrow"],
    )
    if shape.fits():
        return kernel_body(shape, *arguments)
    return plain_body(*arguments)


def solution(mesh):
    rows = P("wide", None, None, None)
    blocks = P("wide", None, None, "narrow")
    weights = [P(None, "narrow"), P(None, None, None, "narrow"), P("narrow", None)]
    vectors = [P("narrow")] * 6
    return jax.shard_map(
        functools.partial(body, mesh),
        mesh=mesh,
        in_specs=tuple([rows] * 3 + [blocks] * 3 + weights + vectors),
        out_specs=tuple([blocks] * 6 + weights + vectors),
        check_vma=False,
    )
```

```python
import functools

import jax
import jax.numpy as jnp
from jax import lax
from jax.experimental import pallas as pl
from jax.experimental.pallas import tpu as pltpu
from jax.sharding import PartitionSpec as P

EPS = 1e-05
LAYOUT = ("NHWC", "HWIO", "NHWC")


def silu_slope(argument):
    logistic = jax.nn.sigmoid(argument)
    return logistic * (1.0 + argument * (1.0 - logistic))


def spatial(inputs, kernel):
    return lax.conv_general_dilated(
        inputs,
        kernel,
        (1, 1),
        ((1, 1), (1, 1)),
        dimension_numbers=LAYOUT,
        preferred_element_type=jnp.float32,
    )


def kernel_grad(inputs, gradient):
    height, breadth = (gradient.shape[1], gradient.shape[2])
    padded = jnp.pad(inputs, ((0, 0), (1, 1), (1, 1), (0, 0)))
    taps = []
    for vertical in range(3):
        for lateral in range(3):
            window = padded[:, vertical : vertical + height, lateral : lateral + breadth, :]
            taps.append(
                jnp.einsum("bhwc,bhwo->co", window, gradient, preferred_element_type=jnp.float32)
            )
    return jnp.stack(taps).reshape(3, 3, inputs.shape[3], gradient.shape[3])


def sums_forward(hidden):
    return (jnp.sum(hidden, axis=(0, 1, 2)), jnp.sum(hidden * hidden, axis=(0, 1, 2)))


def normed_of(hidden, sums, samples):
    average = sums[0] / samples
    inverse = lax.rsqrt(sums[1] / samples - average * average + EPS)
    return ((hidden - average) * inverse, inverse)


def sums_backward(upstream, normed):
    return (jnp.sum(upstream, axis=(0, 1, 2)), jnp.sum(upstream * normed, axis=(0, 1, 2)))


def hidden_grad(upstream, normed, inverse, gain, sums, samples):
    return (
        gain * inverse * (upstream - sums[0] / samples - normed * (sums[1] / samples))
    ).astype(jnp.bfloat16)


def each(function, *lists):
    return [function(*items) for items in zip(*lists)]


def columns(array, axis):
    own = array.shape[axis] // lax.axis_size("narrow")
    return lax.dynamic_slice_in_dim(array, lax.axis_index("narrow") * own, own, axis)


def dot(form, left, right):
    return jnp.einsum(form, left, right, preferred_element_type=jnp.float32)


def plain_body(
    input_five,
    input_seven,
    input_nine,
    upstream_five,
    upstream_seven,
    upstream_nine,
    reduce_weight,
    spatial_weight,
    expand_weight,
    gain_first,
    shift_first,
    gain_second,
    shift_second,
    gain_third,
    shift_third,
):
    inputs = [input_five, input_seven, input_nine]
    upstreams = [upstream_five, upstream_seven, upstream_nine]
    samples = [
        x.shape[0] * lax.axis_size("wide") * x.shape[1] * x.shape[2] for x in inputs
    ]
    whole_reduce = lax.all_gather(reduce_weight, "narrow", axis=1, tiled=True)
    whole_spatial = lax.all_gather(spatial_weight, "narrow", axis=3, tiled=True)
    own_expand = lax.all_to_all(expand_weight, "narrow", 1, 0, tiled=True)
    vectors = jnp.stack([gain_first, shift_first, gain_second, shift_second])
    gain1, shift1, gain2, shift2 = lax.all_gather(vectors, "narrow", axis=1, tiled=True)

    hidden1 = each(lambda x: dot("bhwc,cd->bhwd", x, whole_reduce), inputs)
    sums1 = lax.psum(each(sums_forward, hidden1), "wide")
    normed1, inverse1 = zip(*each(normed_of, hidden1, sums1, samples))
    pre1 = each(lambda n: n * gain1 + shift1, normed1)
    active1 = each(lambda p: jax.nn.silu(p).astype(jnp.bfloat16), pre1)

    hidden2 = each(lambda a: spatial(a, whole_spatial), active1)
    sums2 = lax.psum(each(sums_forward, hidden2), "wide")
    normed2, inverse2 = zip(*each(normed_of, hidden2, sums2, samples))
    pre2 = each(lambda n: n * gain2 + shift2, normed2)
    active2 = each(lambda p: jax.nn.silu(p).astype(jnp.bfloat16), pre2)

    hidden3 = each(lambda a: dot("bhwi,id->bhwd", a, own_expand), active2)
    sums3 = lax.psum(each(sums_forward, hidden3), "wide")
    normed3, inverse3 = zip(*each(normed_of, hidden3, sums3, samples))
    summed = each(
        lambda n, x: n * gain_third + shift_third + columns(x, 3).astype(jnp.float32),
        normed3,
        inputs,
    )
    results = each(lambda z: jax.nn.silu(z).astype(jnp.bfloat16), summed)
    grads_z = each(lambda u, z: u.astype(jnp.float32) * silu_slope(z), upstreams, summed)
    back3 = lax.psum(each(sums_backward, grads_z, normed3), "wide")
    grad3 = each(
        lambda e, n, r, s, m: hidden_grad(e, n, r, gain_third, s, m),
        grads_z,
        normed3,
        inverse3,
        back3,
        samples,
    )
    expand_grad = sum(each(lambda a, g: dot("bhwi,bhwd->id", a, g), active2, grad3))
    active_grad2 = each(
        lambda g: lax.psum(
            dot("bhwd,id->bhwi", g, own_expand).astype(jnp.bfloat16), "narrow"
        ).astype(jnp.float32),
        grad3,
    )
    grads_2 = each(lambda a, p: a * silu_slope(p), active_grad2, pre2)
    back2 = lax.psum(each(sums_backward, grads_2, normed2), "wide")
    grad2 = each(
        lambda e, n, r, s, m: hidden_grad(e, n, r, gain2, s, m),
        grads_2,
        normed2,
        inverse2,
        back2,
        samples,
    )
    spatial_grad = sum(each(lambda a, g: kernel_grad(a, columns(g, 3)), active1, grad2))
    flipped = jnp.transpose(whole_spatial[::-1, ::-1], (0, 1, 3, 2))
    grads_1 = each(lambda g, p: spatial(g, flipped) * silu_slope(p), grad2, pre1)
    back1 = lax.psum(each(sums_backward, grads_1, normed1), "wide")
    grad1 = each(
        lambda e, n, r, s, m: hidden_grad(e, n, r, gain1, s, m),
        grads_1,
        normed1,
        inverse1,
        back1,
        samples,
    )
    reduce_grad = sum(each(lambda x, g: dot("bhwc,bhwd->cd", x, columns(g, 3)), inputs, grad1))
    own_reduce = columns(whole_reduce, 0)
    in_grads = each(lambda g, e: dot("bhwd,cd->bhwc", g, own_reduce) + e, grad1, grads_z)

    low = [g.astype(jnp.bfloat16) for g in (reduce_grad, spatial_grad, expand_grad)]
    low[2] = lax.all_to_all(low[2], "narrow", 0, 1, tiled=True)
    totals = [g.astype(jnp.float32) for g in lax.psum(low, "wide")]

    def params(back, part):
        shift = sum(s[0] for s in back)
        gain = sum(s[1] for s in back)
        return [part(gain), part(shift)]

    def own(vector):
        return columns(vector, 0)

    small = params(back1, own) + params(back2, own) + params(back3, lambda v: v)
    return tuple(results + in_grads + totals + small)


class Shape:
    def __init__(self, mesh, maps, images, depth, inner):
        self.wide, self.narrow = mesh.shape["wide"], mesh.shape["narrow"]
        self.chips = self.wide // 2
        self.maps = maps
        self.images = images
        self.depth, self.inner = depth, inner
        self.own = inner // self.narrow
        self.block = depth // self.narrow
        self.rows = [images * side * side for side in maps]
        self.samples = [float(rows * self.wide) for rows in self.rows]

    def fits(self):
        return (
            self.narrow >= 4
            and self.narrow % 2 == 0
            and self.chips == 4
            and self.wide == 8
            and min(self.maps) >= 3
            and self.block == self.inner
            and self.own % 128 == 0
            and self.images % 16 == 0
            and self.own % (16 * self.wide) == 0
            and self.inner % 512 == 0
        )


def cuts(side, most):
    longest = max(1, most // side)
    number = -(-side // longest)
    edges = [side * n // number for n in range(number + 1)]
    return [(a, b - a) for a, b in zip(edges, edges[1:])]


class Pool:
    def __init__(self, ref):
        self.ref, self.used = ref, 0

    def take(self):
        assert self.used < SEMAPHORES
        self.used += 1
        return self.ref.at[self.used - 1]


MESH = pl.DeviceIdType.MESH
INVERSE, MINUS, SCALE, OFFSET, SHIFTSUM, GAINSUM, LINEAR, CONSTANT = range(8)
GIVEN, SPARE = 72, 80
SEMAPHORES = 600
VMEM_BYTES = 67_000_000
SLAB, CHUNK = 28, 9
WEIGHT_PARTS = 3


def dot_nn(left, right):
    return lax.dot_general(
        left, right, (((1,), (0,)), ((), ())), preferred_element_type=jnp.float32
    )


def dot_nt(left, right):
    return lax.dot_general(
        left, right, (((1,), (1,)), ((), ())), preferred_element_type=jnp.float32
    )


def dot_tn(left, right):
    return lax.dot_general(
        left, right, (((0,), (0,)), ((), ())), preferred_element_type=jnp.float32
    )


def logistic(argument):
    return 0.5 * jnp.tanh(0.5 * argument) + 0.5


class Step:
    def __init__(self, key, run, time, after, rank, hook=None):
        self.key, self.run, self.time = key, run, time
        self.after, self.rank, self.hook = after, rank, hook
        self.ready = 0.0


def arrange(steps, trace=None):
    named = {step.key: step for step in steps}
    done = {}
    now = 0.0
    order = []
    waiting = list(steps)
    while waiting:
        best = None
        for place, step in enumerate(waiting):
            if any(key not in done for key, _ in step.after):
                continue
            at = max([step.ready] + [done[key] + delay for key, delay in step.after])
            choice = (max(at, now), step.rank, place)
            if best is None or choice < best[0]:
                best = (choice, step)
        (start, _, _), step = best
        now = start + step.time
        done[step.key] = now
        waiting.remove(step)
        order.append(step)
        if trace is not None:
            trace.append((start, now, step.key))
        if step.hook is not None:
            step.hook(now, named)
    return order


def block_kernel(shape, *refs):
    wide, narrow, chips = shape.wide, shape.narrow, shape.chips
    inner, own, block, images = shape.inner, shape.own, shape.block, shape.images
    maps = shape.maps
    refs = list(refs)

    def take(count):
        taken = refs[:count]
        del refs[:count]
        return taken

    x_in, u_in = take(3), take(3)
    rw_in, sw_in, ew_in = take(3)
    vec_in = take(6)
    y_out, i_out = take(3), take(3)
    rg_out, sg_out, eg_out = take(3)
    vec_out = take(6)
    xb = take(3)
    rwf, swf, ewf = take(3)
    h1, h2, h3, dz = take(3), take(3), take(3), take(3)
    apad, dpad = take(3), take(3)
    rin, rx = take(3), take(3)
    sacc, eacc, racc = take(3)
    slow, elow, rlow = take(3)
    sr1, er1, rr1 = take(3)
    sr2, er2, rr2 = take(3)
    sfin, efin, rfin = take(3)
    epz, rpz = take(2)
    stat_s, stat_r, sums, vec, vec_all = take(5)
    vec_own, vec_made = take(6), take(6)
    pool = Pool(*take(1))

    w = lax.axis_index("wide")
    z = lax.axis_index("narrow")
    core = lax.rem(w, 2)
    chip = lax.div(w, 2)
    sibling = chip * 2 + (1 - core)
    half = narrow // 2
    inward = jnp.where(z < half, z + 1, z - 1)
    outward = jnp.where(z < half, z - 1, z + 1)
    center = jnp.logical_or(z == half - 1, z == half)
    end = jnp.logical_or(z == 0, z == narrow - 1)
    k_own, k_a2, k_dh, k_p = [lax.rem(z + k, narrow) for k in range(4)]
    finish = []
    arrivals = []

    def once(wait):
        made = []

        def noted():
            if not made:
                made.append(True)
                wait()

        arrivals.append(noted)
        return noted

    def remote(source, target, device):
        send, recv = pool.take(), pool.take()

        def make():
            return pltpu.make_async_remote_copy(
                src_ref=source(),
                dst_ref=target(),
                send_sem=send,
                recv_sem=recv,
                device_id=device,
                device_id_type=MESH,
            )

        make().start()
        finish.append(lambda: make().wait_send())
        return once(lambda: make().wait_recv())

    def local(source, target):
        semaphore = pool.take()

        def make():
            return pltpu.make_async_copy(source(), target(), semaphore)

        make().start()
        return once(lambda: make().wait())

    def span(start, size, unit):
        return pl.ds(pl.multiple_of(start * unit, unit), size)

    def rows_of(g, cut):
        return pl.ds(cut[0] * maps[g] * images, cut[1] * maps[g] * images)

    slabs = [cuts(side, SLAB) for side in maps]
    chunks = [cuts(side, CHUNK) for side in maps]

    def lines(g, cut, function):
        size = maps[g] * images
        if cut[1] == 1:
            function(cut[0], pl.ds(cut[0] * size, size))
        else:
            pl.loop(cut[0], cut[0] + cut[1])(
                lambda y: function(y, pl.ds(pl.multiple_of(y * size, 16), size))
            )

    chip_x = chip + 1 - 2 * lax.rem(chip, 2)
    chip_y = lax.rem(chip + 2, chips)
    chip_far = lax.rem(chip_x + 2, chips)
    origins = [lax.rem(z + narrow - k, narrow) for k in range(1, narrow)]

    class Gather:
        def __init__(self, source, target):
            self.source, self.target = source, target
            self.from_x, self.from_y, self.far, self.crossed = [], [], [], []

        def first(self):
            self.arrived = [
                remote(
                    lambda peer=peer: self.source(w, peer),
                    lambda: self.target(w, z),
                    (w, peer),
                )
                for peer in [lax.rem(z + k, narrow) for k in range(1, narrow)]
            ]

        def send(self, holder, origin, part, device):
            def piece():
                return self.target(holder * 2 + core, origin, part)

            return remote(piece, piece, (device, z))

        def spread(self):
            for origin, wait in zip(origins, self.arrived):
                wait()
                self.from_x.append(self.send(chip, origin, None, chip_x * 2 + core))
                self.from_y.append(self.send(chip, origin, None, chip_y * 2 + core))
            for origin in origins:
                self.crossed.append(self.send(chip, origin, None, sibling))

        def relay(self):
            for origin, got_x, got_y in zip(origins, self.from_x, self.from_y):
                got_x()
                along_y = self.send(chip_x, origin, 0, chip_y * 2 + core)
                got_y()
                along_x = self.send(chip_y, origin, 1, chip_x * 2 + core)
                self.far.append((along_y, along_x))
            for origin in origins:
                self.crossed.append(self.send(chip_x, origin, None, sibling))
                self.crossed.append(self.send(chip_y, origin, None, sibling))

        def cross(self):
            for origin, waits in zip(origins, self.far):
                for wait in waits:
                    wait()
                self.crossed.append(self.send(chip_far, origin, None, sibling))

        def ready(self):
            for wait in self.crossed:
                wait()

    rw_piece, sw_piece, ew_piece = shape.depth // wide, inner // wide, own // wide
    part = 9 // WEIGHT_PARTS

    def half_of(h, size, unit, half):
        if half is None:
            return span(h, size, size)
        return pl.ds(pl.multiple_of(h * size + half * (size // 2), unit), size // 2)

    def sw_item(n):
        taps = pl.ds(n * part, part)
        return Gather(
            lambda h, peer: sw_in.at[taps, span(h, sw_piece, sw_piece), :],
            lambda h, o, half=None: swf.at[taps, half_of(h, sw_piece, 16, half), span(o, own, own)],
        )

    gathers = (
        [
            Gather(
                lambda h, peer: rw_in.at[span(h, rw_piece, rw_piece), :],
                lambda h, o, half=None: rwf.at[half_of(h, rw_piece, 16, half), span(o, own, own)],
            )
        ]
        + [sw_item(n) for n in range(WEIGHT_PARTS)]
        + [
            Gather(
                lambda h, peer: ew_in.at[span(h, ew_piece, ew_piece), span(peer, block, block)],
                lambda h, o, half=None: ewf.at[
                    pl.ds(pl.multiple_of(o * own + h * ew_piece, 16), ew_piece),
                    pl.ds(0, block) if half is None else pl.ds(half * (block // 2), block // 2),
                ],
            )
        ]
    )
    x_wait = [[None] * narrow for _ in range(3)]
    u_wait, y_wait = [None] * 3, [None] * 3
    own_waits, vec_waits = [], []

    def slot(kind, level, g):
        return (kind * 3 + level) * 3 + g

    def put(place, value):
        vec[place : place + 1, :] = value

    def get(place):
        return vec[place : place + 1, :]

    def begin():
        got = [local(lambda a=a: a, lambda b=b: b) for a, b in zip(vec_in, vec_own)]
        barrier = pltpu.get_barrier_semaphore()
        for k in range(1, wide):
            pl.semaphore_signal(
                barrier, inc=1, device_id=(lax.rem(w + k, wide), z), device_id_type=MESH
            )
        for k in range(1, narrow):
            pl.semaphore_signal(
                barrier, inc=1, device_id=(w, lax.rem(z + k, narrow)), device_id_type=MESH
            )
        for source, target in (
            (lambda: rw_in, lambda: rwf.at[:, span(z, own, own)]),
            (lambda: sw_in, lambda: swf.at[:, :, span(z, own, own)]),
            (lambda: ew_in.at[:, span(z, block, block)], lambda: ewf.at[span(z, own, own), :]),
        ):
            own_waits.append(local(source, target))
        for g in range(3):
            for k in range(narrow):
                x_wait[g][k] = local(
                    lambda g=g, k=k: x_in[g].at[:, pl.ds(k * block, block)],
                    lambda g=g, k=k: xb[g].at[k],
                )
        for wait in got:
            wait()
        vec_all[z] = jnp.concatenate(
            [v[...] for v in vec_own[:4]] + [jnp.zeros((4, own), jnp.float32)], axis=0
        )
        pl.semaphore_wait(barrier, wide - 1 + narrow - 1)
        for k in range(1, narrow):
            vec_waits.append(
                remote(lambda: vec_all.at[z], lambda: vec_all.at[z], (w, lax.rem(z + k, narrow)))
            )
        for item in gathers:
            item.first()

    def pads():
        for g in range(3):
            side = maps[g]
            for pad in (apad[g], dpad[g]):
                pad[0] = jnp.zeros((side + 2, images, inner), jnp.bfloat16)
                pad[side + 1] = jnp.zeros((side + 2, images, inner), jnp.bfloat16)
                for edge in (0, side + 1):
                    pad[1 : side + 1, edge] = jnp.zeros((side, images, inner), jnp.bfloat16)
        for acc in (sacc, eacc, racc):

            def clear(a, acc=acc):
                acc[a] = jnp.zeros(acc.shape[1:], jnp.float32)

            pl.loop(0, acc.shape[0])(clear)

    def vectors():
        for wait in vec_waits:
            wait()
        for row in range(4):
            put(
                GIVEN + row,
                jnp.concatenate([vec_all[k, row : row + 1, :] for k in range(narrow)], axis=1),
            )
        for row in (4, 5):
            put(GIVEN + row, vec_own[row][...])

    tiles = inner // 128
    stat_sems, stat_arrived = {}, {}

    def stats_all(e):
        send, recv = stat_sems[e]
        return pltpu.make_async_remote_copy(
            src_ref=stat_r.at[e, pl.ds(0, wide - 1)],
            dst_ref=stat_r.at[e, pl.ds(0, wide - 1)],
            send_sem=send,
            recv_sem=recv,
            device_id=(sibling, z),
            device_id_type=MESH,
        )

    def stats_wait(e):
        stat_arrived[e]()
        total = stat_r[e, 0]
        for k in range(1, wide):
            total = total + stat_r[e, k]
        return [
            jnp.concatenate(
                [total[t * tiles + b : t * tiles + b + 1, :] for b in range(tiles)], axis=1
            )
            for t in range(2)
        ]

    class Sums:
        def __init__(self, e):
            self.row = 2 * e
            self.e = e

        def clear(self):
            sums[self.row : self.row + 2, :] = jnp.zeros((2, inner), jnp.float32)

        def add(self, first, second):
            sums[self.row : self.row + 1, :] += jnp.sum(first, axis=0, keepdims=True)
            sums[self.row + 1 : self.row + 2, :] += jnp.sum(second, axis=0, keepdims=True)

    totals_of = {e: Sums(e) for e in range(18)}

    def send_sums(e):
        row = totals_of[e].row
        for t in range(2):
            for b in range(tiles):
                stat_s[e, t * tiles + b : t * tiles + b + 1, :] = sums[
                    row + t : row + t + 1, b * 128 : (b + 1) * 128
                ]
        stat_r[e, w] = stat_s[e]
        send, recv = pool.take(), pool.take()
        stat_sems[e] = (send, recv)
        stat_arrived[e] = once(lambda: stats_all(e).wait_recv())
        finish.append(lambda: stats_all(e).wait_send())

        def one(k, carry):
            pltpu.make_async_remote_copy(
                src_ref=stat_s.at[e],
                dst_ref=stat_r.at[e, w],
                send_sem=send,
                recv_sem=recv,
                device_id=(lax.rem(w + k, wide), z),
                device_id_type=MESH,
            ).start()
            return carry

        lax.fori_loop(1, wide, one, 0)

    def norm_vectors(g, level):
        first, second = stats_wait(g * 6 + level)
        mean = first / shape.samples[g]
        inverse = lax.rsqrt(second / shape.samples[g] - mean * mean + EPS)
        scale = inverse * get(GIVEN + 2 * level)
        put(slot(INVERSE, level, g), inverse)
        put(slot(MINUS, level, g), -mean * inverse)
        put(slot(SCALE, level, g), scale)
        put(slot(OFFSET, level, g), get(GIVEN + 2 * level + 1) - mean * scale)

    def back_vectors(g, level):
        shift_sum, gain_sum = stats_wait(g * 6 + 5 - level)
        put(slot(SHIFTSUM, level, g), shift_sum)
        put(slot(GAINSUM, level, g), gain_sum)
        scale = get(slot(SCALE, level, g))
        c1 = scale * (gain_sum / shape.samples[g])
        put(slot(LINEAR, level, g), -get(slot(INVERSE, level, g)) * c1)
        put(slot(CONSTANT, level, g), -get(slot(MINUS, level, g)) * c1 - scale * (shift_sum / shape.samples[g]))

    def f1(g, cut):
        run = totals_of[g * 6]
        if cut[0] == 0:
            for wait in x_wait[g]:
                wait()
            run.clear()
        rows = rows_of(g, cut)
        left = jnp.concatenate([xb[g][k, rows, :] for k in range(narrow)], axis=1)
        result = dot_nn(left, rwf[...])
        h1[g][rows, :] = result
        run.add(result, result * result)

    def f1_end(g):
        send_sums(g * 6)
        u_wait[g] = local(lambda: u_in[g], lambda: xb[g].at[k_dh])

    def a1(g):
        scale, offset = get(slot(SCALE, 0, g)), get(slot(OFFSET, 0, g))
        side = maps[g]

        def one(y, rows):
            pre = h1[g][rows, :] * scale + offset
            value = (pre * logistic(pre)).astype(jnp.bfloat16)
            apad[g][y + 1, pl.ds(1, side)] = value.reshape(side, images, inner)

        lines(g, (0, side), one)

    def windows(pad, g, cut, lines_of_taps):
        side = maps[g]
        return jnp.concatenate(
            [
                pad[cut[0] + i : cut[0] + i + cut[1], j : j + side].reshape(
                    cut[1] * side * images, inner
                )
                for i in lines_of_taps
                for j in range(3)
            ],
            axis=1,
        )

    def f2(g, n, cut):
        run = totals_of[g * 6 + 1]
        rows = rows_of(g, cut)
        result = dot_nn(windows(apad[g], g, cut, (n,)), swf[3 * n : 3 * n + 3].reshape(-1, inner))
        if n > 0:
            result = result + h2[g][rows, :]
        h2[g][rows, :] = result
        if n == 2:
            if cut[0] == 0:
                run.clear()
            run.add(result, result * result)

    def a2(g):
        scale, offset = get(slot(SCALE, 1, g)), get(slot(OFFSET, 1, g))

        def one(y, rows):
            pre = h2[g][rows, :] * scale + offset
            xb[g][k_a2, rows, :] = (pre * logistic(pre)).astype(jnp.bfloat16)

        lines(g, (0, maps[g]), one)

    def f3(g):
        run = totals_of[g * 6 + 2]
        run.clear()
        for cut in slabs[g]:
            rows = rows_of(g, cut)
            result = dot_nn(xb[g][k_a2, rows, :], ewf[...])
            h3[g][rows, :] = result
            run.add(result, result * result)

    def a3(g):
        run = totals_of[g * 6 + 3]
        run.clear()
        scale, offset = get(slot(SCALE, 2, g)), get(slot(OFFSET, 2, g))
        inverse, minus = get(slot(INVERSE, 2, g)), get(slot(MINUS, 2, g))

        def one(y, rows):
            hidden = h3[g][rows, :]
            total = hidden * scale + offset + xb[g][k_own, rows, :].astype(jnp.float32)
            sig = logistic(total)
            xb[g][k_p, rows, :] = (total * sig).astype(jnp.bfloat16)
            slope = sig * (1.0 + total * (1.0 - sig))
            grad = xb[g][k_dh, rows, :].astype(jnp.float32) * slope
            dz[g][rows, :] = grad
            run.add(grad, grad * (hidden * inverse + minus))

        lines(g, (0, maps[g]), one)

    def a3_end(g):
        send_sums(g * 6 + 3)
        y_wait[g] = local(lambda: xb[g].at[k_p], lambda: y_out[g])

    def b3(g, cut):
        scale, k1, k0 = get(slot(SCALE, 2, g)), get(slot(LINEAR, 2, g)), get(slot(CONSTANT, 2, g))
        rows = rows_of(g, cut)
        value = dz[g][rows, :] * scale + h3[g][rows, :] * k1 + k0
        low = value.astype(jnp.bfloat16)
        xb[g][k_dh, rows, :] = low
        xb[g][k_p, rows, :] = dot_nt(low, ewf[...]).astype(jnp.bfloat16)
        c = chunks[g].index(cut)
        reductions[g, c] = copies = Reduction(g, c)
        pl.when(end)(lambda: copies.to_inner().start())

    def eg(g):
        result = dot_tn(xb[g][k_a2], xb[g][k_dh])
        for k in range(narrow):
            piece = result[k * own : (k + 1) * own, :].reshape(eacc.shape[1:])
            eacc[k] += piece

    reductions = {}

    class Reduction:
        def __init__(self, g, c):
            self.g, self.rows = g, rows_of(g, chunks[g][c])
            self.sems = [pool.take() for _ in range(5)]
            self.inwards = once(self.add_outer)
            self.across = once(self.add_other)
            self.home = once(lambda: pl.when(end)(lambda: self.to_center().wait_recv()))
            finish.append(self.sent)

        def copy(self, source, target, send, recv, device):
            return pltpu.make_async_remote_copy(
                src_ref=source.at[self.rows, :],
                dst_ref=target.at[self.rows, :],
                send_sem=self.sems[send],
                recv_sem=self.sems[recv],
                device_id=(w, device),
                device_id_type=MESH,
            )

        def to_inner(self):
            return self.copy(xb[self.g].at[k_p], rin[self.g], 0, 1, inward)

        def to_center(self):
            return self.copy(xb[self.g].at[k_p], rx[self.g], 2, 3, inward)

        def to_outer(self):
            return self.copy(rx[self.g], rx[self.g], 4, 3, outward)

        def add_outer(self):
            g, rows = self.g, self.rows

            @pl.when(jnp.logical_not(end))
            def _():
                self.to_inner().wait_recv()
                xb[g][k_p, rows, :] = (
                    xb[g][k_p, rows, :].astype(jnp.float32) + rin[g][rows, :].astype(jnp.float32)
                ).astype(jnp.bfloat16)
                pl.when(center)(lambda: self.to_center().start())
                pl.when(jnp.logical_not(center))(lambda: self.to_inner().start())

        def add_other(self):
            g, rows = self.g, self.rows

            @pl.when(jnp.logical_not(end))
            def _():
                self.to_center().wait_recv()

                @pl.when(center)
                def _():
                    rx[g][rows, :] = (
                        rx[g][rows, :].astype(jnp.float32)
                        + xb[g][k_p, rows, :].astype(jnp.float32)
                    ).astype(jnp.bfloat16)

                self.to_outer().start()

        def sent(self):
            pl.when(center)(lambda: self.to_center().wait_send())
            pl.when(jnp.logical_not(center))(lambda: self.to_inner().wait_send())
            pl.when(jnp.logical_not(end))(lambda: self.to_outer().wait_send())

    def za(g, c):
        reductions[g, c].inwards()

    def zb(g, c):
        reductions[g, c].across()

    def g2(g, c):
        run = totals_of[g * 6 + 4]
        if c == 0:
            run.clear()
        reductions[g, c].home()
        scale, offset = get(slot(SCALE, 1, g)), get(slot(OFFSET, 1, g))
        inverse, minus = get(slot(INVERSE, 1, g)), get(slot(MINUS, 1, g))

        def one(y, rows):
            hidden = h2[g][rows, :]
            pre = hidden * scale + offset
            sig = logistic(pre)
            grad = rx[g][rows, :].astype(jnp.float32) * (sig * (1.0 + pre * (1.0 - sig)))
            h3[g][rows, :] = grad
            run.add(grad, grad * (hidden * inverse + minus))

        lines(g, chunks[g][c], one)

    def d2(g):
        scale, k1, k0 = get(slot(SCALE, 1, g)), get(slot(LINEAR, 1, g)), get(slot(CONSTANT, 1, g))
        side = maps[g]

        def one(y, rows):
            value = h3[g][rows, :] * scale + h2[g][rows, :] * k1 + k0
            dpad[g][y + 1, pl.ds(1, side)] = value.astype(jnp.bfloat16).reshape(side, images, inner)

        lines(g, (0, side), one)

    def sg(g):
        side = maps[g]
        left = apad[g][1 : side + 1, 1 : side + 1].reshape(shape.rows[g], inner)
        right = jnp.concatenate(
            [
                dpad[g][2 - i : 2 - i + side, 2 - j : 2 - j + side, :, span(z, own, own)].reshape(
                    shape.rows[g], own
                )
                for i in range(3)
                for j in range(3)
            ],
            axis=1,
        )
        result = dot_tn(left, right)
        for t in range(9):
            piece = result[:, t * own : (t + 1) * own].reshape(sacc.shape[1:])
            sacc[t] += piece

    def f1b(g, cut):
        run = totals_of[g * 6 + 5]
        if cut[0] == 0:
            run.clear()
        rows = rows_of(g, cut)
        left = windows(dpad[g], g, cut, range(3))
        right = jnp.concatenate([swf[8 - t] for t in range(9)], axis=1)
        h2[g][rows, :] = dot_nt(left, right)

    def g1(g, cut):
        run = totals_of[g * 6 + 5]
        scale, offset = get(slot(SCALE, 0, g)), get(slot(OFFSET, 0, g))
        inverse, minus = get(slot(INVERSE, 0, g)), get(slot(MINUS, 0, g))

        def one(y, rows):
            hidden = h1[g][rows, :]
            pre = hidden * scale + offset
            sig = logistic(pre)
            grad = h2[g][rows, :] * (sig * (1.0 + pre * (1.0 - sig)))
            h2[g][rows, :] = grad
            run.add(grad, grad * (hidden * inverse + minus))

        lines(g, cut, one)

    def d1(g):
        scale, k1, k0 = get(slot(SCALE, 0, g)), get(slot(LINEAR, 0, g)), get(slot(CONSTANT, 0, g))

        def one(y, rows):
            value = h2[g][rows, :] * scale + h1[g][rows, :] * k1 + k0
            xb[g][k_dh, rows, :] = value.astype(jnp.bfloat16)

        lines(g, (0, maps[g]), one)

    def ig(g):
        for cut in slabs[g]:
            rows = rows_of(g, cut)
            right = rwf[span(z, block, block), :]
            h3[g][rows, :] = dot_nt(xb[g][k_dh, rows, :], right) + dz[g][rows, :]
        finish.append(local(lambda: h3[g], lambda: i_out[g]))

    def rg(g):
        result = dot_tn(xb[g][k_own], xb[g][k_dh])
        for k in range(narrow):
            piece = result[:, k * own : (k + 1) * own].reshape(racc.shape[1:])
            racc[k] += piece

    class Total:
        def __init__(self, acc, low, first, second, final, piece, out):
            self.acc, self.low, self.first, self.second = acc, low, first, second
            self.final, self.piece, self.out = final, piece, out
            self.count = acc.shape[0]

        def one(self):
            def cast(a):
                self.low[a] = self.acc[a, :, 1 - core].astype(jnp.bfloat16)

            pl.loop(0, self.count)(cast)
            self.got1 = remote(lambda: self.low, lambda: self.first, (sibling, z))

        def two(self):
            self.got1()

            def add(a):
                self.first[a] = (
                    self.first[a].astype(jnp.float32) + self.acc[a, :, core]
                ).astype(jnp.bfloat16)

            pl.loop(0, self.count)(add)
            self.got2 = []
            for j in range(1, chips):
                peer = lax.rem(chip + j, chips)
                self.got2.append(
                    remote(
                        lambda peer=peer: self.first.at[:, peer],
                        lambda: self.second.at[chip],
                        (peer * 2 + core, z),
                    )
                )

        def three(self):
            for wait in self.got2:
                wait()
            self.second[chip] = self.first[:, chip]
            target = self.final.at[:, chip, core] if self.piece is None else self.piece

            def add(a):
                total = self.second[0, a].astype(jnp.float32)
                for k in range(1, chips):
                    total = total + self.second[k, a].astype(jnp.float32)
                target[a] = total.astype(jnp.bfloat16)

            pl.loop(0, self.count)(add)
            if self.piece is None:
                self.send_pieces()
                return
            self.got3 = []
            for k in range(1, narrow):
                peer = lax.rem(z + k, narrow)
                self.got3.append(
                    remote(
                        lambda peer=peer: self.piece.at[peer],
                        lambda: self.final.at[z, chip, core],
                        (w, peer),
                    )
                )
            self.final[z, chip, core] = self.piece[z]

        def exchange(self):
            for wait in self.got3:
                wait()
            self.send_pieces()

        def send_pieces(self):
            self.got4, self.got5 = [], []

            def piece():
                return self.final.at[:, chip, core]

            for j in range(1, chips):
                peer = lax.rem(chip + j, chips)
                self.got4.append((j, remote(piece, piece, (peer * 2 + core, z))))
            self.got5.append(remote(piece, piece, (sibling, z)))

        def four(self):
            for j, arrived in self.got4:
                arrived()
                holder = lax.rem(chip + chips - j, chips)

                def piece(holder=holder):
                    return self.final.at[:, holder, core]

                self.got5.append(remote(piece, piece, (sibling, z)))

        def five(self):
            for wait in self.got5:
                wait()
            finish.append(local(lambda: self.final, lambda: self.out))

    stotal = Total(sacc, slow, sr1, sr2, sfin, None, sg_out)
    etotal = Total(eacc, elow, er1, er2, efin, epz, eg_out)
    rtotal = Total(racc, rlow, rr1, rr2, rfin, rpz, rg_out)

    def params():
        for place in range(6):
            level, kind = place // 2, GAINSUM if place % 2 == 0 else SHIFTSUM
            total = sum(get(slot(kind, level, g)) for g in range(3))
            if level == 2:
                vec_made[place][...] = total
            else:
                put(SPARE, total)
                vec_made[place][...] = vec[SPARE : SPARE + 1, span(z, own, own)]
            finish.append(
                local(lambda place=place: vec_made[place], lambda place=place: vec_out[place])
            )

    steps = []
    order = T.order

    def add(key, run, time, after, rank, hook=None):
        steps.append(Step(key, run, time, after, rank, hook))

    START, CLEAR, VECTORS = (begin,), (pads,), (vectors,)
    add(START, begin, 5.0, [], 0)
    add(CLEAR, pads, 1.0, [(START, 0.0)], 1)
    add(VECTORS, vectors, 0.2, [(START, 5.0)], 2)

    def spread(n):
        gathers[n].spread()

    def relay(n):
        gathers[n].relay()

    def cross(n):
        gathers[n].cross()

    def ready(n):
        if n == 0:
            for wait in own_waits:
                wait()
        gathers[n].ready()

    for n in range(len(gathers)):
        wait = T.xy[n]
        for f, time, after in (
            (spread, 0.2, [(START, T.z[n])]),
            (relay, 0.2, [((spread, n), wait)]),
            (cross, 0.1, [((relay, n), wait * 0.7)]),
            (ready, 0.1, [((cross, n), 1.5)]),
        ):
            if n > 0 and f is not ready:
                after = after + [((f, n - 1), T.xy[n] * 0.8 if f is relay else 0.0)]
            add((f, n), functools.partial(f, n), time, after, 0.0 if n < 4 else 0.1)

    link = {za: 0.0, zb: 0.0, g2: 0.0}

    def transfer(key, size):
        def hook(now, named):
            link[key[0]] = max(link[key[0]], now) + size * T.hop
            named[key].ready = link[key[0]] + T.lat

        return hook

    class Do:
        def __init__(self, g):
            self.g = g

        def f1(self, s):
            f1(self.g, slabs[self.g][s])
            if s == len(slabs[self.g]) - 1:
                f1_end(self.g)

        def a1(self):
            norm_vectors(self.g, 0)
            a1(self.g)

        def f2(self, n, s):
            f2(self.g, n, slabs[self.g][s])
            if n == 2 and s == len(slabs[self.g]) - 1:
                send_sums(self.g * 6 + 1)

        def a2(self):
            norm_vectors(self.g, 1)
            a2(self.g)
            f3(self.g)
            send_sums(self.g * 6 + 2)

        def a3(self):
            norm_vectors(self.g, 2)
            u_wait[self.g]()
            a3(self.g)
            a3_end(self.g)

        def b3(self, c):
            if c == 0:
                back_vectors(self.g, 2)
                y_wait[self.g]()
            b3(self.g, chunks[self.g][c])

        def g2(self, c):
            g2(self.g, c)
            if c == len(chunks[self.g]) - 1:
                send_sums(self.g * 6 + 4)

        def d2(self):
            back_vectors(self.g, 1)
            d2(self.g)

        def f1b(self, s):
            f1b(self.g, slabs[self.g][s])
            g1(self.g, slabs[self.g][s])
            if s == len(slabs[self.g]) - 1:
                send_sums(self.g * 6 + 5)

        def d1(self):
            back_vectors(self.g, 0)
            d1(self.g)

    before = None
    for turn, g in enumerate(order):
        do = Do(g)
        size = [shape.rows[g] * n / maps[g] for _, n in chunks[g]]
        scale = shape.rows[g] / 1000.0
        per, last = len(slabs[g]), len(chunks[g]) - 1
        early, late = 2 + turn * 0.3, 4 + turn * 0.3
        for s in range(per):
            after = [((ready, 0), 0.0)] if s == 0 else [((f1, g, s - 1), 0.0)]
            add((f1, g, s), functools.partial(do.f1, s), T.f1 * scale / per, after, early)
        after = [((f1, g, per - 1), T.stat0), (VECTORS, 0.0), (CLEAR, 0.0)]
        add((a1, g), do.a1, T.a1 * scale + 0.2, after, early)
        behind = (a1, g)
        for n in range(3):
            for s in range(per):
                after = [(behind, 0.0), ((ready, n + 1), 0.0)]
                behind = (f2, g, n, s)
                add(behind, functools.partial(do.f2, n, s), T.f2 * scale / per / 3, after, early - 0.1 * n)
        after = [(behind, T.stat), ((ready, 4), 0.0)]
        add((a2, g), do.a2, T.a2 * scale + 0.2, after, early - 0.5)
        add((a3, g), do.a3, T.a3 * scale + 0.2, [((a2, g), T.stat)], early - 0.5)
        for c in range(last + 1):
            after = [((a3, g), T.stat)] if c == 0 else [((b3, g, c - 1), 0.0)]
            if c == 0 and before is not None:
                after.append((before, 0.0))
            add((b3, g, c), functools.partial(do.b3, c), T.b3 * size[c] / 1000.0, after, 1 + turn * 0.3, transfer((za, g, c), size[c]))
            after = [((b3, g, c), 0.0)] + ([((za, g, c - 1), 0.0)] if c else [])
            add((za, g, c), functools.partial(za, g, c), T.za, after, 0, transfer((zb, g, c), size[c]))
            after = [((za, g, c), 0.0)] + ([((zb, g, c - 1), 0.0)] if c else [])
            add((zb, g, c), functools.partial(zb, g, c), T.za, after, 0, transfer((g2, g, c), size[c]))
            after = [((zb, g, c), 0.0)] + ([((g2, g, c - 1), 0.0)] if c else [])
            add((g2, g, c), functools.partial(do.g2, c), T.g2 * size[c] / 1000.0, after, late - 1.5)
        before = (b3, g, last)
        add((d2, g), do.d2, T.d2 * scale + 0.2, [((g2, g, last), T.stat)], late - 1)
        add((eg, g), functools.partial(eg, g), T.eg * scale, [(before, 0.0)], 6)
        final = turn == len(order) - 1
        add((sg, g), functools.partial(sg, g), T.sg * scale, [((d2, g), 0.0)], 3.0 if final else late - T.sg_rank if turn else 5)
        for s in range(per):
            after = [((d2, g), 0.0)] if s == 0 else [((f1b, g, s - 1), 0.0)]
            if turn == len(order) - 2 and s == per - 1:
                after.append(((g2, order[-1], len(chunks[order[-1]]) - 1), 0.0))
            add((f1b, g, s), functools.partial(do.f1b, s), T.f1b * scale / per, after, late - 0.4)
        after = [((f1b, g, per - 1), T.stat_late), ((eg, g), 0.0)]
        add((d1, g), do.d1, T.d1 * scale + 0.2, after, late - 0.5)
        add((rg, g), functools.partial(rg, g), T.rg * scale, [((d1, g), 0.0)], late - 0.5)
        add((ig, g), functools.partial(ig, g), T.ig * scale, [((d1, g), 0.0)], 8)
    for total, source, xfer in ((etotal, eg, 3.0), (stotal, sg, 6.5), (rtotal, rg, 3.5)):
        add((total, 1), total.one, 0.3, [((source, g), 0.0) for g in range(3)], 1)
        add((total, 2), total.two, 0.3, [((total, 1), 2.5)], 1)
        after = [((total, 2), xfer + 2)]
        if total is etotal:
            after.append(((zb, order[-1], len(chunks[order[-1]]) - 1), 0.0))
        add((total, 3), total.three, 0.4, after, 1)
        if total.piece is not None:
            add((total, 4), total.exchange, 0.2, [((total, 3), 5.0 if total is etotal else 2.5)], 1)
        after = [((total, 3 if total.piece is None else 4), xfer + 2)]
        add((total, 5), total.four, 0.2, after, 1)
        add((total, 6), total.five, 0.1, [((total, 5), 2.5)], 7)
    add((params,), params, 0.3, [((d1, g), 0.0) for g in range(3)], 7)
    for step in arrange(steps, TRACE)[:PLAN_END]:
        step.run()
    for wait in arrivals:
        wait()
    for wait in finish:
        wait()


PLAN_END = None
TRACE = None


class T:
    order = (2, 1, 0)
    z = (8.0, 14.5, 18.5, 23.0, 24.0)
    xy = (5.0, 5.0, 5.0, 5.0, 2.0)
    stat0, stat, stat_late = 4.5, 2.8, 5.0
    f1, a1, f2, a2, a3, b3 = 2.5, 0.7, 5.4, 1.3, 2.0, 2.1
    hop, lat, za = 0.022, 2.2, 0.1
    g2, d2, eg, sg, f1b, d1, rg, ig = 1.4, 0.4, 0.7, 2.0, 6.3, 0.4, 0.7, 0.7
    sg_rank = 0.45


def kernel_call(shape, args):
    inner, own, block, depth = shape.inner, shape.own, shape.block, shape.depth
    wide, narrow, chips, images = shape.wide, shape.narrow, shape.chips, shape.images
    bf16, f32 = jnp.bfloat16, jnp.float32

    def struct(dims, kind):
        return jax.ShapeDtypeStruct(dims, kind)

    spread = [
        (9, chips, 2, inner // wide, own),
        (narrow, chips, 2, own // wide, block),
        (narrow, chips, 2, block // wide, own),
    ]
    outs = (
        [struct((rows, block), bf16) for rows in shape.rows]
        + [struct((rows, block), f32) for rows in shape.rows]
        + [struct(spread[2], bf16), struct(spread[0], bf16), struct(spread[1], bf16)]
        + [struct((1, own), f32)] * 4
        + [struct((1, block), f32)] * 2
    )
    anywhere = pl.BlockSpec(memory_space=pl.ANY)

    def each_rows(columns, kind):
        return [pltpu.VMEM((rows, columns), kind) for rows in shape.rows]

    def padded():
        return [pltpu.VMEM((side + 2, side + 2, images, inner), bf16) for side in shape.maps]

    scratch = (
        [pltpu.VMEM((narrow, rows, block), bf16) for rows in shape.rows]
        + [
            pltpu.VMEM((depth, inner), bf16),
            pltpu.VMEM((9, inner, inner), bf16),
            pltpu.VMEM((inner, block), bf16),
        ]
        + each_rows(inner, f32)
        + each_rows(inner, f32)
        + each_rows(block, f32)
        + each_rows(block, f32)
        + padded()
        + padded()
        + each_rows(inner, bf16)
        + each_rows(inner, bf16)
        + [pltpu.VMEM(dims, f32) for dims in spread]
        + [pltpu.VMEM((a, c, b, lanes), bf16) for a, c, _, b, lanes in spread]
        + [pltpu.VMEM((a, c, b, lanes), bf16) for a, c, _, b, lanes in spread]
        + [pltpu.VMEM((c, a, b, lanes), bf16) for a, c, _, b, lanes in spread]
        + [pltpu.VMEM(dims, bf16) for dims in spread]
        + [pltpu.VMEM((a, b, lanes), bf16) for a, _, _, b, lanes in spread[1:]]
        + [
            pltpu.VMEM((18, 2 * inner // 128, 128), f32),
            pltpu.VMEM((18, wide, 2 * inner // 128, 128), f32),
            pltpu.VMEM((40, inner), f32),
            pltpu.VMEM((96, inner), f32),
            pltpu.VMEM((narrow, 8, own), f32),
        ]
        + ([pltpu.VMEM((1, own), f32)] * 4 + [pltpu.VMEM((1, block), f32)] * 2) * 2
        + [pltpu.SemaphoreType.DMA((SEMAPHORES,))]
    )
    return pl.pallas_call(
        functools.partial(block_kernel, shape),
        out_shape=outs,
        in_specs=[anywhere] * 15,
        out_specs=[anywhere] * 15,
        scratch_shapes=scratch,
        compiler_params=pltpu.CompilerParams(
            collective_id=0, has_side_effects=True, vmem_limit_bytes=VMEM_BYTES
        ),
        name="bottleneck",
    )(*args)


def last_kernel(shape, *refs):
    narrow, block = shape.narrow, shape.block
    source, target, held, high, sems = refs[:15], refs[15:30], refs[30:45], refs[45:48], refs[48]
    pool = Pool(sems)
    finish = []

    def copy(source, target):
        semaphore = pool.take()

        def make():
            return pltpu.make_async_copy(source, target, semaphore)

        make().start()
        return lambda: make().wait()

    places = [6, 5, 8, 2, 4, 7, 3, 1, 0] + list(range(9, 15))
    got = {place: copy(source[place], held[place]) for place in places}
    for place in places:
        got[place]()
        if place not in (6, 7, 8):
            finish.append(copy(held[place], target[place]))
            continue
        wide = high[place - 6]

        def widen(a, place=place, wide=wide):
            wide[a] = held[place][a].astype(jnp.float32)

        pl.loop(0, wide.shape[0])(widen)
        if place < 8:
            finish.append(copy(wide, target[place]))
            continue
        for k in range(narrow):
            finish.append(
                copy(wide.at[k], target[place].at[:, :, :, pl.ds(k * block, block)])
            )
    for wait in finish:
        wait()


def last_call(shape, args):
    f32 = jnp.float32
    outs = [jax.ShapeDtypeStruct(a.shape, f32 if 6 <= n < 9 else a.dtype) for n, a in enumerate(args)]
    outs[8] = jax.ShapeDtypeStruct((*args[8].shape[1:-1], shape.depth), f32)
    anywhere = pl.BlockSpec(memory_space=pl.ANY)
    return pl.pallas_call(
        functools.partial(last_kernel, shape),
        out_shape=outs,
        in_specs=[anywhere] * 15,
        out_specs=[anywhere] * 15,
        scratch_shapes=[pltpu.VMEM(a.shape, a.dtype) for a in args]
        + [pltpu.VMEM(a.shape, f32) for a in args[6:9]]
        + [pltpu.SemaphoreType.DMA((64,))],
        compiler_params=pltpu.CompilerParams(vmem_limit_bytes=VMEM_BYTES),
        name="results",
    )(*args)


def kernel_body(shape, *arguments):
    inputs, upstreams = arguments[:3], arguments[3:6]
    reduce_weight, spatial_weight, expand_weight = arguments[6:9]
    vectors = arguments[9:]

    def flat(array):
        return jnp.transpose(array, (1, 2, 0, 3)).reshape(-1, array.shape[3])

    def unflat(array, side):
        return jnp.transpose(
            array.reshape(side, side, shape.images, array.shape[1]), (2, 0, 1, 3)
        )

    results = kernel_call(
        shape,
        [flat(x) for x in inputs]
        + [flat(u) for u in upstreams]
        + [
            reduce_weight,
            spatial_weight.reshape(9, shape.inner, shape.own),
            expand_weight,
        ]
        + [v.reshape(1, -1) for v in vectors],
    )
    results = last_call(shape, results)
    maps = list(shape.maps)
    images = [unflat(r, side) for r, side in zip(results[:6], maps + maps)]
    weights = [
        results[6].reshape(reduce_weight.shape),
        results[7].reshape(spatial_weight.shape),
        results[8].reshape(expand_weight.shape),
    ]
    return tuple(images + weights + [r.reshape(-1) for r in results[9:]])


def body(mesh, *arguments):
    inputs, reduce_weight = arguments[0], arguments[6]
    shape = Shape(
        mesh,
        [x.shape[1] for x in arguments[:3]],
        inputs.shape[0],
        inputs.shape[3],
        arguments[8].shape[0] * mesh.shape["narrow"],
    )
    if shape.fits():
        return kernel_body(shape, *arguments)
    return plain_body(*arguments)


def solution(mesh):
    rows = P("wide", None, None, None)
    blocks = P("wide", None, None, "narrow")
    weights = [P(None, "narrow"), P(None, None, None, "narrow"), P("narrow", None)]
    vectors = [P("narrow")] * 6
    return jax.shard_map(
        functools.partial(body, mesh),
        mesh=mesh,
        in_specs=tuple([rows] * 3 + [blocks] * 3 + weights + vectors),
        out_specs=tuple([blocks] * 6 + weights + vectors),
        check_vma=False,
    )
```

```python
import functools

import jax
import jax.numpy as jnp
from jax import lax
from jax.experimental import pallas as pl
from jax.experimental.pallas import tpu as pltpu
from jax.sharding import PartitionSpec as P

EPS = 1e-05
LAYOUT = ("NHWC", "HWIO", "NHWC")


def silu_slope(argument):
    logistic = jax.nn.sigmoid(argument)
    return logistic * (1.0 + argument * (1.0 - logistic))


def spatial(inputs, kernel):
    return lax.conv_general_dilated(
        inputs,
        kernel,
        (1, 1),
        ((1, 1), (1, 1)),
        dimension_numbers=LAYOUT,
        preferred_element_type=jnp.float32,
    )


def kernel_grad(inputs, gradient):
    height, breadth = (gradient.shape[1], gradient.shape[2])
    padded = jnp.pad(inputs, ((0, 0), (1, 1), (1, 1), (0, 0)))
    taps = []
    for vertical in range(3):
        for lateral in range(3):
            window = padded[:, vertical : vertical + height, lateral : lateral + breadth, :]
            taps.append(
                jnp.einsum("bhwc,bhwo->co", window, gradient, preferred_element_type=jnp.float32)
            )
    return jnp.stack(taps).reshape(3, 3, inputs.shape[3], gradient.shape[3])


def sums_forward(hidden):
    return (jnp.sum(hidden, axis=(0, 1, 2)), jnp.sum(hidden * hidden, axis=(0, 1, 2)))


def normed_of(hidden, sums, samples):
    average = sums[0] / samples
    inverse = lax.rsqrt(sums[1] / samples - average * average + EPS)
    return ((hidden - average) * inverse, inverse)


def sums_backward(upstream, normed):
    return (jnp.sum(upstream, axis=(0, 1, 2)), jnp.sum(upstream * normed, axis=(0, 1, 2)))


def hidden_grad(upstream, normed, inverse, gain, sums, samples):
    return (
        gain * inverse * (upstream - sums[0] / samples - normed * (sums[1] / samples))
    ).astype(jnp.bfloat16)


def each(function, *lists):
    return [function(*items) for items in zip(*lists)]


def columns(array, axis):
    own = array.shape[axis] // lax.axis_size("narrow")
    return lax.dynamic_slice_in_dim(array, lax.axis_index("narrow") * own, own, axis)


def dot(form, left, right):
    return jnp.einsum(form, left, right, preferred_element_type=jnp.float32)


def plain_body(
    input_five,
    input_seven,
    input_nine,
    upstream_five,
    upstream_seven,
    upstream_nine,
    reduce_weight,
    spatial_weight,
    expand_weight,
    gain_first,
    shift_first,
    gain_second,
    shift_second,
    gain_third,
    shift_third,
):
    inputs = [input_five, input_seven, input_nine]
    upstreams = [upstream_five, upstream_seven, upstream_nine]
    samples = [
        x.shape[0] * lax.axis_size("wide") * x.shape[1] * x.shape[2] for x in inputs
    ]
    whole_reduce = lax.all_gather(reduce_weight, "narrow", axis=1, tiled=True)
    whole_spatial = lax.all_gather(spatial_weight, "narrow", axis=3, tiled=True)
    own_expand = lax.all_to_all(expand_weight, "narrow", 1, 0, tiled=True)
    vectors = jnp.stack([gain_first, shift_first, gain_second, shift_second])
    gain1, shift1, gain2, shift2 = lax.all_gather(vectors, "narrow", axis=1, tiled=True)

    hidden1 = each(lambda x: dot("bhwc,cd->bhwd", x, whole_reduce), inputs)
    sums1 = lax.psum(each(sums_forward, hidden1), "wide")
    normed1, inverse1 = zip(*each(normed_of, hidden1, sums1, samples))
    pre1 = each(lambda n: n * gain1 + shift1, normed1)
    active1 = each(lambda p: jax.nn.silu(p).astype(jnp.bfloat16), pre1)

    hidden2 = each(lambda a: spatial(a, whole_spatial), active1)
    sums2 = lax.psum(each(sums_forward, hidden2), "wide")
    normed2, inverse2 = zip(*each(normed_of, hidden2, sums2, samples))
    pre2 = each(lambda n: n * gain2 + shift2, normed2)
    active2 = each(lambda p: jax.nn.silu(p).astype(jnp.bfloat16), pre2)

    hidden3 = each(lambda a: dot("bhwi,id->bhwd", a, own_expand), active2)
    sums3 = lax.psum(each(sums_forward, hidden3), "wide")
    normed3, inverse3 = zip(*each(normed_of, hidden3, sums3, samples))
    summed = each(
        lambda n, x: n * gain_third + shift_third + columns(x, 3).astype(jnp.float32),
        normed3,
        inputs,
    )
    results = each(lambda z: jax.nn.silu(z).astype(jnp.bfloat16), summed)
    grads_z = each(lambda u, z: u.astype(jnp.float32) * silu_slope(z), upstreams, summed)
    back3 = lax.psum(each(sums_backward, grads_z, normed3), "wide")
    grad3 = each(
        lambda e, n, r, s, m: hidden_grad(e, n, r, gain_third, s, m),
        grads_z,
        normed3,
        inverse3,
        back3,
        samples,
    )
    expand_grad = sum(each(lambda a, g: dot("bhwi,bhwd->id", a, g), active2, grad3))
    active_grad2 = each(
        lambda g: lax.psum(
            dot("bhwd,id->bhwi", g, own_expand).astype(jnp.bfloat16), "narrow"
        ).astype(jnp.float32),
        grad3,
    )
    grads_2 = each(lambda a, p: a * silu_slope(p), active_grad2, pre2)
    back2 = lax.psum(each(sums_backward, grads_2, normed2), "wide")
    grad2 = each(
        lambda e, n, r, s, m: hidden_grad(e, n, r, gain2, s, m),
        grads_2,
        normed2,
        inverse2,
        back2,
        samples,
    )
    spatial_grad = sum(each(lambda a, g: kernel_grad(a, columns(g, 3)), active1, grad2))
    flipped = jnp.transpose(whole_spatial[::-1, ::-1], (0, 1, 3, 2))
    grads_1 = each(lambda g, p: spatial(g, flipped) * silu_slope(p), grad2, pre1)
    back1 = lax.psum(each(sums_backward, grads_1, normed1), "wide")
    grad1 = each(
        lambda e, n, r, s, m: hidden_grad(e, n, r, gain1, s, m),
        grads_1,
        normed1,
        inverse1,
        back1,
        samples,
    )
    reduce_grad = sum(each(lambda x, g: dot("bhwc,bhwd->cd", x, columns(g, 3)), inputs, grad1))
    own_reduce = columns(whole_reduce, 0)
    in_grads = each(lambda g, e: dot("bhwd,cd->bhwc", g, own_reduce) + e, grad1, grads_z)

    low = [g.astype(jnp.bfloat16) for g in (reduce_grad, spatial_grad, expand_grad)]
    low[2] = lax.all_to_all(low[2], "narrow", 0, 1, tiled=True)
    totals = [g.astype(jnp.float32) for g in lax.psum(low, "wide")]

    def params(back, part):
        shift = sum(s[0] for s in back)
        gain = sum(s[1] for s in back)
        return [part(gain), part(shift)]

    def own(vector):
        return columns(vector, 0)

    small = params(back1, own) + params(back2, own) + params(back3, lambda v: v)
    return tuple(results + in_grads + totals + small)


class Shape:
    def __init__(self, mesh, maps, images, depth, inner):
        self.wide, self.narrow = mesh.shape["wide"], mesh.shape["narrow"]
        self.chips = self.wide // 2
        self.maps = maps
        self.images = images
        self.depth, self.inner = depth, inner
        self.own = inner // self.narrow
        self.block = depth // self.narrow
        self.rows = [images * side * side for side in maps]
        self.samples = [float(rows * self.wide) for rows in self.rows]

    def fits(self):
        return (
            self.narrow >= 4
            and self.narrow % 2 == 0
            and self.chips == 4
            and self.wide == 8
            and min(self.maps) >= 3
            and self.block == self.inner
            and self.own % 128 == 0
            and self.images % 16 == 0
            and self.own % (16 * self.wide) == 0
            and self.inner % 512 == 0
        )


def cuts(side, most):
    longest = max(1, most // side)
    number = -(-side // longest)
    edges = [side * n // number for n in range(number + 1)]
    return [(a, b - a) for a, b in zip(edges, edges[1:])]


class Pool:
    def __init__(self, ref):
        self.ref, self.used = ref, 0

    def take(self):
        assert self.used < SEMAPHORES
        self.used += 1
        return self.ref.at[self.used - 1]


MESH = pl.DeviceIdType.MESH
INVERSE, MINUS, SCALE, OFFSET, SHIFTSUM, GAINSUM, LINEAR, CONSTANT = range(8)
GIVEN, SPARE = 72, 80
SEMAPHORES = 600
VMEM_BYTES = 67_000_000
SLAB, CHUNK = 28, 9
WEIGHT_PARTS = 3


def dot_nn(left, right):
    return lax.dot_general(
        left, right, (((1,), (0,)), ((), ())), preferred_element_type=jnp.float32
    )


def dot_nt(left, right):
    return lax.dot_general(
        left, right, (((1,), (1,)), ((), ())), preferred_element_type=jnp.float32
    )


def dot_tn(left, right):
    return lax.dot_general(
        left, right, (((0,), (0,)), ((), ())), preferred_element_type=jnp.float32
    )


def logistic(argument):
    return 0.5 * jnp.tanh(0.5 * argument) + 0.5


class Step:
    def __init__(self, key, run, time, after, rank, hook=None):
        self.key, self.run, self.time = key, run, time
        self.after, self.rank, self.hook = after, rank, hook
        self.ready = 0.0


def arrange(steps, trace=None):
    named = {step.key: step for step in steps}
    done = {}
    now = 0.0
    order = []
    waiting = list(steps)
    while waiting:
        best = None
        for place, step in enumerate(waiting):
            if any(key not in done for key, _ in step.after):
                continue
            at = max([step.ready] + [done[key] + delay for key, delay in step.after])
            choice = (max(at, now), step.rank, place)
            if best is None or choice < best[0]:
                best = (choice, step)
        (start, _, _), step = best
        now = start + step.time
        done[step.key] = now
        waiting.remove(step)
        order.append(step)
        if trace is not None:
            trace.append((start, now, step.key))
        if step.hook is not None:
            step.hook(now, named)
    return order


def block_kernel(shape, *refs):
    wide, narrow, chips = shape.wide, shape.narrow, shape.chips
    inner, own, block, images = shape.inner, shape.own, shape.block, shape.images
    maps = shape.maps
    refs = list(refs)

    def take(count):
        taken = refs[:count]
        del refs[:count]
        return taken

    x_in, u_in = take(3), take(3)
    rw_in, sw_in, ew_in = take(3)
    vec_in = take(6)
    y_out, i_out = take(3), take(3)
    rg_out, sg_out, eg_out = take(3)
    vec_out = take(6)
    xb = take(3)
    rwf, swf, ewf = take(3)
    h1, h2, h3, dz = take(3), take(3), take(3), take(3)
    apad, dpad = take(3), take(3)
    rin, rx = take(3), take(3)
    sacc, eacc, racc = take(3)
    slow, elow, rlow = take(3)
    sr1, er1, rr1 = take(3)
    sr2, er2, rr2 = take(3)
    sfin, efin, rfin = take(3)
    epz, rpz = take(2)
    stat_s, stat_r, sums, vec, vec_all = take(5)
    vec_own, vec_made = take(6), take(6)
    pool = Pool(*take(1))

    w = lax.axis_index("wide")
    z = lax.axis_index("narrow")
    core = lax.rem(w, 2)
    chip = lax.div(w, 2)
    sibling = chip * 2 + (1 - core)
    half = narrow // 2
    inward = jnp.where(z < half, z + 1, z - 1)
    outward = jnp.where(z < half, z - 1, z + 1)
    center = jnp.logical_or(z == half - 1, z == half)
    end = jnp.logical_or(z == 0, z == narrow - 1)
    k_own, k_a2, k_dh, k_p = [lax.rem(z + k, narrow) for k in range(4)]
    finish = []
    arrivals = []

    def once(wait):
        made = []

        def noted():
            if not made:
                made.append(True)
                wait()

        arrivals.append(noted)
        return noted

    def remote(source, target, device):
        send, recv = pool.take(), pool.take()

        def make():
            return pltpu.make_async_remote_copy(
                src_ref=source(),
                dst_ref=target(),
                send_sem=send,
                recv_sem=recv,
                device_id=device,
                device_id_type=MESH,
            )

        make().start()
        finish.append(lambda: make().wait_send())
        return once(lambda: make().wait_recv())

    def local(source, target):
        semaphore = pool.take()

        def make():
            return pltpu.make_async_copy(source(), target(), semaphore)

        make().start()
        return once(lambda: make().wait())

    def span(start, size, unit):
        return pl.ds(pl.multiple_of(start * unit, unit), size)

    def rows_of(g, cut):
        return pl.ds(cut[0] * maps[g] * images, cut[1] * maps[g] * images)

    slabs = [cuts(side, SLAB) for side in maps]
    chunks = [cuts(side, CHUNK) for side in maps]

    def lines(g, cut, function):
        size = maps[g] * images
        if cut[1] == 1:
            function(cut[0], pl.ds(cut[0] * size, size))
        else:
            pl.loop(cut[0], cut[0] + cut[1])(
                lambda y: function(y, pl.ds(pl.multiple_of(y * size, 16), size))
            )

    chip_x = chip + 1 - 2 * lax.rem(chip, 2)
    chip_y = lax.rem(chip + 2, chips)
    chip_far = lax.rem(chip_x + 2, chips)
    origins = [lax.rem(z + narrow - k, narrow) for k in range(1, narrow)]

    class Gather:
        def __init__(self, source, target):
            self.source, self.target = source, target
            self.from_x, self.from_y, self.far, self.crossed = [], [], [], []

        def first(self):
            self.arrived = [
                remote(
                    lambda peer=peer: self.source(w, peer),
                    lambda: self.target(w, z),
                    (w, peer),
                )
                for peer in [lax.rem(z + k, narrow) for k in range(1, narrow)]
            ]

        def send(self, holder, origin, part, device):
            def piece():
                return self.target(holder * 2 + core, origin, part)

            return remote(piece, piece, (device, z))

        def spread(self):
            for origin, wait in zip(origins, self.arrived):
                wait()
                self.from_x.append(self.send(chip, origin, None, chip_x * 2 + core))
                self.from_y.append(self.send(chip, origin, None, chip_y * 2 + core))
            for origin in origins:
                self.crossed.append(self.send(chip, origin, None, sibling))

        def relay(self):
            for origin, got_x, got_y in zip(origins, self.from_x, self.from_y):
                got_x()
                along_y = self.send(chip_x, origin, 0, chip_y * 2 + core)
                got_y()
                along_x = self.send(chip_y, origin, 1, chip_x * 2 + core)
                self.far.append((along_y, along_x))
            for origin in origins:
                self.crossed.append(self.send(chip_x, origin, None, sibling))
                self.crossed.append(self.send(chip_y, origin, None, sibling))

        def cross(self):
            for origin, waits in zip(origins, self.far):
                for wait in waits:
                    wait()
                self.crossed.append(self.send(chip_far, origin, None, sibling))

        def ready(self):
            for wait in self.crossed:
                wait()

    rw_piece, sw_piece, ew_piece = shape.depth // wide, inner // wide, own // wide
    part = 9 // WEIGHT_PARTS

    def half_of(h, size, unit, half):
        if half is None:
            return span(h, size, size)
        return pl.ds(pl.multiple_of(h * size + half * (size // 2), unit), size // 2)

    def sw_item(n):
        taps = pl.ds(n * part, part)
        return Gather(
            lambda h, peer: sw_in.at[taps, span(h, sw_piece, sw_piece), :],
            lambda h, o, half=None: swf.at[taps, half_of(h, sw_piece, 16, half), span(o, own, own)],
        )

    gathers = (
        [
            Gather(
                lambda h, peer: rw_in.at[span(h, rw_piece, rw_piece), :],
                lambda h, o, half=None: rwf.at[half_of(h, rw_piece, 16, half), span(o, own, own)],
            )
        ]
        + [sw_item(n) for n in range(WEIGHT_PARTS)]
        + [
            Gather(
                lambda h, peer: ew_in.at[span(h, ew_piece, ew_piece), span(peer, block, block)],
                lambda h, o, half=None: ewf.at[
                    pl.ds(pl.multiple_of(o * own + h * ew_piece, 16), ew_piece),
                    pl.ds(0, block) if half is None else pl.ds(half * (block // 2), block // 2),
                ],
            )
        ]
    )
    x_wait = [[None] * narrow for _ in range(3)]
    u_wait, y_wait = [None] * 3, [None] * 3
    own_waits, vec_waits = [], []

    def slot(kind, level, g):
        return (kind * 3 + level) * 3 + g

    def put(place, value):
        vec[place : place + 1, :] = value

    def get(place):
        return vec[place : place + 1, :]

    def begin():
        barrier = pltpu.get_barrier_semaphore()
        for k in range(1, wide):
            pl.semaphore_signal(
                barrier, inc=1, device_id=(lax.rem(w + k, wide), z), device_id_type=MESH
            )
        for k in range(1, narrow):
            pl.semaphore_signal(
                barrier, inc=1, device_id=(w, lax.rem(z + k, narrow)), device_id_type=MESH
            )
        got = [local(lambda a=a: a, lambda b=b: b) for a, b in zip(vec_in, vec_own)]
        for source, target in (
            (lambda: rw_in, lambda: rwf.at[:, span(z, own, own)]),
            (lambda: sw_in, lambda: swf.at[:, :, span(z, own, own)]),
            (lambda: ew_in.at[:, span(z, block, block)], lambda: ewf.at[span(z, own, own), :]),
        ):
            own_waits.append(local(source, target))
        for g in range(3):
            for k in range(narrow):
                x_wait[g][k] = local(
                    lambda g=g, k=k: x_in[g].at[:, pl.ds(k * block, block)],
                    lambda g=g, k=k: xb[g].at[k],
                )
        for wait in got:
            wait()
        vec_all[z] = jnp.concatenate(
            [v[...] for v in vec_own[:4]] + [jnp.zeros((4, own), jnp.float32)], axis=0
        )
        pl.semaphore_wait(barrier, wide - 1 + narrow - 1)
        for k in range(1, narrow):
            vec_waits.append(
                remote(lambda: vec_all.at[z], lambda: vec_all.at[z], (w, lax.rem(z + k, narrow)))
            )
        for item in gathers:
            item.first()

    def pads():
        for g in range(3):
            side = maps[g]
            for pad in (apad[g], dpad[g]):
                pad[0] = jnp.zeros((side + 2, images, inner), jnp.bfloat16)
                pad[side + 1] = jnp.zeros((side + 2, images, inner), jnp.bfloat16)
                for edge in (0, side + 1):
                    pad[1 : side + 1, edge] = jnp.zeros((side, images, inner), jnp.bfloat16)
        for acc in (sacc, eacc, racc):

            def clear(a, acc=acc):
                acc[a] = jnp.zeros(acc.shape[1:], jnp.float32)

            pl.loop(0, acc.shape[0])(clear)

    def vectors():
        for wait in vec_waits:
            wait()
        for row in range(4):
            put(
                GIVEN + row,
                jnp.concatenate([vec_all[k, row : row + 1, :] for k in range(narrow)], axis=1),
            )
        for row in (4, 5):
            put(GIVEN + row, vec_own[row][...])

    tiles = inner // 128
    stat_sems, stat_arrived = {}, {}

    def stats_all(e):
        send, recv = stat_sems[e]
        return pltpu.make_async_remote_copy(
            src_ref=stat_r.at[e, pl.ds(0, wide - 1)],
            dst_ref=stat_r.at[e, pl.ds(0, wide - 1)],
            send_sem=send,
            recv_sem=recv,
            device_id=(sibling, z),
            device_id_type=MESH,
        )

    def stats_wait(e):
        stat_arrived[e]()
        total = stat_r[e, 0]
        for k in range(1, wide):
            total = total + stat_r[e, k]
        return [
            jnp.concatenate(
                [total[t * tiles + b : t * tiles + b + 1, :] for b in range(tiles)], axis=1
            )
            for t in range(2)
        ]

    class Sums:
        def __init__(self, e):
            self.row = 2 * e
            self.e = e

        def clear(self):
            sums[self.row : self.row + 2, :] = jnp.zeros((2, inner), jnp.float32)

        def add(self, first, second):
            sums[self.row : self.row + 1, :] += jnp.sum(first, axis=0, keepdims=True)
            sums[self.row + 1 : self.row + 2, :] += jnp.sum(second, axis=0, keepdims=True)

    totals_of = {e: Sums(e) for e in range(18)}

    def send_sums(e):
        row = totals_of[e].row
        for t in range(2):
            for b in range(tiles):
                stat_s[e, t * tiles + b : t * tiles + b + 1, :] = sums[
                    row + t : row + t + 1, b * 128 : (b + 1) * 128
                ]
        stat_r[e, w] = stat_s[e]
        send, recv = pool.take(), pool.take()
        stat_sems[e] = (send, recv)
        stat_arrived[e] = once(lambda: stats_all(e).wait_recv())
        finish.append(lambda: stats_all(e).wait_send())

        def one(k, carry):
            pltpu.make_async_remote_copy(
                src_ref=stat_s.at[e],
                dst_ref=stat_r.at[e, w],
                send_sem=send,
                recv_sem=recv,
                device_id=(lax.rem(w + k, wide), z),
                device_id_type=MESH,
            ).start()
            return carry

        lax.fori_loop(1, wide, one, 0)

    def norm_vectors(g, level):
        first, second = stats_wait(g * 6 + level)
        mean = first / shape.samples[g]
        inverse = lax.rsqrt(second / shape.samples[g] - mean * mean + EPS)
        scale = inverse * get(GIVEN + 2 * level)
        put(slot(INVERSE, level, g), inverse)
        put(slot(MINUS, level, g), -mean * inverse)
        put(slot(SCALE, level, g), scale)
        put(slot(OFFSET, level, g), get(GIVEN + 2 * level + 1) - mean * scale)

    def back_vectors(g, level):
        shift_sum, gain_sum = stats_wait(g * 6 + 5 - level)
        put(slot(SHIFTSUM, level, g), shift_sum)
        put(slot(GAINSUM, level, g), gain_sum)
        scale = get(slot(SCALE, level, g))
        c1 = scale * (gain_sum / shape.samples[g])
        put(slot(LINEAR, level, g), -get(slot(INVERSE, level, g)) * c1)
        put(slot(CONSTANT, level, g), -get(slot(MINUS, level, g)) * c1 - scale * (shift_sum / shape.samples[g]))

    def f1(g, cut):
        run = totals_of[g * 6]
        if cut[0] == 0:
            for wait in x_wait[g]:
                wait()
            run.clear()
        rows = rows_of(g, cut)
        left = jnp.concatenate([xb[g][k, rows, :] for k in range(narrow)], axis=1)
        result = dot_nn(left, rwf[...])
        h1[g][rows, :] = result
        run.add(result, result * result)

    def f1_end(g):
        send_sums(g * 6)
        u_wait[g] = local(lambda: u_in[g], lambda: xb[g].at[k_dh])

    def a1(g):
        scale, offset = get(slot(SCALE, 0, g)), get(slot(OFFSET, 0, g))
        side = maps[g]

        def one(y, rows):
            pre = h1[g][rows, :] * scale + offset
            value = (pre * logistic(pre)).astype(jnp.bfloat16)
            apad[g][y + 1, pl.ds(1, side)] = value.reshape(side, images, inner)

        lines(g, (0, side), one)

    def windows(pad, g, cut, lines_of_taps):
        side = maps[g]
        return jnp.concatenate(
            [
                pad[cut[0] + i : cut[0] + i + cut[1], j : j + side].reshape(
                    cut[1] * side * images, inner
                )
                for i in lines_of_taps
                for j in range(3)
            ],
            axis=1,
        )

    def f2(g, n, cut):
        run = totals_of[g * 6 + 1]
        rows = rows_of(g, cut)
        result = dot_nn(windows(apad[g], g, cut, (n,)), swf[3 * n : 3 * n + 3].reshape(-1, inner))
        if n > 0:
            result = result + h2[g][rows, :]
        h2[g][rows, :] = result
        if n == 2:
            if cut[0] == 0:
                run.clear()
            run.add(result, result * result)

    def a2(g):
        scale, offset = get(slot(SCALE, 1, g)), get(slot(OFFSET, 1, g))

        def one(y, rows):
            pre = h2[g][rows, :] * scale + offset
            xb[g][k_a2, rows, :] = (pre * logistic(pre)).astype(jnp.bfloat16)

        lines(g, (0, maps[g]), one)

    def f3(g):
        run = totals_of[g * 6 + 2]
        run.clear()
        for cut in slabs[g]:
            rows = rows_of(g, cut)
            result = dot_nn(xb[g][k_a2, rows, :], ewf[...])
            h3[g][rows, :] = result
            run.add(result, result * result)

    def a3(g):
        run = totals_of[g * 6 + 3]
        run.clear()
        scale, offset = get(slot(SCALE, 2, g)), get(slot(OFFSET, 2, g))
        inverse, minus = get(slot(INVERSE, 2, g)), get(slot(MINUS, 2, g))

        def one(y, rows):
            hidden = h3[g][rows, :]
            total = hidden * scale + offset + xb[g][k_own, rows, :].astype(jnp.float32)
            sig = logistic(total)
            xb[g][k_p, rows, :] = (total * sig).astype(jnp.bfloat16)
            slope = sig * (1.0 + total * (1.0 - sig))
            grad = xb[g][k_dh, rows, :].astype(jnp.float32) * slope
            dz[g][rows, :] = grad
            run.add(grad, grad * (hidden * inverse + minus))

        lines(g, (0, maps[g]), one)

    def a3_end(g):
        send_sums(g * 6 + 3)
        y_wait[g] = local(lambda: xb[g].at[k_p], lambda: y_out[g])

    def b3(g, cut):
        scale, k1, k0 = get(slot(SCALE, 2, g)), get(slot(LINEAR, 2, g)), get(slot(CONSTANT, 2, g))
        rows = rows_of(g, cut)
        value = dz[g][rows, :] * scale + h3[g][rows, :] * k1 + k0
        low = value.astype(jnp.bfloat16)
        xb[g][k_dh, rows, :] = low
        xb[g][k_p, rows, :] = dot_nt(low, ewf[...]).astype(jnp.bfloat16)
        c = chunks[g].index(cut)
        reductions[g, c] = copies = Reduction(g, c)
        pl.when(end)(lambda: copies.to_inner().start())

    def eg(g):
        result = dot_tn(xb[g][k_a2], xb[g][k_dh])
        for k in range(narrow):
            piece = result[k * own : (k + 1) * own, :].reshape(eacc.shape[1:])
            eacc[k] += piece

    reductions = {}

    class Reduction:
        def __init__(self, g, c):
            self.g, self.rows = g, rows_of(g, chunks[g][c])
            self.sems = [pool.take() for _ in range(5)]
            self.inwards = once(self.add_outer)
            self.across = once(self.add_other)
            self.home = once(lambda: pl.when(end)(lambda: self.to_center().wait_recv()))
            finish.append(self.sent)

        def copy(self, source, target, send, recv, device):
            return pltpu.make_async_remote_copy(
                src_ref=source.at[self.rows, :],
                dst_ref=target.at[self.rows, :],
                send_sem=self.sems[send],
                recv_sem=self.sems[recv],
                device_id=(w, device),
                device_id_type=MESH,
            )

        def to_inner(self):
            return self.copy(xb[self.g].at[k_p], rin[self.g], 0, 1, inward)

        def to_center(self):
            return self.copy(xb[self.g].at[k_p], rx[self.g], 2, 3, inward)

        def to_outer(self):
            return self.copy(rx[self.g], rx[self.g], 4, 3, outward)

        def add_outer(self):
            g, rows = self.g, self.rows

            @pl.when(jnp.logical_not(end))
            def _():
                self.to_inner().wait_recv()
                xb[g][k_p, rows, :] = (
                    xb[g][k_p, rows, :].astype(jnp.float32) + rin[g][rows, :].astype(jnp.float32)
                ).astype(jnp.bfloat16)
                pl.when(center)(lambda: self.to_center().start())
                pl.when(jnp.logical_not(center))(lambda: self.to_inner().start())

        def add_other(self):
            g, rows = self.g, self.rows

            @pl.when(jnp.logical_not(end))
            def _():
                self.to_center().wait_recv()

                @pl.when(center)
                def _():
                    rx[g][rows, :] = (
                        rx[g][rows, :].astype(jnp.float32)
                        + xb[g][k_p, rows, :].astype(jnp.float32)
                    ).astype(jnp.bfloat16)

                self.to_outer().start()

        def sent(self):
            pl.when(center)(lambda: self.to_center().wait_send())
            pl.when(jnp.logical_not(center))(lambda: self.to_inner().wait_send())
            pl.when(jnp.logical_not(end))(lambda: self.to_outer().wait_send())

    def za(g, c):
        reductions[g, c].inwards()

    def zb(g, c):
        reductions[g, c].across()

    def g2(g, c):
        run = totals_of[g * 6 + 4]
        if c == 0:
            run.clear()
        reductions[g, c].home()
        scale, offset = get(slot(SCALE, 1, g)), get(slot(OFFSET, 1, g))
        inverse, minus = get(slot(INVERSE, 1, g)), get(slot(MINUS, 1, g))

        def one(y, rows):
            hidden = h2[g][rows, :]
            pre = hidden * scale + offset
            sig = logistic(pre)
            grad = rx[g][rows, :].astype(jnp.float32) * (sig * (1.0 + pre * (1.0 - sig)))
            h3[g][rows, :] = grad
            run.add(grad, grad * (hidden * inverse + minus))

        lines(g, chunks[g][c], one)

    def d2(g):
        scale, k1, k0 = get(slot(SCALE, 1, g)), get(slot(LINEAR, 1, g)), get(slot(CONSTANT, 1, g))
        side = maps[g]

        def one(y, rows):
            value = h3[g][rows, :] * scale + h2[g][rows, :] * k1 + k0
            dpad[g][y + 1, pl.ds(1, side)] = value.astype(jnp.bfloat16).reshape(side, images, inner)

        lines(g, (0, side), one)

    def sg(g):
        side = maps[g]
        left = apad[g][1 : side + 1, 1 : side + 1].reshape(shape.rows[g], inner)
        right = jnp.concatenate(
            [
                dpad[g][2 - i : 2 - i + side, 2 - j : 2 - j + side, :, span(z, own, own)].reshape(
                    shape.rows[g], own
                )
                for i in range(3)
                for j in range(3)
            ],
            axis=1,
        )
        result = dot_tn(left, right)
        for t in range(9):
            piece = result[:, t * own : (t + 1) * own].reshape(sacc.shape[1:])
            sacc[t] += piece

    def f1b(g, cut):
        run = totals_of[g * 6 + 5]
        if cut[0] == 0:
            run.clear()
        rows = rows_of(g, cut)
        left = windows(dpad[g], g, cut, range(3))
        right = jnp.concatenate([swf[8 - t] for t in range(9)], axis=1)
        h2[g][rows, :] = dot_nt(left, right)

    def g1(g, cut):
        run = totals_of[g * 6 + 5]
        scale, offset = get(slot(SCALE, 0, g)), get(slot(OFFSET, 0, g))
        inverse, minus = get(slot(INVERSE, 0, g)), get(slot(MINUS, 0, g))

        def one(y, rows):
            hidden = h1[g][rows, :]
            pre = hidden * scale + offset
            sig = logistic(pre)
            grad = h2[g][rows, :] * (sig * (1.0 + pre * (1.0 - sig)))
            h2[g][rows, :] = grad
            run.add(grad, grad * (hidden * inverse + minus))

        lines(g, cut, one)

    def d1(g):
        scale, k1, k0 = get(slot(SCALE, 0, g)), get(slot(LINEAR, 0, g)), get(slot(CONSTANT, 0, g))

        def one(y, rows):
            value = h2[g][rows, :] * scale + h1[g][rows, :] * k1 + k0
            xb[g][k_dh, rows, :] = value.astype(jnp.bfloat16)

        lines(g, (0, maps[g]), one)

    def ig(g):
        for cut in slabs[g]:
            rows = rows_of(g, cut)
            right = rwf[span(z, block, block), :]
            h3[g][rows, :] = dot_nt(xb[g][k_dh, rows, :], right) + dz[g][rows, :]
        finish.append(local(lambda: h3[g], lambda: i_out[g]))

    def rg(g):
        result = dot_tn(xb[g][k_own], xb[g][k_dh])
        for k in range(narrow):
            piece = result[:, k * own : (k + 1) * own].reshape(racc.shape[1:])
            racc[k] += piece

    class Total:
        def __init__(self, acc, low, first, second, final, piece, out):
            self.acc, self.low, self.first, self.second = acc, low, first, second
            self.final, self.piece, self.out = final, piece, out
            self.count = acc.shape[0]

        def one(self):
            def cast(a):
                self.low[a] = self.acc[a, :, 1 - core].astype(jnp.bfloat16)

            pl.loop(0, self.count)(cast)
            self.got1 = remote(lambda: self.low, lambda: self.first, (sibling, z))

        def two(self):
            self.got1()

            def add(a):
                self.first[a] = (
                    self.first[a].astype(jnp.float32) + self.acc[a, :, core]
                ).astype(jnp.bfloat16)

            pl.loop(0, self.count)(add)
            self.got2 = []
            for j in range(1, chips):
                peer = lax.rem(chip + j, chips)
                self.got2.append(
                    remote(
                        lambda peer=peer: self.first.at[:, peer],
                        lambda: self.second.at[chip],
                        (peer * 2 + core, z),
                    )
                )

        def three(self):
            for wait in self.got2:
                wait()
            self.second[chip] = self.first[:, chip]
            target = self.final.at[:, chip, core] if self.piece is None else self.piece

            def add(a):
                total = self.second[0, a].astype(jnp.float32)
                for k in range(1, chips):
                    total = total + self.second[k, a].astype(jnp.float32)
                target[a] = total.astype(jnp.bfloat16)

            pl.loop(0, self.count)(add)
            if self.piece is None:
                self.send_pieces()
                return
            self.got3 = []
            for k in range(1, narrow):
                peer = lax.rem(z + k, narrow)
                self.got3.append(
                    remote(
                        lambda peer=peer: self.piece.at[peer],
                        lambda: self.final.at[z, chip, core],
                        (w, peer),
                    )
                )
            self.final[z, chip, core] = self.piece[z]

        def exchange(self):
            for wait in self.got3:
                wait()
            self.send_pieces()

        def send_pieces(self):
            self.got4, self.got5 = [], []

            def piece():
                return self.final.at[:, chip, core]

            for j in range(1, chips):
                peer = lax.rem(chip + j, chips)
                self.got4.append((j, remote(piece, piece, (peer * 2 + core, z))))
            self.got5.append(remote(piece, piece, (sibling, z)))

        def four(self):
            for j, arrived in self.got4:
                arrived()
                holder = lax.rem(chip + chips - j, chips)

                def piece(holder=holder):
                    return self.final.at[:, holder, core]

                self.got5.append(remote(piece, piece, (sibling, z)))

        def five(self):
            for wait in self.got5:
                wait()
            finish.append(local(lambda: self.final, lambda: self.out))

    stotal = Total(sacc, slow, sr1, sr2, sfin, None, sg_out)
    etotal = Total(eacc, elow, er1, er2, efin, epz, eg_out)
    rtotal = Total(racc, rlow, rr1, rr2, rfin, rpz, rg_out)

    def params():
        for place in range(6):
            level, kind = place // 2, GAINSUM if place % 2 == 0 else SHIFTSUM
            total = sum(get(slot(kind, level, g)) for g in range(3))
            if level == 2:
                vec_made[place][...] = total
            else:
                put(SPARE, total)
                vec_made[place][...] = vec[SPARE : SPARE + 1, span(z, own, own)]
            finish.append(
                local(lambda place=place: vec_made[place], lambda place=place: vec_out[place])
            )

    steps = []
    order = T.order

    def add(key, run, time, after, rank, hook=None):
        steps.append(Step(key, run, time, after, rank, hook))

    START, CLEAR, VECTORS = (begin,), (pads,), (vectors,)
    add(START, begin, 5.0, [], 0)
    add(CLEAR, pads, 1.0, [(START, 0.0)], 1)
    add(VECTORS, vectors, 0.2, [(START, 5.0)], 2)

    def spread(n):
        gathers[n].spread()

    def relay(n):
        gathers[n].relay()

    def cross(n):
        gathers[n].cross()

    def ready(n):
        if n == 0:
            for wait in own_waits:
                wait()
        gathers[n].ready()

    for n in range(len(gathers)):
        wait = T.xy[n]
        for f, time, after in (
            (spread, 0.2, [(START, T.z[n])]),
            (relay, 0.2, [((spread, n), wait)]),
            (cross, 0.1, [((relay, n), wait * 0.7)]),
            (ready, 0.1, [((cross, n), 1.5)]),
        ):
            if n > 0 and f is not ready:
                after = after + [((f, n - 1), T.xy[n] * 0.8 if f is relay else 0.0)]
            add((f, n), functools.partial(f, n), time, after, 0.0 if n < 4 else 0.1)

    link = {za: 0.0, zb: 0.0, g2: 0.0}

    def transfer(key, size):
        def hook(now, named):
            link[key[0]] = max(link[key[0]], now) + size * T.hop
            named[key].ready = link[key[0]] + T.lat

        return hook

    class Do:
        def __init__(self, g):
            self.g = g

        def f1(self, s):
            f1(self.g, slabs[self.g][s])
            if s == len(slabs[self.g]) - 1:
                f1_end(self.g)

        def a1(self):
            norm_vectors(self.g, 0)
            a1(self.g)

        def f2(self, n, s):
            f2(self.g, n, slabs[self.g][s])
            if n == 2 and s == len(slabs[self.g]) - 1:
                send_sums(self.g * 6 + 1)

        def a2(self):
            norm_vectors(self.g, 1)
            a2(self.g)
            f3(self.g)
            send_sums(self.g * 6 + 2)

        def a3(self):
            norm_vectors(self.g, 2)
            u_wait[self.g]()
            a3(self.g)
            a3_end(self.g)

        def b3(self, c):
            if c == 0:
                back_vectors(self.g, 2)
                y_wait[self.g]()
            b3(self.g, chunks[self.g][c])

        def g2(self, c):
            g2(self.g, c)
            if c == len(chunks[self.g]) - 1:
                send_sums(self.g * 6 + 4)

        def d2(self):
            back_vectors(self.g, 1)
            d2(self.g)

        def f1b(self, s):
            f1b(self.g, slabs[self.g][s])
            g1(self.g, slabs[self.g][s])
            if s == len(slabs[self.g]) - 1:
                send_sums(self.g * 6 + 5)

        def d1(self):
            back_vectors(self.g, 0)
            d1(self.g)

    before = None
    for turn, g in enumerate(order):
        do = Do(g)
        size = [shape.rows[g] * n / maps[g] for _, n in chunks[g]]
        scale = shape.rows[g] / 1000.0
        per, last = len(slabs[g]), len(chunks[g]) - 1
        early, late = 2 + turn * 0.3, 4 + turn * 0.3
        for s in range(per):
            after = [((ready, 0), 0.0)] if s == 0 else [((f1, g, s - 1), 0.0)]
            add((f1, g, s), functools.partial(do.f1, s), T.f1 * scale / per, after, early)
        after = [((f1, g, per - 1), T.stat0), (VECTORS, 0.0), (CLEAR, 0.0)]
        add((a1, g), do.a1, T.a1 * scale + 0.2, after, early)
        behind = (a1, g)
        for n in range(3):
            for s in range(per):
                after = [(behind, 0.0), ((ready, n + 1), 0.0)]
                behind = (f2, g, n, s)
                add(behind, functools.partial(do.f2, n, s), T.f2 * scale / per / 3, after, early - 0.1 * n)
        after = [(behind, T.stat), ((ready, 4), 0.0)]
        add((a2, g), do.a2, T.a2 * scale + 0.2, after, early - 0.5)
        add((a3, g), do.a3, T.a3 * scale + 0.2, [((a2, g), T.stat)], early - 0.5)
        for c in range(last + 1):
            after = [((a3, g), T.stat)] if c == 0 else [((b3, g, c - 1), 0.0)]
            if c == 0 and before is not None:
                after.append((before, 0.0))
            add((b3, g, c), functools.partial(do.b3, c), T.b3 * size[c] / 1000.0, after, 1 + turn * 0.3, transfer((za, g, c), size[c]))
            after = [((b3, g, c), 0.0)] + ([((za, g, c - 1), 0.0)] if c else [])
            add((za, g, c), functools.partial(za, g, c), T.za, after, 0, transfer((zb, g, c), size[c]))
            after = [((za, g, c), 0.0)] + ([((zb, g, c - 1), 0.0)] if c else [])
            add((zb, g, c), functools.partial(zb, g, c), T.za, after, 0, transfer((g2, g, c), size[c]))
            after = [((zb, g, c), 0.0)] + ([((g2, g, c - 1), 0.0)] if c else [])
            add((g2, g, c), functools.partial(do.g2, c), T.g2 * size[c] / 1000.0, after, late - 1.5)
        before = (b3, g, last)
        add((d2, g), do.d2, T.d2 * scale + 0.2, [((g2, g, last), T.stat)], late - 1)
        add((eg, g), functools.partial(eg, g), T.eg * scale, [(before, 0.0)], 6)
        final = turn == len(order) - 1
        add((sg, g), functools.partial(sg, g), T.sg * scale, [((d2, g), 0.0)], 3.0 if final else late - T.sg_rank if turn else 5)
        for s in range(per):
            after = [((d2, g), 0.0)] if s == 0 else [((f1b, g, s - 1), 0.0)]
            if turn == len(order) - 2 and s == per - 1:
                after.append(((g2, order[-1], len(chunks[order[-1]]) - 1), 0.0))
            add((f1b, g, s), functools.partial(do.f1b, s), T.f1b * scale / per, after, late - 0.4)
        after = [((f1b, g, per - 1), T.stat_late), ((eg, g), 0.0)]
        add((d1, g), do.d1, T.d1 * scale + 0.2, after, late - 0.5)
        add((rg, g), functools.partial(rg, g), T.rg * scale, [((d1, g), 0.0)], late - 0.5)
        add((ig, g), functools.partial(ig, g), T.ig * scale, [((d1, g), 0.0)], 8)
    for total, source, xfer in ((etotal, eg, 3.0), (stotal, sg, 6.5), (rtotal, rg, 3.5)):
        add((total, 1), total.one, 0.3, [((source, g), 0.0) for g in range(3)], 1)
        add((total, 2), total.two, 0.3, [((total, 1), 2.5)], 1)
        after = [((total, 2), xfer + 2)]
        if total is etotal:
            after.append(((zb, order[-1], len(chunks[order[-1]]) - 1), 0.0))
        add((total, 3), total.three, 0.4, after, 1)
        if total.piece is not None:
            add((total, 4), total.exchange, 0.2, [((total, 3), 5.0 if total is etotal else 2.5)], 1)
        after = [((total, 3 if total.piece is None else 4), xfer + 2)]
        add((total, 5), total.four, 0.2, after, 1)
        add((total, 6), total.five, 0.1, [((total, 5), 2.5)], 7)
    add((params,), params, 0.3, [((d1, g), 0.0) for g in range(3)], 7)
    for step in arrange(steps, TRACE)[:PLAN_END]:
        step.run()
    for wait in arrivals:
        wait()
    for wait in finish:
        wait()


PLAN_END = None
TRACE = None


class T:
    order = (2, 1, 0)
    z = (8.0, 14.5, 18.5, 23.0, 24.0)
    xy = (5.0, 5.0, 5.0, 5.0, 2.0)
    stat0, stat, stat_late = 4.5, 2.8, 5.0
    f1, a1, f2, a2, a3, b3 = 2.5, 0.7, 5.4, 1.3, 2.0, 2.1
    hop, lat, za = 0.022, 2.2, 0.1
    g2, d2, eg, sg, f1b, d1, rg, ig = 1.4, 0.4, 0.7, 2.0, 6.3, 0.4, 0.7, 0.7
    sg_rank = 0.45


def kernel_call(shape, args):
    inner, own, block, depth = shape.inner, shape.own, shape.block, shape.depth
    wide, narrow, chips, images = shape.wide, shape.narrow, shape.chips, shape.images
    bf16, f32 = jnp.bfloat16, jnp.float32

    def struct(dims, kind):
        return jax.ShapeDtypeStruct(dims, kind)

    spread = [
        (9, chips, 2, inner // wide, own),
        (narrow, chips, 2, own // wide, block),
        (narrow, chips, 2, block // wide, own),
    ]
    outs = (
        [struct((rows, block), bf16) for rows in shape.rows]
        + [struct((rows, block), f32) for rows in shape.rows]
        + [struct(spread[2], bf16), struct(spread[0], bf16), struct(spread[1], bf16)]
        + [struct((1, own), f32)] * 4
        + [struct((1, block), f32)] * 2
    )
    anywhere = pl.BlockSpec(memory_space=pl.ANY)

    def each_rows(columns, kind):
        return [pltpu.VMEM((rows, columns), kind) for rows in shape.rows]

    def padded():
        return [pltpu.VMEM((side + 2, side + 2, images, inner), bf16) for side in shape.maps]

    scratch = (
        [pltpu.VMEM((narrow, rows, block), bf16) for rows in shape.rows]
        + [
            pltpu.VMEM((depth, inner), bf16),
            pltpu.VMEM((9, inner, inner), bf16),
            pltpu.VMEM((inner, block), bf16),
        ]
        + each_rows(inner, f32)
        + each_rows(inner, f32)
        + each_rows(block, f32)
        + each_rows(block, f32)
        + padded()
        + padded()
        + each_rows(inner, bf16)
        + each_rows(inner, bf16)
        + [pltpu.VMEM(dims, f32) for dims in spread]
        + [pltpu.VMEM((a, c, b, lanes), bf16) for a, c, _, b, lanes in spread]
        + [pltpu.VMEM((a, c, b, lanes), bf16) for a, c, _, b, lanes in spread]
        + [pltpu.VMEM((c, a, b, lanes), bf16) for a, c, _, b, lanes in spread]
        + [pltpu.VMEM(dims, bf16) for dims in spread]
        + [pltpu.VMEM((a, b, lanes), bf16) for a, _, _, b, lanes in spread[1:]]
        + [
            pltpu.VMEM((18, 2 * inner // 128, 128), f32),
            pltpu.VMEM((18, wide, 2 * inner // 128, 128), f32),
            pltpu.VMEM((40, inner), f32),
            pltpu.VMEM((96, inner), f32),
            pltpu.VMEM((narrow, 8, own), f32),
        ]
        + ([pltpu.VMEM((1, own), f32)] * 4 + [pltpu.VMEM((1, block), f32)] * 2) * 2
        + [pltpu.SemaphoreType.DMA((SEMAPHORES,))]
    )
    return pl.pallas_call(
        functools.partial(block_kernel, shape),
        out_shape=outs,
        in_specs=[anywhere] * 15,
        out_specs=[anywhere] * 15,
        scratch_shapes=scratch,
        compiler_params=pltpu.CompilerParams(
            collective_id=0, has_side_effects=True, vmem_limit_bytes=VMEM_BYTES
        ),
        name="bottleneck",
    )(*args)


def last_kernel(shape, *refs):
    narrow, block = shape.narrow, shape.block
    source, target, held, high, sems = refs[:15], refs[15:30], refs[30:45], refs[45:48], refs[48]
    pool = Pool(sems)
    finish = []

    def copy(source, target):
        semaphore = pool.take()

        def make():
            return pltpu.make_async_copy(source, target, semaphore)

        make().start()
        return lambda: make().wait()

    places = [6, 5, 8, 2, 4, 7, 3, 1, 0] + list(range(9, 15))
    got = {place: copy(source[place], held[place]) for place in places}
    for place in places:
        got[place]()
        if place not in (6, 7, 8):
            finish.append(copy(held[place], target[place]))
            continue
        wide = high[place - 6]

        def widen(a, place=place, wide=wide):
            wide[a] = held[place][a].astype(jnp.float32)

        pl.loop(0, wide.shape[0])(widen)
        if place < 8:
            finish.append(copy(wide, target[place]))
            continue
        for k in range(narrow):
            finish.append(
                copy(wide.at[k], target[place].at[:, :, :, pl.ds(k * block, block)])
            )
    for wait in finish:
        wait()


def last_call(shape, args):
    f32 = jnp.float32
    outs = [jax.ShapeDtypeStruct(a.shape, f32 if 6 <= n < 9 else a.dtype) for n, a in enumerate(args)]
    outs[8] = jax.ShapeDtypeStruct((*args[8].shape[1:-1], shape.depth), f32)
    anywhere = pl.BlockSpec(memory_space=pl.ANY)
    return pl.pallas_call(
        functools.partial(last_kernel, shape),
        out_shape=outs,
        in_specs=[anywhere] * 15,
        out_specs=[anywhere] * 15,
        scratch_shapes=[pltpu.VMEM(a.shape, a.dtype) for a in args]
        + [pltpu.VMEM(a.shape, f32) for a in args[6:9]]
        + [pltpu.SemaphoreType.DMA((64,))],
        compiler_params=pltpu.CompilerParams(vmem_limit_bytes=VMEM_BYTES),
        name="results",
    )(*args)


def kernel_body(shape, *arguments):
    inputs, upstreams = arguments[:3], arguments[3:6]
    reduce_weight, spatial_weight, expand_weight = arguments[6:9]
    vectors = arguments[9:]

    def flat(array):
        return jnp.transpose(array, (1, 2, 0, 3)).reshape(-1, array.shape[3])

    def unflat(array, side):
        return jnp.transpose(
            array.reshape(side, side, shape.images, array.shape[1]), (2, 0, 1, 3)
        )

    results = kernel_call(
        shape,
        [flat(x) for x in inputs]
        + [flat(u) for u in upstreams]
        + [
            reduce_weight,
            spatial_weight.reshape(9, shape.inner, shape.own),
            expand_weight,
        ]
        + [v.reshape(1, -1) for v in vectors],
    )
    results = last_call(shape, results)
    maps = list(shape.maps)
    images = [unflat(r, side) for r, side in zip(results[:6], maps + maps)]
    weights = [
        results[6].reshape(reduce_weight.shape),
        results[7].reshape(spatial_weight.shape),
        results[8].reshape(expand_weight.shape),
    ]
    return tuple(images + weights + [r.reshape(-1) for r in results[9:]])


def body(mesh, *arguments):
    inputs, reduce_weight = arguments[0], arguments[6]
    shape = Shape(
        mesh,
        [x.shape[1] for x in arguments[:3]],
        inputs.shape[0],
        inputs.shape[3],
        arguments[8].shape[0] * mesh.shape["narrow"],
    )
    if shape.fits():
        return kernel_body(shape, *arguments)
    return plain_body(*arguments)


def solution(mesh):
    rows = P("wide", None, None, None)
    blocks = P("wide", None, None, "narrow")
    weights = [P(None, "narrow"), P(None, None, None, "narrow"), P("narrow", None)]
    vectors = [P("narrow")] * 6
    return jax.shard_map(
        functools.partial(body, mesh),
        mesh=mesh,
        in_specs=tuple([rows] * 3 + [blocks] * 3 + weights + vectors),
        out_specs=tuple([blocks] * 6 + weights + vectors),
        check_vma=False,
    )
```
